32 devices in a mesh: dp: 8 (over z, y), tensor: 4 (over x, core).
Axes of the slice: x: 2, y: 2, z: 4, core: 2. Of those that a mesh axis runs over, the one named last changes fastest.
Arguments:
- tokens: bfloat16 [8, 1024, 768], P(None, 'dp'), may hold values from -6 to 6, as said below
- dealing_order: int32 [8], replicated, may hold values from 0 to 7, each once
- lengths: int32 [8], replicated, may hold values from 1 to 1024, 6144 in all
- project_weight: float32 [2, 768, 3, 768], P(None, 'dp', None, 'tensor'), may hold values from -0.14433757 to 0.14433757, as said below
- gate_up_weight: float32 [2, 768, 2, 3072], P(None, 'dp', None, 'tensor'), may hold values from -0.14433757 to 0.14433757, as said below
- output_weight: float32 [2, 768, 768], P(None, 'tensor', 'dp'), may hold values from -3 to 3
- down_weight: float32 [2, 3072, 768], P(None, 'tensor', 'dp'), may hold values from -0.109375 to 0.109375
- norm_gains: float32 [2, 2, 768], replicated, may hold values from 0.1 to 1.9
- norm_biases: float32 [2, 2, 768], replicated, may hold values from -1.75 to 1.75
- cotangent: bfloat16 [8, 1024, 768], P('dp', 'tensor'), may hold values from -6 to 6
Outputs:
- layer_outputs: float32 [8, 1024, 768], P('dp', 'tensor')
- tokens_gradient: float32 [8, 1024, 768], P(None, 'dp')
- project_gradient: float32 [2, 768, 3, 768], P(None, 'dp', None, 'tensor')
- gate_up_gradient: float32 [2, 768, 2, 3072], P(None, 'dp', None, 'tensor')
- output_gradient: float32 [2, 768, 768], P(None, 'tensor', 'dp')
- down_gradient: float32 [2, 3072, 768], P(None, 'tensor', 'dp')
- gains_gradient: float32 [2, 2, 768], replicated
- biases_gradient: float32 [2, 2, 768], replicated
The draws below stay inside these ranges and needn't reach their ends.
Inputs may be any that keep to these rules, and one draw needn't show every extreme that they name: `dealing_order`: a permutation of the 8 sequences. The lengths sum to 6144 and the longest is exactly 1024. `tokens`: entries of mean 0 and deviation 1. `project_weight`: entries of mean 0 and deviation 768 ** -0.5. `gate_up_weight`: entries of mean 0 and deviation 768 ** -0.5.
All inputs are finite; a program needn't handle non-finite values.
Results may differ from the reference program's by a relative error of at most 0.024.
Values may be sent and summed in bfloat16 or wider, within the bound.
No kernel may reach another device: no remote copies, remote signals or barrier semaphores. Data moves between devices by JAX's collectives and lax.ppermute only.
A program may use at most 192 MiB of HBM per device.

```python
import math
import jax
import jax.numpy as jnp
import numpy as np
from jax import lax

D = 768
HD = 64
FF = 3072
LAYERS = 2
MAXLEN = 1024
SEQS = 8


def bell_spread(key, shape, deviation, limit):
    return jnp.clip(jax.random.normal(key, shape, jnp.float32) * deviation, -limit, limit)


def draw_tokens(key, part):
    key = jax.random.fold_in(key, 11)
    shape = (SEQS, MAXLEN, D)
    values = bell_spread(key, shape, 1.0, 6.0)
    return values.astype(jnp.bfloat16)


def draw_project_weight(key, part):
    key = jax.random.fold_in(key, 12)
    shape = (LAYERS, D, 3, D)
    deviation = D ** (-0.5)
    values = bell_spread(key, shape, deviation, 4.0 * deviation)
    return values.astype(jnp.float32)


def draw_gate_up_weight(key, part):
    key = jax.random.fold_in(key, 13)
    shape = (LAYERS, D, 2, FF)
    deviation = D ** (-0.5)
    values = bell_spread(key, shape, deviation, 4.0 * deviation)
    return values.astype(jnp.float32)


def levels(stream_key, shape, cuts, least, high):
    level, own = 1.0, jax.random.fold_in(stream_key, 6)
    for position, blocks in cuts:
        heights = jnp.exp(jax.random.uniform(jax.random.fold_in(own, position), (blocks,), jnp.float32, least / len(cuts), high / len(cuts)))
        level = level * jnp.repeat(heights, shape[position] // blocks).reshape([-1 if axis == position else 1 for axis in range(len(shape))])
    return level


def length_profile(count, total, bound, skew):
    weights = [(1 << 20) // math.isqrt(rank ** skew) + 1 for rank in range(2, count + 1)]
    surplus, holding = total - bound - (count - 1), [1] * (count - 1)
    while surplus > 0:
        candidates = [i for i in range(count - 1) if holding[i] < bound]
        mass, remaining = sum([weights[i] for i in candidates]), surplus
        for i in candidates:
            addition = min(bound - holding[i], max(1, remaining * weights[i] // mass), surplus)
            holding[i] = holding[i] + addition
            surplus = surplus - addition
    return np.array([bound] + holding)


def uneven(stream_key, number_of, total, reach, skew):
    if number_of == 2:
        one = jax.random.randint(stream_key, (), max(1, total - reach), min(reach, total - 1) + 1)
        return jnp.stack([one, total - one])
    sizes = jnp.asarray(length_profile(number_of, total, reach, skew), jnp.int32)
    twos = (number_of - 1) // 2
    source_of, receiver = sizes[1:1 + 2 * twos:2], sizes[2:2 + 2 * twos:2]
    slack = jnp.minimum(source_of - 1, reach - receiver)
    passed = jax.random.randint(jax.random.fold_in(stream_key, 1), (twos,), 0, 1 << 20) % (slack + 1)
    sizes = sizes.at[1:1 + 2 * twos:2].set(source_of - passed).at[2:2 + 2 * twos:2].set(receiver + passed)
    return sizes[jax.random.permutation(jax.random.fold_in(stream_key, 2), number_of)]


def noise(rng, dims, scale, reach, pieces=(), held_as=jnp.bfloat16):
    factor_of = levels(rng, dims, pieces, -0.22, 0.18) if pieces else 1.0
    drawn = jax.random.normal(rng, dims, jnp.float32) * scale * factor_of
    return jnp.minimum(jnp.maximum(drawn, -reach), reach).astype(held_as)


def setup_inputs(seed: int = 0) -> dict:
    keys = jax.random.split(jax.random.key(seed), 11)
    tokens = draw_tokens(jax.random.fold_in(keys[10], 71), 0)
    dealing_order = jax.random.permutation(keys[1], SEQS).astype(jnp.int32)
    lengths = uneven(keys[2], SEQS, SEQS * MAXLEN * 3 // 4, MAXLEN, 1).astype(jnp.int32)
    project_weight = draw_project_weight(jax.random.fold_in(keys[10], 71), 0)
    gate_up_weight = draw_gate_up_weight(jax.random.fold_in(keys[10], 71), 0)
    output_weight = noise(keys[5], (LAYERS, D, D), 4 ** -0.5, 3.0, ((1, 4), (2, 8)), jnp.float32)
    down_weight = noise(keys[6], (LAYERS, FF, D), FF ** -0.5, 0.109375, ((1, 4), (2, 8)), jnp.float32)
    norm_gains = jnp.clip(1.0 + 0.18 * jax.random.normal(keys[7], (LAYERS, 2, D), jnp.float32), 0.1, 1.9)
    norm_biases = noise(keys[8], (LAYERS, 2, D), 0.3, 1.75, (), jnp.float32)
    cotangent = noise(keys[9], (SEQS, MAXLEN, D), 1.0, 6.0, ((0, 8), (1, 4)))
    return dict(tokens=tokens, dealing_order=dealing_order, lengths=lengths, project_weight=project_weight, gate_up_weight=gate_up_weight, output_weight=output_weight, down_weight=down_weight, norm_gains=norm_gains, norm_biases=norm_biases, cotangent=cotangent)


epsilon = 1e-05
rotary_base = 1000.0
highest = lax.Precision.HIGHEST

@jax.custom_vjp
def low(v):
    return lax.optimization_barrier(v.astype(jnp.bfloat16)).astype(jnp.float32)

@jax.custom_vjp
def low_back(v):
    return v

def low_keep(v):
    return (low(v), None)

def low_pass(kept, grad):
    return (grad,)

def back_keep(v):
    return (v, None)

def back_low(kept, grad):
    return (low(grad),)
low.defvjp(low_keep, low_pass)
low_back.defvjp(back_keep, back_low)

def matmul(left, right):
    return jnp.dot(left, right, precision=highest)

def layer_norm(values, gain_vector, shift_vector):
    centred = values - lax.optimization_barrier(jnp.mean(values, axis=-1, keepdims=True))
    spread = lax.optimization_barrier(jnp.mean(centred * centred, axis=-1, keepdims=True))
    return centred * lax.rsqrt(spread + epsilon) * gain_vector + shift_vector

def rotary_tables(length, head_size):
    half_size = head_size // 2
    places = jnp.arange(length, dtype=jnp.float32)[:, None]
    freq_steps = jnp.arange(half_size, dtype=jnp.float32)[None, :]
    angles = places * jnp.exp(freq_steps * (-2.0 * math.log(rotary_base) / head_size))
    return (jnp.cos(angles)[:, None, :], jnp.sin(angles)[:, None, :])

def rotate(values, cosine_table, sine_table):
    half_size = values.shape[-1] // 2
    first_half = values[..., :half_size]
    second = values[..., half_size:]
    return jnp.concatenate([first_half * cosine_table - second * sine_table, second * cosine_table + first_half * sine_table], axis=-1)

def attend(operands):
    queries, key_rows, values_in, length = operands
    score_scale = 1.0 / math.sqrt(queries.shape[-1])
    scores = jnp.einsum('qhd,khd->hqk', queries, key_rows, precision=highest) * score_scale
    scores = low_back(scores)
    usable = jnp.arange(scores.shape[-1]) < length
    scores = jnp.where(usable[None, None, :], scores, -1e+30)
    weights = jax.nn.softmax(scores, axis=-1)
    return jnp.einsum('hqk,khd->qhd', low(weights), values_in, precision=highest)

def one_layer(inputs, lengths_now, project_weight, gate_up_weight, output_weight, down_weight, gain_pair, shift_pair):
    groups, length, model_width = inputs.shape
    head_count = model_width // HD
    flat_rows = inputs.reshape(groups * length, model_width)
    projected = low_back(matmul(low(flat_rows), low(project_weight).reshape(model_width, -1)))
    projected = projected.reshape(groups, length, 3, head_count, HD)
    cosine_table, sine_table = rotary_tables(length, HD)
    queries = low(rotate(projected[:, :, 0], cosine_table, sine_table))
    key_rows = low(rotate(projected[:, :, 1], cosine_table, sine_table))
    values_in = low(projected[:, :, 2])
    context = lax.map(jax.checkpoint(attend), (queries, key_rows, values_in, lengths_now))
    context = low(low_back(context)).reshape(groups * length, model_width)
    attended = low_back(matmul(context, low(output_weight)))
    hidden = layer_norm(flat_rows + attended, gain_pair[0], shift_pair[0])
    gate_up = low_back(matmul(low(hidden), low(gate_up_weight).reshape(model_width, -1)))
    gate_up = gate_up.reshape(groups * length, 2, gate_up_weight.shape[-1])
    active = low(jax.nn.silu(gate_up[:, 0]) * gate_up[:, 1])
    mixed_part = low_back(matmul(active, low(down_weight)))
    result = layer_norm(hidden + mixed_part, gain_pair[1], shift_pair[1])
    return result.reshape(groups, length, model_width)

def whole_block(block_inputs, lengths_now, block_params):
    project_weight, gate_up_weight, output_weight, down_weight, norm_gains, norm_biases = block_params
    current = block_inputs
    for depth_index in range(LAYERS):
        current = one_layer(current, lengths_now, project_weight[depth_index], gate_up_weight[depth_index], output_weight[depth_index], down_weight[depth_index], norm_gains[depth_index], norm_biases[depth_index])
    usable = jnp.arange(block_inputs.shape[1])[None, :] < lengths_now[:, None]
    return jnp.where(usable[:, :, None], current, jnp.zeros_like(current))

def reference(tokens, dealing_order, lengths, project_weight, gate_up_weight, output_weight, down_weight, norm_gains, norm_biases, cotangent):
    dealt = tokens[dealing_order].astype(jnp.float32)
    dealt_lengths = lengths[dealing_order]
    seq_total = dealt.shape[0]
    group_size = math.gcd(seq_total, max(1, 4096 // MAXLEN))
    block_count = seq_total // group_size
    params = (project_weight, gate_up_weight, output_weight, down_weight, norm_gains, norm_biases)
    shaped = dealt.reshape(block_count, group_size, MAXLEN, D)
    lengths_shaped = dealt_lengths.reshape(block_count, group_size)
    cotangents = cotangent.astype(jnp.float32).reshape(block_count, group_size, MAXLEN, D)

    def accumulate(totals, operands):
        inputs, lengths_now, seeds = operands
        result, pullback = jax.vjp(lambda block_inputs, block_params: whole_block(block_inputs, lengths_now, block_params), inputs, params)
        input_grad, param_grads = pullback(seeds)
        totals = jax.tree.map(jnp.add, totals, param_grads)
        return (totals, (result, input_grad))
    zero_grads = jax.tree.map(jnp.zeros_like, params)
    totals, (results, input_grads) = lax.scan(accumulate, zero_grads, (shaped, lengths_shaped, cotangents))
    layer_outputs = results.reshape(seq_total, MAXLEN, D).astype(jnp.float32)
    returned = jnp.zeros((seq_total, MAXLEN, D), jnp.float32).at[dealing_order].set(input_grads.reshape(seq_total, MAXLEN, D))
    return (layer_outputs, returned, totals[0], totals[1], totals[2], totals[3], totals[4], totals[5])
```

```python
import functools
import math

import jax
import jax.numpy as jnp
import numpy as np
from jax import lax
from jax.experimental import pallas as pl
from jax.experimental.pallas import tpu as pltpu
from jax.sharding import PartitionSpec as P

HD = 64
LAYERS = 2
epsilon = 1e-05
rotary_base = 1000.0
LOG2E = math.log2(math.e)
F32 = jnp.float32
BF16 = jnp.bfloat16
VMEM_LIMIT = 16 * 1024 * 1024
COST = 0.001


def sds(*shape, dtype=BF16):
    return jax.ShapeDtypeStruct(shape, dtype)


def call(kernel, outs, *operands, flops=0, trans=0, scalars=0, scratch=()):
    vmem = pl.BlockSpec(memory_space=pltpu.VMEM)
    smem = pl.BlockSpec(memory_space=pltpu.SMEM)
    moved = sum(a.size * a.dtype.itemsize for a in list(operands) + list(outs))
    return pl.pallas_call(
        kernel,
        in_specs=[smem] * scalars + [vmem] * (len(operands) - scalars),
        out_specs=[vmem] * len(outs),
        out_shape=list(outs),
        scratch_shapes=list(scratch),
        compiler_params=pltpu.CompilerParams(vmem_limit_bytes=VMEM_LIMIT),
        cost_estimate=pl.CostEstimate(
            flops=int(COST * flops),
            bytes_accessed=int(COST * moved),
            transcendentals=int(COST * trans),
        ),
    )(*operands)


def swap_core(value):
    return lax.ppermute(value, "tensor", [(i, i ^ 1) for i in range(lax.axis_size("tensor"))])


def swap_x(value):
    return lax.ppermute(value, "tensor", [(i, i ^ 2) for i in range(lax.axis_size("tensor"))])


def swap_dp(value, step):
    return lax.ppermute(value, "dp", [(i, i ^ step) for i in range(lax.axis_size("dp"))])


def place_kernel(index_ref, *refs):
    *pieces, whole_ref = refs
    rows = pieces[0].shape[0]
    for offset, piece in enumerate(pieces):
        start = pl.multiple_of((index_ref[0] ^ offset) * rows, rows)
        whole_ref[pl.ds(start, rows), :] = piece[...]


def gather_rows(shard):
    count = lax.axis_size("dp")
    rows, width = shard.shape
    if count != 8 or rows % 16:
        return lax.all_gather(shard, "dp", axis=0, tiled=True)
    index = lax.axis_index("dp").astype(jnp.int32).reshape(1)
    along = [swap_dp(shard, step) for step in (2, 4, 6)]
    near = swap_dp(shard, 1)
    across = [swap_dp(piece, 1) for piece in along]
    pieces = [shard, near, along[0], across[0], along[1], across[1], along[2], across[2]]
    return call(place_kernel, [sds(count * rows, width)], index, *pieces, scalars=1)[0]


def scatter_sum(kept, sent):
    count = lax.axis_size("dp")
    pair = (kept.astype(F32) + swap_dp(sent, 1).astype(F32)).astype(BF16)
    groups = [[i for i in range(count) if i % 2 == parity] for parity in (0, 1)]
    arrived = lax.all_to_all(pair, "dp", 0, 0, axis_index_groups=groups, tiled=True)
    return jnp.sum(arrived.astype(F32), axis=0)


def sum_everywhere(value):
    for step in (1, 2):
        value = value + lax.ppermute(value, "tensor", [(i, i ^ step) for i in range(4)])
    count = lax.axis_size("dp")
    step = 1
    while step < count:
        value = value + swap_dp(value, step)
        step *= 2
    return value


def dot_nt(left, right):
    return lax.dot_general(left, right, (((1,), (1,)), ((), ())), preferred_element_type=F32)


def dot_nn(left, right):
    return lax.dot_general(left, right, (((1,), (0,)), ((), ())), preferred_element_type=F32)


def dot_tn(left, right):
    return lax.dot_general(left, right, (((0,), (0,)), ((), ())), preferred_element_type=F32)


def swap_halves(values):
    width = values.shape[-1]
    lane = lax.broadcasted_iota(jnp.int32, values.shape, 1)
    return jnp.where(
        lane % HD < HD // 2,
        pltpu.roll(values, width - HD // 2, 1),
        pltpu.roll(values, HD // 2, 1),
    )


def widen(table, width):
    return jnp.concatenate([table] * (width // table.shape[1]), axis=1)


def qkv_kernel(*refs):
    *x_refs, w_ref, cos_ref, sin_ref, bias_ref, q_ref, k_ref, v_ref, kt_ref, vt_ref = refs
    inner = v_ref.shape[1]
    extra = q_ref.shape[1] - inner
    weight = w_ref[:, : 3 * inner]
    for step, x_ref in enumerate(x_refs):
        block = x_ref.shape[0]
        here = pl.ds(step * block, block)
        projected = dot_nn(x_ref[...], weight)
        pair = projected[:, : 2 * inner]
        turned = pair * widen(cos_ref[here, :], 2 * inner) + swap_halves(pair) * widen(
            sin_ref[here, :], 2 * inner
        )
        lane = lax.broadcasted_iota(jnp.int32, (block, extra), 1)
        queries = turned[:, :inner] * (1.0 / math.sqrt(HD))
        keys = turned[:, inner:]
        values = projected[:, 2 * inner :]
        one = jnp.where(lane == 0, 1.0, 0.0)
        mark = jnp.where(lane == 0, bias_ref[here, :extra], 0.0)
        q_ref[here, :] = jnp.concatenate([queries, one], axis=1).astype(BF16)
        k_ref[here, :] = jnp.concatenate([keys, mark], axis=1).astype(BF16)
        v_ref[here, :] = values.astype(BF16)
        kt_ref[:, here] = keys.T.astype(BF16)
        vt_ref[:, here] = values.T.astype(BF16)


def qkv_call(pieces, weight, tables, inner):
    rows = sum(p.shape[0] for p in pieces)
    width = weight.shape[0]
    return call(
        qkv_kernel,
        [sds(rows, inner + HD), sds(rows, inner + HD), sds(rows, inner)] + [sds(inner, rows)] * 2,
        *pieces, weight, *tables,
        flops=2 * rows * width * 3 * inner,
    )


def head_mask(shape, head, inner):
    lane = lax.broadcasted_iota(jnp.int32, shape, 1)
    return ((lane >= head * HD) & (lane < (head + 1) * HD)) | (lane >= inner)


def attend_kernel(chunk, q_ref, k_ref, vt_ref, w_ref, c_ref, lse_ref, theirs_ref, mine_ref):
    inner = c_ref.shape[1]
    weight = w_ref[:, 3 * inner :]
    half = c_ref.shape[0] // 2
    for part in (1, 0):
        queries = q_ref[pl.ds((2 * chunk + part) * half, half), :]
        columns, stats = [], []
        for head in range(inner // HD):
            masked = jnp.where(head_mask(queries.shape, head, inner), queries, 0)
            scores = dot_nt(k_ref[...], masked)
            shift = jnp.max(scores, axis=0, keepdims=True) * LOG2E
            exps = jnp.exp2(scores * LOG2E - shift)
            total = jnp.sum(exps, axis=0, keepdims=True)
            mixed = dot_nn(vt_ref[head * HD : (head + 1) * HD, :], exps.astype(BF16))
            columns.append(mixed * (1.0 / total))
            stats.append(shift + jnp.log2(total))
        context = jnp.concatenate(columns, axis=0).T.astype(BF16)
        here = pl.ds(part * half, half)
        c_ref[here, :] = context
        pad = lse_ref.shape[0] - len(stats)
        lse_ref[:, here] = jnp.concatenate(stats + [jnp.zeros((pad, half), F32)], axis=0)
        partial = dot_nt(context, weight)
        if part:
            theirs_ref[...] = partial.astype(BF16)
        else:
            mine_ref[...] = partial


def attend_call(chunk, chunks, queries, keys, values_t, weight):
    length, padded = queries.shape
    rows, inner, width = length // chunks, padded - HD, weight.shape[0]
    return call(
        functools.partial(attend_kernel, chunk),
        [
            sds(rows, inner), sds(8, rows, dtype=F32),
            sds(rows // 2, width), sds(rows // 2, width, dtype=F32),
        ],
        queries, keys, values_t, weight,
        flops=4 * rows * length * 256 * (inner // HD) + 2 * rows * inner * width,
        trans=rows * length * (inner // HD),
    )


def norm_kernel(base_ref, pair_ref, other_ref, gain_ref, shift_ref, sum_ref, out_ref, low_ref):
    values = base_ref[...].astype(F32) + (pair_ref[...] + other_ref[...].astype(F32))
    sum_ref[...] = values
    centred = values - jnp.mean(values, axis=-1, keepdims=True)
    scaled = lax.rsqrt(jnp.mean(centred * centred, axis=-1, keepdims=True) + epsilon)
    result = centred * scaled * gain_ref[...] + shift_ref[...]
    out_ref[...] = result
    low_ref[...] = result.astype(BF16)


def norm_call(base, pair, other, gain, shift):
    rows, width = pair.shape
    return call(
        norm_kernel,
        [sds(rows, width, dtype=F32), sds(rows, width, dtype=F32), sds(rows, width)],
        base, pair, other, gain, shift,
        flops=10 * rows * width,
    )


def norm_back_kernel(*refs):
    *in_refs, values_ref, gain_ref, out_ref, low_ref, vec_ref = refs
    incoming = in_refs[0][...].astype(F32)
    for ref in in_refs[1:]:
        incoming = incoming + ref[...].astype(F32)
    values = values_ref[...]
    centred = values - jnp.mean(values, axis=-1, keepdims=True)
    scaled = lax.rsqrt(jnp.mean(centred * centred, axis=-1, keepdims=True) + epsilon)
    normal = centred * scaled
    weighted = incoming * gain_ref[...]
    result = scaled * (
        weighted
        - jnp.mean(weighted, axis=-1, keepdims=True)
        - normal * jnp.mean(weighted * normal, axis=-1, keepdims=True)
    )
    out_ref[...] = result
    low_ref[...] = result.astype(BF16)
    vec_ref[0:1, :] = jnp.sum(incoming * normal, axis=0, keepdims=True)
    vec_ref[1:2, :] = jnp.sum(incoming, axis=0, keepdims=True)


def norm_back_call(incoming, values, gain):
    rows, width = values.shape
    return call(
        norm_back_kernel,
        [sds(rows, width, dtype=F32), sds(rows, width), sds(2, width, dtype=F32)],
        *incoming, values, gain,
        flops=16 * rows * width,
    )


def mlp_kernel(mine_in, theirs_in, w_ref, gu_ref, act_ref, theirs_ref, mine_ref):
    hidden = act_ref.shape[1]
    half = mine_in.shape[0]
    for part, x_ref in ((1, theirs_in), (0, mine_in)):
        here = pl.ds(part * half, half)
        rows = x_ref[...]
        gate = dot_nn(rows, w_ref[:, :hidden])
        up = dot_nn(rows, w_ref[:, hidden : 2 * hidden])
        active = (gate * jax.nn.sigmoid(gate) * up).astype(BF16)
        gu_ref[here, :hidden] = gate.astype(BF16)
        gu_ref[here, hidden:] = up.astype(BF16)
        act_ref[here, :] = active
        partial = dot_nt(active, w_ref[:, 2 * hidden :])
        if part:
            theirs_ref[...] = partial.astype(BF16)
        else:
            mine_ref[...] = partial


def mlp_call(mine, theirs, weight):
    half, width = mine.shape
    hidden = weight.shape[1] // 3
    return call(
        mlp_kernel,
        [
            sds(2 * half, 2 * hidden), sds(2 * half, hidden),
            sds(half, width), sds(half, width, dtype=F32),
        ],
        mine, theirs, weight,
        flops=4 * half * width * weight.shape[1],
        trans=2 * half * hidden,
    )


def mlp_back_kernel(mine_in, theirs_in, gu_ref, w_ref, dg_ref, theirs_ref, mine_ref):
    hidden = gu_ref.shape[1] // 2
    half = mine_in.shape[0]
    for part, x_ref in ((1, theirs_in), (0, mine_in)):
        here = pl.ds(part * half, half)
        active_grad = dot_nn(x_ref[...], w_ref[:, 2 * hidden :])
        gate = gu_ref[here, :hidden].astype(F32)
        up = gu_ref[here, hidden:].astype(F32)
        sigmoid = jax.nn.sigmoid(gate)
        gate_grad = (active_grad * up * sigmoid * (1.0 + gate * (1.0 - sigmoid))).astype(BF16)
        up_grad = (active_grad * gate * sigmoid).astype(BF16)
        dg_ref[here, :hidden] = gate_grad
        dg_ref[here, hidden:] = up_grad
        partial = dot_nt(gate_grad, w_ref[:, :hidden]) + dot_nt(
            up_grad, w_ref[:, hidden : 2 * hidden]
        )
        if part:
            theirs_ref[...] = partial.astype(BF16)
        else:
            mine_ref[...] = partial


def mlp_back_call(mine, theirs, gate_up, weight):
    half, width = mine.shape
    return call(
        mlp_back_kernel,
        [
            sds(*gate_up.shape), sds(half, width), sds(half, width, dtype=F32),
        ],
        mine, theirs, gate_up, weight,
        flops=4 * half * width * weight.shape[1],
        trans=2 * half * weight.shape[1] // 3,
    )


def context_back_kernel(mine_in, theirs_in, w_ref, dc_ref):
    inner = dc_ref.shape[1]
    half = mine_in.shape[0]
    weight = w_ref[:, 3 * inner :]
    dc_ref[:half, :] = dot_nn(mine_in[...], weight).astype(BF16)
    dc_ref[half:, :] = dot_nn(theirs_in[...], weight).astype(BF16)


def context_back_call(mine, theirs, weight):
    half, width = mine.shape
    inner = weight.shape[1] // 4
    return call(
        context_back_kernel, [sds(2 * half, inner)], mine, theirs, weight,
        flops=4 * half * width * inner,
    )[0]


def attend_back_kernel(
    q_ref, dc_ref, lse_ref, k_ref, v_ref, kt_ref, cosq_ref, sinq_ref, cos_ref, sin_ref,
    dp_ref, dk_ref, dv_ref,
):
    step = pl.program_id(0)
    inner = v_ref.shape[1]
    block, padded = q_ref.shape

    @pl.when(step == 0)
    def _():
        dk_ref[...] = jnp.zeros_like(dk_ref)
        dv_ref[...] = jnp.zeros_like(dv_ref)

    def turn_back(gradient, cosine, sine):
        cosine = widen(cosine, gradient.shape[1])
        sine = widen(sine, gradient.shape[1])
        return (gradient * cosine - swap_halves(gradient) * sine)[:, :inner]

    queries = q_ref[...]
    context_grad = dc_ref[...]
    columns = []
    for head in range(inner // HD):
        masked = jnp.where(head_mask(queries.shape, head, inner), queries, 0)
        masked_grad = jnp.where(head_mask(context_grad.shape, head, inner), context_grad, 0)
        scores = dot_nt(k_ref[...], masked)
        weights = jnp.exp2(scores * LOG2E - lse_ref[head : head + 1, :])
        weight_grad = dot_nt(v_ref[...], masked_grad)
        inner_sum = jnp.sum(weights * weight_grad, axis=0, keepdims=True)
        score_grad = (weights * (weight_grad - inner_sum)).astype(BF16)
        dk_ref[...] += dot_nn(score_grad, masked)
        dv_ref[...] += dot_nn(weights.astype(BF16), masked_grad)
        columns.append(dot_nn(kt_ref[head * HD : (head + 1) * HD, :], score_grad))
    columns.append(jnp.zeros((padded - inner, block), F32))
    query_grad = jnp.concatenate(columns, axis=0).T * (1.0 / math.sqrt(HD))
    here = pl.ds(pl.multiple_of(step * block, block), block)
    dp_ref[here, :inner] = turn_back(query_grad, cosq_ref[...], sinq_ref[...]).astype(BF16)

    @pl.when(step == pl.num_programs(0) - 1)
    def _():
        dp_ref[:, inner : 2 * inner] = turn_back(
            dk_ref[...], cos_ref[...], sin_ref[...]
        ).astype(BF16)
        dp_ref[:, 2 * inner :] = dv_ref[...].astype(BF16)


def attend_back_call(queries, context_grad, logsum, keys, values, keys_t, cosine, sine):
    rows, padded = queries.shape
    inner = padded - HD
    heads = inner // HD
    block = 256
    row_spec = lambda n: pl.BlockSpec((block, n), lambda i: (i, 0))
    whole = lambda a: pl.BlockSpec(a.shape, lambda i: (0, 0))
    return pl.pallas_call(
        attend_back_kernel,
        grid=(rows // block,),
        in_specs=[
            row_spec(padded), row_spec(inner), pl.BlockSpec((8, block), lambda i: (0, i)),
            whole(keys), whole(values), whole(keys_t), row_spec(128), row_spec(128),
            whole(cosine), whole(sine),
        ],
        out_specs=pl.BlockSpec((rows, 3 * inner), lambda i: (0, 0)),
        out_shape=sds(rows, 3 * inner),
        scratch_shapes=[pltpu.VMEM((rows, padded), F32), pltpu.VMEM((rows, inner), F32)],
        compiler_params=pltpu.CompilerParams(
            vmem_limit_bytes=VMEM_LIMIT, dimension_semantics=("arbitrary",)
        ),
        cost_estimate=pl.CostEstimate(
            flops=int(COST * 10 * rows * rows * 256 * heads),
            bytes_accessed=int(COST * 16 * rows * padded),
            transcendentals=int(COST * rows * rows * heads),
        ),
    )(queries, context_grad, logsum, keys, values, keys_t, cosine, sine, cosine, sine)


def input_back_kernel(chunk, dp_ref, w_ref, theirs_ref, mine_ref):
    half = mine_ref.shape[0]
    total = dp_ref.shape[1]
    weight = w_ref[:, :total]
    theirs_ref[...] = dot_nt(dp_ref[pl.ds((2 * chunk + 1) * half, half), :], weight).astype(BF16)
    mine_ref[...] = dot_nt(dp_ref[pl.ds(2 * chunk * half, half), :], weight)


def input_back_call(chunk, chunks, triple, weight):
    half, width = triple.shape[0] // (2 * chunks), weight.shape[0]
    return call(
        functools.partial(input_back_kernel, chunk),
        [sds(half, width), sds(half, width, dtype=F32)],
        triple, weight,
        flops=4 * half * triple.shape[1] * width,
    )


def input_last_kernel(index_ref, dp_ref, w_ref, *refs):
    *grad_refs, kept_ref, sent_ref = refs
    core, side = index_ref[0], index_ref[1]
    rows, total = dp_ref.shape
    quarter = rows // 4
    split = kept_ref.shape[1]
    weight = w_ref[:, :total]
    for step in range(4):
        chunk, part = step // 2, step % 2
        partial = dot_nt(dp_ref[pl.ds(step * quarter, quarter), :], weight)
        if not part:
            partial = partial + jnp.where(side == chunk, grad_refs[chunk][...], 0.0)
        start = pl.multiple_of((2 * chunk + (core ^ part)) * quarter, quarter)
        low, high = partial[:, :split], partial[:, split:]
        kept_ref[pl.ds(start, quarter), :] = jnp.where(core == 0, low, high)
        sent_ref[pl.ds(start, quarter), :] = jnp.where(core == 0, high, low).astype(BF16)


def input_last_call(index, triple, weight, grads):
    rows, width = triple.shape[0], weight.shape[0]
    return call(
        input_last_kernel,
        [sds(rows, width // 2, dtype=F32), sds(rows, width // 2)],
        index, triple, weight, *grads,
        flops=2 * rows * triple.shape[1] * width, scalars=1,
    )


def weight_kernel(counts, index_ref, *refs):
    *in_refs, kept_ref, sent_ref = refs
    parity = index_ref[0]
    blocks, rows, _ = kept_ref.shape
    wide = 4 * rows if blocks % 2 == 0 and (4 * rows) % 128 == 0 else 2 * blocks * rows
    column = 0
    lefts, rights = [], []
    for left_count, right_count in counts:
        lefts.append(in_refs[:left_count])
        rights.append(in_refs[left_count : left_count + right_count])
        in_refs = in_refs[left_count + right_count :]
    for left, right in zip(lefts, rights):
        width = right[0].shape[1]
        share = min(width, 768)
        ratio = len(left) // len(right)
        for first in range(0, 2 * blocks * rows, wide):
            for start in range(0, width, share):
                total = None
                for number, left_ref in enumerate(left):
                    size = left_ref.shape[0]
                    right_ref = right[number // ratio]
                    term = dot_tn(
                        left_ref[:, first : first + wide],
                        right_ref[
                            pl.ds((number % ratio) * size, size), start : start + share
                        ],
                    )
                    total = term if total is None else total + term
                for offset in range(0, wide, 2 * rows):
                    even = total[offset : offset + rows].astype(BF16)
                    odd = total[offset + rows : offset + 2 * rows].astype(BF16)
                    block = (first + offset) // (2 * rows)
                    where = pl.ds(column + start, share)
                    kept_ref[block, :, where] = jnp.where(parity == 0, even, odd)
                    sent_ref[block, :, where] = jnp.where(parity == 0, odd, even)
        column += width


def weight_call(parity, pairs, count):
    width = pairs[0][0][0].shape[1]
    total = sum(right[0].shape[1] for _, right in pairs)
    rows = sum(piece.shape[0] for piece in pairs[0][0])
    operands = [piece for left, right in pairs for piece in (*left, *right)]
    counts = tuple((len(left), len(right)) for left, right in pairs)
    shape = sds(count // 2, width // count, total)
    return call(
        functools.partial(weight_kernel, counts),
        [shape, shape],
        parity, *operands,
        flops=2 * rows * width * total, scalars=1,
    )


def finish_pair(mine, theirs):
    pair = mine + swap_core(theirs).astype(F32)
    return pair, swap_x(pair.astype(BF16))


def layer_forward(pieces, residual, first_weight, second_weight, gains, shifts, tables, inner):
    chunks = len(residual)
    queries, keys, values, keys_t, values_t = qkv_call(pieces, first_weight, tables, inner)
    context, logsum, first_sum, hidden, hidden_pieces = [], [], [], [], []
    partial = []
    for k in range(chunks):
        c, l, theirs, mine = attend_call(k, chunks, queries, keys, values_t, first_weight)
        context.append(c)
        logsum.append(l)
        partial.append((mine, theirs))
    for k in range(chunks):
        s, h, low = norm_call(
            residual[k], *finish_pair(*partial[k]), gains[0:1], shifts[0:1]
        )
        first_sum.append(s)
        hidden.append(h)
        hidden_pieces.append((low, swap_core(low)))
    gate_up, active, second_sum, result, result_pieces, partial = [], [], [], [], [], []
    for k in range(chunks):
        g, a, theirs, mine = mlp_call(*hidden_pieces[k], second_weight)
        gate_up.append(g)
        active.append(a)
        partial.append((mine, theirs))
    for k in range(chunks):
        s, y, low = norm_call(hidden[k], *finish_pair(*partial[k]), gains[1:2], shifts[1:2])
        second_sum.append(s)
        result.append(y)
        result_pieces.append(low)
    saved = (
        pieces, queries, keys, values, keys_t, context, jnp.concatenate(logsum, axis=1),
        first_sum, [p for pair in hidden_pieces for p in pair], gate_up, active, second_sum,
    )
    return result, result_pieces, saved


def layer_backward(incoming, saved, first_weight, second_weight, gains, tables, parity, count):
    (
        pieces, queries, keys, values, keys_t, context, logsum,
        first_sum, hidden_pieces, gate_up, active, second_sum,
    ) = saved
    chunks = len(incoming)
    second_grad, mixed, vectors_two = [], [], 0.0
    for k in range(chunks):
        grad, low, vector = norm_back_call(incoming[k], second_sum[k], gains[1:2])
        second_grad.append(grad)
        vectors_two = vectors_two + vector
        mixed.append((low, swap_core(low)))
    pair_grads, partial = [], []
    for k in range(chunks):
        dg, theirs, mine = mlp_back_call(*mixed[k], gate_up[k], second_weight)
        pair_grads.append(dg)
        partial.append((mine, theirs))
    first_grad, attended, context_grad, vectors_one = [], [], [], 0.0
    for k in range(chunks):
        incoming_k = (second_grad[k], *finish_pair(*partial[k]))
        grad, low, vector = norm_back_call(incoming_k, first_sum[k], gains[0:1])
        first_grad.append(grad)
        vectors_one = vectors_one + vector
        attended.append((low, swap_core(low)))
        context_grad.append(context_back_call(*attended[k], first_weight))
    flat = lambda pairs: [p for pair in pairs for p in pair]
    second_grads = weight_call(
        parity, [(hidden_pieces, pair_grads), (flat(mixed), active)], count
    )
    triple = attend_back_call(
        queries, jnp.concatenate(context_grad, axis=0), logsum, keys, values, keys_t, *tables[:2]
    )
    first_grads = weight_call(parity, [(pieces, [triple]), (flat(attended), context)], count)
    return first_grad, triple, first_grads, second_grads, (vectors_one, vectors_two)


def rotary_tables(length):
    half = HD // 2
    angles = np.arange(length, dtype=np.float64)[:, None] * np.exp(
        np.arange(half, dtype=np.float64)[None, :] * (-2.0 * math.log(rotary_base) / HD)
    )
    cosine, sine = np.cos(angles), np.sin(angles)
    return (
        np.concatenate([cosine] * 4, axis=1).astype(np.float32),
        np.concatenate([-sine, sine] * 2, axis=1).astype(np.float32),
    )


def deal(tokens, dealing_order, quarter_index):
    count, part, width = tokens.shape
    share = part // 4
    mine = lax.dynamic_slice_in_dim(tokens, quarter_index * share, share, 1)
    picked = jnp.take(mine, dealing_order, axis=0)
    arrived = lax.all_to_all(picked, "dp", split_axis=0, concat_axis=0, tiled=True)
    far = swap_x(arrived)
    pieces = jnp.stack([arrived, swap_core(arrived), far, swap_core(far)])
    blocks = [
        lax.dynamic_index_in_dim(pieces, quarter_index ^ slot, 0, keepdims=False)
        for slot in range(4)
    ]
    return jnp.stack(blocks, axis=1).reshape(count * part, width)


def on_device(
    tokens, dealing_order, lengths, project_weight, gate_up_weight, output_weight, down_weight,
    norm_gains, norm_biases, cotangent,
):
    dp_index = lax.axis_index("dp")
    tensor_index = lax.axis_index("tensor")
    core, side = tensor_index % 2, tensor_index // 2
    count, part, width = tokens.shape
    dp_count = lax.axis_size("dp")
    length = 4 * cotangent.shape[1]
    quarter = length // 4
    chunks = 2
    inner = output_weight.shape[1]
    hidden = down_weight.shape[1]
    rows_here = project_weight.shape[1]

    def shards(layer):
        first = jnp.concatenate(
            [project_weight[layer].reshape(rows_here, -1), output_weight[layer].T], axis=1
        ).astype(BF16)
        second = jnp.concatenate(
            [gate_up_weight[layer].reshape(rows_here, -1), down_weight[layer].T], axis=1
        ).astype(BF16)
        return first, second

    weights = [tuple(gather_rows(shard) for shard in shards(0))]
    for layer in range(1, LAYERS):
        weights.append(
            tuple(lax.all_gather(shard, "dp", axis=0, tiled=True) for shard in shards(layer))
        )

    length_now = jnp.take(lengths, jnp.take(dealing_order, dp_index))

    def local_order(rows):
        split = rows.reshape(chunks, 2, quarter, rows.shape[-1])
        return jnp.where(core == 0, split, split[:, ::-1])

    places = jnp.arange(length)[:, None]
    marks = jnp.where(places < length_now, 0.0, -1e30).astype(F32)
    tables = tuple(
        local_order(table).reshape(length, 128)
        for table in (*map(jnp.asarray, rotary_tables(length)), jnp.broadcast_to(marks, (length, 128)))
    )
    usable = [
        ((2 * k + core) * quarter + jnp.arange(quarter) < length_now)[:, None]
        for k in range(chunks)
    ]

    dealt = local_order(deal(tokens, dealing_order, tensor_index))
    pieces = [dealt[k, h] for k in range(chunks) for h in range(2)]
    current = pieces[::2]
    saved_all = []
    for layer in range(LAYERS):
        current, low, saved = layer_forward(
            pieces, current, *weights[layer], norm_gains[layer], norm_biases[layer], tables, inner
        )
        saved_all.append(saved)
        if layer < LAYERS - 1:
            pieces = [p for piece in low for p in (piece, swap_core(piece))]
    shown = jnp.where(side == 0, current[0], current[1])
    shown_usable = jnp.where(side == 0, usable[0], usable[1])
    layer_outputs = jnp.where(shown_usable, shown, 0.0)[None]

    own = cotangent[0]
    other = swap_x(own)
    seeds = [jnp.where(side == 0, own, other), jnp.where(side == 0, other, own)]
    incoming = [(jnp.where(usable[k], seeds[k], jnp.zeros_like(own)),) for k in range(chunks)]
    parity = (dp_index % 2).astype(jnp.int32).reshape(1)
    first_sets, second_sets, norm_sets = [], [], []
    for layer in reversed(range(LAYERS)):
        first_grad, triple, first_grads, second_grads, vectors = layer_backward(
            incoming, saved_all[layer], *weights[layer], norm_gains[layer], tables, parity, dp_count
        )
        if layer:
            partial = [input_back_call(k, chunks, triple, weights[layer][0]) for k in range(chunks)]
            incoming = [
                (first_grad[k], *finish_pair(partial[k][1], partial[k][0])) for k in range(chunks)
            ]
        first_sets.insert(0, scatter_sum(*first_grads))
        second_sets.insert(0, scatter_sum(*second_grads))
        norm_sets.insert(0, jnp.stack(vectors))
    norms_total = sum_everywhere(jnp.stack(norm_sets) * 0.5)

    where = jnp.stack([core, side]).astype(jnp.int32)
    kept, sent = input_last_call(where, triple, weights[0][0], first_grad)
    pair = (kept + swap_core(sent).astype(F32)).reshape(count, 2, part // 2, width // 2)
    mine = lax.dynamic_index_in_dim(pair, side, 1, keepdims=False)
    theirs = lax.dynamic_index_in_dim(pair, 1 - side, 1, keepdims=False).astype(BF16)
    total = (mine + swap_x(theirs).astype(F32)).astype(BF16)
    received = lax.all_to_all(total, "dp", split_axis=0, concat_axis=0, tiled=True)
    other = swap_x(received)
    half = jnp.where(
        side == 0,
        jnp.concatenate([received, other], axis=1),
        jnp.concatenate([other, received], axis=1),
    )
    other = swap_core(half)
    full = jnp.where(
        core == 0,
        jnp.concatenate([half, other], axis=2),
        jnp.concatenate([other, half], axis=2),
    )
    returned = jnp.take(full, jnp.argsort(dealing_order), axis=0).astype(F32)

    first_total, second_total = jnp.stack(first_sets), jnp.stack(second_sets)
    return (
        layer_outputs,
        returned,
        first_total[..., : 3 * inner].reshape(project_weight.shape),
        second_total[..., : 2 * hidden].reshape(gate_up_weight.shape),
        jnp.swapaxes(first_total[..., 3 * inner :], 1, 2),
        jnp.swapaxes(second_total[..., 2 * hidden :], 1, 2),
        norms_total[:, :, 0],
        norms_total[:, :, 1],
    )


def solution(mesh):
    placed = (
        P(None, "dp", None),
        P(),
        P(),
        P(None, "dp", None, "tensor"),
        P(None, "dp", None, "tensor"),
        P(None, "tensor", "dp"),
        P(None, "tensor", "dp"),
        P(),
        P(),
        P("dp", "tensor", None),
    )
    return jax.shard_map(
        on_device,
        mesh=mesh,
        in_specs=placed,
        out_specs=(
            P("dp", "tensor", None),
            P(None, "dp", None),
            P(None, "dp", None, "tensor"),
            P(None, "dp", None, "tensor"),
            P(None, "tensor", "dp"),
            P(None, "tensor", "dp"),
            P(),
            P(),
        ),
        check_vma=False,
    )
```

```python
import functools
import math

import jax
import jax.numpy as jnp
import numpy as np
from jax import lax
from jax.experimental import pallas as pl
from jax.experimental.pallas import tpu as pltpu
from jax.sharding import PartitionSpec as P

HD = 64
LAYERS = 2
epsilon = 1e-05
rotary_base = 1000.0
LOG2E = math.log2(math.e)
F32 = jnp.float32
BF16 = jnp.bfloat16
VMEM_LIMIT = 12 * 1024 * 1024
COST = 0.001
KEEP = True


def sds(*shape, dtype=BF16):
    return jax.ShapeDtypeStruct(shape, dtype)


class Order:
    last = ()
    waiting = ()
    kept = []


def keep(*arrays):
    Order.kept.extend(arrays)


def drop(*arrays):
    gone = {id(a) for a in arrays}
    Order.kept = [a for a in Order.kept if id(a) not in gone]


def call(kernel, outs, *operands, flops=0, trans=0, scalars=0, after=(), alias=None):
    after = (*after, *Order.waiting, *Order.last)
    Order.waiting = ()
    taken = {id(a) for a in operands}
    held = [a for a in Order.kept if id(a) not in taken] if KEEP else []
    vmem = pl.BlockSpec(memory_space=pltpu.VMEM)
    smem = pl.BlockSpec(memory_space=pltpu.SMEM)
    moved = sum(a.size * a.dtype.itemsize for a in list(operands) + list(outs))
    used = len(operands)

    def body(*refs):
        kernel(*refs[:used], *refs[used + len(held) + len(after) :])

    results = pl.pallas_call(
        body,
        in_specs=[smem] * scalars
        + [vmem] * (used - scalars + len(held))
        + [pl.BlockSpec(memory_space=pl.ANY)] * len(after),
        out_specs=[vmem] * len(outs),
        out_shape=list(outs),
        input_output_aliases=alias or {},
        compiler_params=pltpu.CompilerParams(vmem_limit_bytes=VMEM_LIMIT),
        cost_estimate=pl.CostEstimate(
            flops=int(COST * flops),
            bytes_accessed=int(COST * moved),
            transcendentals=int(COST * trans),
        ),
    )(*operands, *held, *after)
    Order.last = (min(results, key=lambda r: r.size * r.dtype.itemsize),)
    return results


def swap_core(value):
    return lax.ppermute(value, "tensor", [(i, i ^ 1) for i in range(lax.axis_size("tensor"))])


def swap_x(value):
    return lax.ppermute(value, "tensor", [(i, i ^ 2) for i in range(lax.axis_size("tensor"))])


def swap_dp(value, step):
    return lax.ppermute(value, "dp", [(i, i ^ step) for i in range(lax.axis_size("dp"))])


def stepwise(rows):
    return lax.axis_size("dp") == 8 and rows % 16 == 0


def place_kernel(spots, split, index_ref, *refs):
    *pieces, first_ref, second_ref = refs
    rows = pieces[0].shape[0]
    for (offset, column), piece in zip(spots, pieces):
        here = pl.ds(pl.multiple_of((index_ref[3] ^ offset) * rows, rows), rows)
        width = piece.shape[1]
        if column < split:
            first_ref[here, :] = piece[:, :split]
            second_ref[here, : width - split] = piece[:, split:]
        else:
            second_ref[here, column - split : column - split + width] = piece[...]


def copy_kernel(in_ref, out_ref):
    out_ref[...] = in_ref[...]


def gather_start(shard, halves):
    if not stepwise(shard.shape[0]):
        return {(0, 0): lax.all_gather(shard, "dp", axis=0, tiled=True)}
    pieces = {(0, 0): shard, (1, 0): swap_dp(shard, 1)}
    for step in (2, 4, 6):
        column = 0
        for part in halves if step > 2 else [shard]:
            along = swap_dp(part, step)
            pieces[step, column] = along
            pieces[step + 1, column] = swap_dp(along, 1)
            column += part.shape[1]
    return pieces


def first_gather(shard, meanwhile):
    if not stepwise(shard.shape[0]):
        for step in meanwhile:
            step()
        return {(0, 0): lax.all_gather(shard, "dp", axis=0, tiled=True)}
    pieces = {(0, 0): shard, (1, 0): swap_dp(shard, 1)}
    sent, across = shard, pieces[1, 0]
    for number, step in enumerate((4, 6, 2)):
        along = swap_dp(sent, step)
        pieces[step, 0] = along
        if step != 2:
            sent = call(copy_kernel, [sds(*shard.shape)], shard, after=[along, across])[0]
        across = pieces[step + 1, 0] = swap_dp(along, 1)
        if number < len(meanwhile):
            meanwhile[number]()
    return pieces


def gather_finish(where, pieces, split, after=()):
    if len(pieces) == 1:
        whole = pieces[0, 0]
        return whole[:, :split], whole[:, split:]
    rows, width = pieces[0, 0].shape
    outs = [sds(8 * rows, n) for n in (split, width - split)]
    return call(
        functools.partial(place_kernel, tuple(pieces), split),
        outs, where, *pieces.values(), scalars=1, after=after,
    )


def scatter_add_kernel(index_ref, kept_ref, *refs):
    steps = kept_ref.shape[0]
    other_refs, out_refs = refs[:-steps], refs[-steps:]
    own = index_ref[3] // 2
    for step, out_ref in enumerate(out_refs):
        start = 0
        for other_ref in other_refs:
            here = pl.ds(start, other_ref.shape[2])
            total = kept_ref[own ^ step, :, here].astype(F32) + other_ref[own ^ step].astype(F32)
            out_ref[:, here] = total.astype(BF16)
            start += other_ref.shape[2]


def scatter_start(sums):
    if isinstance(sums, (list, tuple)):
        return [sums[0]] + [swap_dp(part, 1) for part in sums[1:]]
    return [lax.psum_scatter(sums, "dp", scatter_dimension=0, tiled=True)]


def scatter_finish(where, started):
    if len(started) == 1:
        return started
    kept, *others = started
    count, rows, width = kept.shape
    outs = call(scatter_add_kernel, [sds(rows, width)] * count, where, kept, *others, scalars=1)
    return [outs[0]] + [swap_dp(out, 2 * step) for step, out in enumerate(outs) if step]


def total_kernel(*refs):
    *in_refs, out_ref = refs
    out_ref[...] = total_of(in_refs)


def total_call(parts):
    rows, width = parts[0].shape[-2:]
    return [call(total_kernel, [sds(rows, width, dtype=F32)], *parts)[0]]


def dot_nt(left, right):
    return lax.dot_general(left, right, (((1,), (1,)), ((), ())), preferred_element_type=F32)


def dot_nn(left, right):
    return lax.dot_general(left, right, (((1,), (0,)), ((), ())), preferred_element_type=F32)


def dot_tn(left, right):
    return lax.dot_general(left, right, (((0,), (0,)), ((), ())), preferred_element_type=F32)


def swap_halves(values):
    width = values.shape[-1]
    lane = lax.broadcasted_iota(jnp.int32, values.shape, 1)
    return jnp.where(
        lane % HD < HD // 2,
        pltpu.roll(values, width - HD // 2, 1),
        pltpu.roll(values, HD // 2, 1),
    )


def widen(table, width):
    return jnp.concatenate([table] * (width // table.shape[1]), axis=1)


def qkv_kernel(*refs):
    *x_refs, w_ref, cos_ref, sin_ref, bias_ref, q_ref, k_ref, v_ref, kt_ref, vt_ref = refs
    inner = v_ref.shape[1]
    extra = q_ref.shape[1] - inner
    weight = w_ref[:, : 3 * inner]
    block = 256
    parts = [
        x_ref.at[pl.ds(start, block), :]
        for x_ref in x_refs
        for start in range(0, x_ref.shape[0], block)
    ]
    for step, x_ref in enumerate(parts):
        here = pl.ds(step * block, block)
        projected = dot_nn(x_ref[...], weight)
        pair = projected[:, : 2 * inner]
        turned = pair * widen(cos_ref[here, :], 2 * inner) + swap_halves(pair) * widen(
            sin_ref[here, :], 2 * inner
        )
        lane = lax.broadcasted_iota(jnp.int32, (block, extra), 1)
        queries = turned[:, :inner] * (1.0 / math.sqrt(HD))
        keys = turned[:, inner:]
        values = projected[:, 2 * inner :]
        one = jnp.where(lane == 0, 1.0, 0.0)
        mark = jnp.where(lane == 0, bias_ref[here, :extra], 0.0)
        q_ref[here, :] = jnp.concatenate([queries, one], axis=1).astype(BF16)
        k_ref[here, :] = jnp.concatenate([keys, mark], axis=1).astype(BF16)
        v_ref[here, :] = values.astype(BF16)
        kt_ref[:, here] = keys.T.astype(BF16)
        vt_ref[:, here] = values.T.astype(BF16)


def qkv_call(pieces, weight, tables, inner, after):
    rows = sum(p.shape[0] for p in pieces)
    width = weight.shape[0]
    return call(
        qkv_kernel,
        [sds(rows, inner + HD), sds(rows, inner + HD), sds(rows, inner)] + [sds(inner, rows)] * 2,
        *pieces, weight, *tables,
        flops=2 * rows * width * 3 * inner,
        after=after,
    )


def head_mask(shape, head, inner):
    lane = lax.broadcasted_iota(jnp.int32, shape, 1)
    return ((lane >= head * HD) & (lane < (head + 1) * HD)) | (lane >= inner)


def attend_kernel(part, q_ref, k_ref, vt_ref, w_ref, c_ref, lse_ref, out_ref):
    rows, inner = c_ref.shape
    queries = q_ref[pl.ds(part * rows, rows), :]
    columns, stats = [], []
    for head in range(inner // HD):
        masked = jnp.where(head_mask(queries.shape, head, inner), queries, 0)
        scores = dot_nt(k_ref[...], masked)
        shift = jnp.max(scores, axis=0, keepdims=True) * LOG2E
        exps = jnp.exp2(scores * LOG2E - shift)
        total = jnp.sum(exps, axis=0, keepdims=True)
        mixed = dot_nn(vt_ref[head * HD : (head + 1) * HD, :], exps.astype(BF16))
        columns.append(mixed * (1.0 / total))
        stats.append(shift + jnp.log2(total))
    context = jnp.concatenate(columns, axis=0).T.astype(BF16)
    c_ref[...] = context
    pad = lse_ref.shape[0] - len(stats)
    lse_ref[...] = jnp.concatenate(stats + [jnp.zeros((pad, rows), F32)], axis=0)
    out_ref[...] = dot_nt(context, w_ref[:, 3 * inner :]).astype(out_ref.dtype)


def attend_call(part, queries, keys, values_t, weight, dtype, after=()):
    length, padded = queries.shape
    rows, inner, width = length // 4, padded - HD, weight.shape[0]
    return call(
        functools.partial(attend_kernel, part),
        [sds(rows, inner), sds(8, rows, dtype=F32), sds(rows, width, dtype=dtype)],
        queries, keys, values_t, weight,
        flops=4 * rows * length * 256 * (inner // HD) + 2 * rows * inner * width,
        trans=rows * length * (inner // HD),
        after=after,
    )


def norm_kernel(base_ref, pair_ref, other_ref, gain_ref, shift_ref, low_ref, normal_ref, scale_ref, *out):
    values = base_ref[...].astype(F32) + (pair_ref[...] + other_ref[...].astype(F32))
    centred = values - jnp.mean(values, axis=-1, keepdims=True)
    scaled = lax.rsqrt(jnp.mean(centred * centred, axis=-1, keepdims=True) + epsilon)
    normal = centred * scaled
    result = normal * gain_ref[...] + shift_ref[...]
    low_ref[...] = result.astype(BF16)
    normal_ref[...] = normal.astype(BF16)
    scale_ref[...] = jnp.broadcast_to(scaled, scale_ref.shape)
    for ref in out:
        ref[...] = result


def norm_call(base, pair, other, gain, shift, last, after=()):
    rows, width = pair.shape
    return call(
        norm_kernel,
        [sds(rows, width), sds(rows, width), sds(rows, 128, dtype=F32)]
        + [sds(rows, width, dtype=F32)] * last,
        base, pair, other, gain, shift,
        flops=10 * rows * width,
        after=after,
    )


def norm_back_kernel(*refs):
    *in_refs, normal_ref, scale_ref, gain_ref, low_ref, vec_ref = refs
    incoming = in_refs[0][...].astype(F32)
    for ref in in_refs[1:]:
        incoming = incoming + ref[...].astype(F32)
    normal = normal_ref[...].astype(F32)
    weighted = incoming * gain_ref[...]
    result = scale_ref[:, 0:1] * (
        weighted
        - jnp.mean(weighted, axis=-1, keepdims=True)
        - normal * jnp.mean(weighted * normal, axis=-1, keepdims=True)
    )
    low_ref[...] = result.astype(BF16)
    vec_ref[0:1, :] = jnp.sum(incoming * normal, axis=0, keepdims=True)
    vec_ref[1:2, :] = jnp.sum(incoming, axis=0, keepdims=True)


def norm_back_call(incoming, normal, scale, gain, after=()):
    rows, width = normal.shape
    return call(
        norm_back_kernel,
        [sds(rows, width), sds(2, width, dtype=F32)],
        *incoming, normal, scale, gain,
        flops=16 * rows * width,
        after=after,
    )


def mask_of(where_ref, chunk, rows):
    place = lax.broadcasted_iota(jnp.int32, (rows, 128), 0)
    usable = (2 * chunk + where_ref[0]) * rows + place < where_ref[4]
    return jnp.where(usable, 1.0, 0.0)[:, 0:1]


def seed_kernel(chunk, where_ref, own_ref, other_ref, out_ref):
    seed = jnp.where(where_ref[1] == chunk, own_ref[...].astype(F32), other_ref[...].astype(F32))
    out_ref[...] = (seed * mask_of(where_ref, chunk, out_ref.shape[0])).astype(BF16)


def show_kernel(where_ref, first_ref, second_ref, out_ref):
    rows = out_ref.shape[0]
    first = first_ref[...] * mask_of(where_ref, 0, rows)
    second = second_ref[...] * mask_of(where_ref, 1, rows)
    out_ref[...] = jnp.where(where_ref[1] == 0, first, second)


def gather_vectors_kernel(*refs):
    *in_refs, out_ref = refs
    for row in range(out_ref.shape[0] // 2):
        pair = in_refs[2 * row][...] + in_refs[2 * row + 1][...]
        out_ref[2 * row : 2 * row + 2, :] = pair * 0.5


def norms_kernel(left_ref, right_ref, gains_ref, biases_ref):
    for row in range(left_ref.shape[0] // 2):
        for member, out_ref in enumerate((gains_ref, biases_ref)):
            here = pl.ds(2 * row + member, 1)
            out_ref[row // 2, pl.ds(row % 2, 1), :] = left_ref[here, :] + right_ref[here, :]


def add_kernel(left_ref, right_ref, out_ref):
    total = left_ref[...].astype(F32) + right_ref[...].astype(F32)
    out_ref[...] = total.astype(out_ref.dtype)


def add_call(left, right, dtype, after=()):
    return call(add_kernel, [sds(*left.shape, dtype=dtype)], left, right, after=after)[0]


def mlp_parts(w_ref):
    hidden = w_ref.shape[1] // 3
    return [w_ref[:, part * hidden : (part + 1) * hidden] for part in range(3)]


def mlp_kernel(x_ref, w_ref, out_ref):
    gate_weight, up_weight, down_weight = mlp_parts(w_ref)
    rows = x_ref[...]
    gate = dot_nn(rows, gate_weight)
    up = dot_nn(rows, up_weight)
    active = (gate * jax.nn.sigmoid(gate) * up).astype(BF16)
    out_ref[...] = dot_nt(active, down_weight).astype(out_ref.dtype)


def mlp_call(piece, weight, dtype):
    rows, width = piece.shape
    return call(
        mlp_kernel, [sds(rows, width, dtype=dtype)], piece, weight,
        flops=2 * rows * width * weight.shape[1],
        trans=rows * weight.shape[1] // 3,
    )[0]


def mlp_back_kernel(x_ref, grad_ref, w_ref, act_ref, dg_ref, out_ref):
    gate_weight, up_weight, down_weight = mlp_parts(w_ref)
    hidden = act_ref.shape[1]
    rows = x_ref[...]
    gate = dot_nn(rows, gate_weight)
    up = dot_nn(rows, up_weight)
    active_grad = dot_nn(grad_ref[...], down_weight)
    sigmoid = jax.nn.sigmoid(gate)
    silu = gate * sigmoid
    act_ref[...] = (silu * up).astype(BF16)
    gate_grad = (active_grad * up * sigmoid * (1.0 + gate * (1.0 - sigmoid))).astype(BF16)
    up_grad = (active_grad * silu).astype(BF16)
    dg_ref[:, :hidden] = gate_grad
    dg_ref[:, hidden:] = up_grad
    partial = dot_nt(gate_grad, gate_weight) + dot_nt(up_grad, up_weight)
    out_ref[...] = partial.astype(out_ref.dtype)


def mlp_back_call(piece, grad, weight, dtype):
    rows, width = piece.shape
    hidden = weight.shape[1] // 3
    return call(
        mlp_back_kernel,
        [sds(rows, hidden), sds(rows, 2 * hidden), sds(rows, width, dtype=dtype)],
        piece, grad, weight,
        flops=10 * rows * width * hidden,
        trans=rows * hidden,
    )


def context_back_kernel(mine_in, theirs_in, w_ref, dc_ref):
    inner = dc_ref.shape[1]
    half = mine_in.shape[0]
    weight = w_ref[:, 3 * inner :]
    dc_ref[:half, :] = dot_nn(mine_in[...], weight).astype(BF16)
    dc_ref[half:, :] = dot_nn(theirs_in[...], weight).astype(BF16)


def context_back_call(mine, theirs, weight):
    half, width = mine.shape
    inner = weight.shape[1] // 4
    return call(
        context_back_kernel, [sds(2 * half, inner)], mine, theirs, weight,
        flops=4 * half * width * inner,
    )[0]


def attend_back_kernel(
    first, last, q_ref, dc_ref, lse_ref, k_ref, v_ref, kt_ref, cos_ref, sin_ref, *refs
):
    if first:
        dk_in, dv_in, *refs = refs
    if last and first:
        dq_in, *refs = refs
    dq_ref, dk_ref, dv_ref = refs
    rows, inner = dc_ref.shape
    length, padded = k_ref.shape
    block = min(256, rows)

    def turn_back(gradient, cosine, sine):
        cosine = widen(cosine, gradient.shape[1])
        sine = widen(sine, gradient.shape[1])
        return (gradient * cosine - swap_halves(gradient) * sine)[:, :inner]

    if first:
        dk_ref[...] = dk_in[...]
        dv_ref[...] = dv_in[...]
    else:
        dk_ref[...] = jnp.zeros_like(dk_ref)
        dv_ref[...] = jnp.zeros_like(dv_ref)

    def step_of(step, carry):
        start = pl.multiple_of(step * block, block)
        here = pl.ds(start, block)
        there = pl.ds(pl.multiple_of(first + step * block, block), block)
        queries = q_ref[there, :]
        context_grad = dc_ref[here, :]
        columns = []
        for head in range(inner // HD):
            masked = jnp.where(head_mask(queries.shape, head, inner), queries, 0)
            masked_grad = jnp.where(head_mask(context_grad.shape, head, inner), context_grad, 0)
            scores = dot_nt(k_ref[...], masked)
            weights = jnp.exp2(scores * LOG2E - lse_ref[head : head + 1, there])
            weight_grad = dot_nt(v_ref[...], masked_grad)
            inner_sum = jnp.sum(weights * weight_grad, axis=0, keepdims=True)
            score_grad = (weights * (weight_grad - inner_sum)).astype(BF16)
            dk_ref[...] += dot_nn(score_grad, masked)
            dv_ref[...] += dot_nn(weights.astype(BF16), masked_grad)
            columns.append(dot_nn(kt_ref[head * HD : (head + 1) * HD, :], score_grad))
        columns.append(jnp.zeros((padded - inner, block), F32))
        query_grad = jnp.concatenate(columns, axis=0).T * (1.0 / math.sqrt(HD))
        turned = turn_back(query_grad, cos_ref[there, :], sin_ref[there, :]).astype(BF16)
        dq_ref[there if last else here, :inner] = turned
        return carry

    lax.fori_loop(0, rows // block, step_of, 0)
    if last:
        if first:
            dq_ref[:first, :inner] = dq_in[...]
        dq_ref[:, inner : 2 * inner] = turn_back(dk_ref[...], cos_ref[...], sin_ref[...]).astype(
            BF16
        )
        dq_ref[:, 2 * inner :] = dv_ref[...].astype(BF16)


def attend_back_call(first, last, operands, carried, after):
    length, padded = operands[0].shape
    rows, inner = operands[1].shape
    out = sds(length, 3 * inner) if last else sds(rows, inner)
    return call(
        functools.partial(attend_back_kernel, first, last),
        [out, sds(length, padded, dtype=F32), sds(length, inner, dtype=F32)],
        *operands, *carried,
        flops=10 * rows * length * 256 * (inner // HD),
        trans=rows * length * (inner // HD),
        after=after,
    )


def input_back_kernel(part, dp_ref, w_ref, out_ref):
    rows = out_ref.shape[0]
    here = pl.ds(part * rows, rows)
    out_ref[...] = dot_nt(dp_ref[here, :], w_ref[:, : dp_ref.shape[1]]).astype(out_ref.dtype)


def input_back_call(part, triple, weight, dtype, after=()):
    rows, width = triple.shape[0] // 4, weight.shape[0]
    return call(
        functools.partial(input_back_kernel, part),
        [sds(rows, width, dtype=dtype)],
        triple, weight,
        flops=2 * rows * triple.shape[1] * width,
        after=after,
    )[0]


def input_last_kernel(index_ref, dp_ref, w_ref, *refs):
    *grad_refs, kept_ref, sent_ref = refs
    core, side = index_ref[0], index_ref[1]
    rows, total = dp_ref.shape
    quarter = rows // 4
    split = kept_ref.shape[1]
    weight = w_ref[:, :total]
    for step in range(4):
        chunk, part = step // 2, step % 2
        partial = dot_nt(dp_ref[pl.ds(step * quarter, quarter), :], weight)
        if not part:
            partial = partial + jnp.where(side == chunk, grad_refs[chunk][...].astype(F32), 0.0)
        start = pl.multiple_of((2 * chunk + (core ^ part)) * quarter, quarter)
        low, high = partial[:, :split], partial[:, split:]
        kept_ref[pl.ds(start, quarter), :] = jnp.where(core == 0, low, high)
        sent_ref[pl.ds(start, quarter), :] = jnp.where(core == 0, high, low).astype(BF16)


def input_last_call(index, triple, weight, grads, after):
    rows, width = triple.shape[0], weight.shape[0]
    return call(
        input_last_kernel,
        [sds(rows, width // 2, dtype=F32), sds(rows, width // 2)],
        index, triple, weight, *grads,
        flops=2 * rows * triple.shape[1] * width, scalars=1, after=after,
    )


def side_kernel(index_ref, kept_ref, other_ref, mine_ref, theirs_ref):
    side = index_ref[1]
    count, half, _ = mine_ref.shape
    for block in range(count):
        halves = []
        for part in range(2):
            here = pl.ds((2 * block + part) * half, half)
            halves.append(kept_ref[here, :] + other_ref[here, :].astype(F32))
        mine_ref[block] = jnp.where(side == 0, halves[0], halves[1])
        theirs_ref[block] = jnp.where(side == 0, halves[1], halves[0]).astype(BF16)


SHARE = 768


def weight_kernel(counts, index_ref, *refs):
    in_count = sum(left + right for left, right in counts)
    in_refs, (kept_ref, *sent_refs) = refs[:in_count], refs[in_count:]
    blocks, rows, _ = kept_ref.shape
    width = blocks * rows * (2 if sent_refs else 1)
    wide = 4 * rows if width % (4 * rows) == 0 and (4 * rows) % 128 == 0 else width
    column = 0
    lefts, rights = [], []
    for left_count, right_count in counts:
        lefts.append(in_refs[:left_count])
        rights.append(in_refs[left_count : left_count + right_count])
        in_refs = in_refs[left_count + right_count :]
    for left, right in zip(lefts, rights):
        columns = right[0].shape[1]
        share = min(columns, SHARE)
        ratio = len(left) // len(right)
        for start in range(0, columns, share):
            for first in range(0, width, wide):
                total = None
                for number, left_ref in enumerate(left):
                    size = left_ref.shape[0]
                    right_ref = right[number // ratio]
                    term = dot_tn(
                        left_ref[:, first : first + wide],
                        right_ref[
                            pl.ds((number % ratio) * size, size), start : start + share
                        ],
                    )
                    total = term if total is None else total + term
                where = pl.ds(column + start, share)
                there = pl.ds((column + start) % SHARE, share)
                for offset in range(0, wide, 2 * rows):
                    even = total[offset : offset + rows].astype(BF16)
                    odd = total[offset + rows : offset + 2 * rows].astype(BF16)
                    block = (first + offset) // (2 * rows)
                    if not sent_refs:
                        kept_ref[2 * block, :, where] = even
                        kept_ref[2 * block + 1, :, where] = odd
                    else:
                        sent_ref = sent_refs[(column + start) // SHARE]
                        kept_ref[block, :, where] = jnp.where(index_ref[5] == 0, even, odd)
                        sent_ref[block, :, there] = jnp.where(index_ref[5] == 0, odd, even)
        column += columns


def weight_call(parity, pairs, count, after=()):
    width = pairs[0][0][0].shape[1]
    total = sum(right[0].shape[1] for _, right in pairs)
    rows = sum(piece.shape[0] for piece in pairs[0][0])
    operands = [piece for left, right in pairs for piece in (*left, *right)]
    counts = tuple((len(left), len(right)) for left, right in pairs)
    flops = 2 * rows * width * total
    if parity is None:
        return call(
            functools.partial(weight_kernel, counts, None),
            [sds(count, width // count, total)],
            *operands, flops=flops, after=after,
        )[0]
    shape = (count // 2, width // count)
    return call(
        functools.partial(weight_kernel, counts),
        [sds(*shape, total)] + [sds(*shape, SHARE)] * (total // SHARE),
        parity, *operands, flops=flops, scalars=1, after=after,
    )


def total_of(refs):
    parts = [
        part
        for ref in refs
        for part in ([ref[i] for i in range(ref.shape[0])] if len(ref.shape) == 3 else [ref[...]])
    ]
    total = parts[0].astype(F32)
    for part in parts[1:]:
        total = total + part.astype(F32)
    return total


def grads_kernel(counts, *refs):
    out_refs = refs[-4:]
    position = 0
    for layer, groups in enumerate(counts):
        parts = []
        for count in groups:
            parts.append(total_of(refs[position : position + count]))
            position += count
        whole = jnp.concatenate(parts, axis=1)
        project_ref, gate_up_ref, output_ref, down_ref = out_refs
        inner, hidden = output_ref.shape[1], down_ref.shape[2]
        for part in range(3):
            project_ref[layer, part] = whole[:, part * inner : (part + 1) * inner]
        output_ref[layer] = whole[:, 3 * inner : 4 * inner].T
        for part in range(2):
            start = 4 * inner + part * hidden
            gate_up_ref[layer, :, part, :] = whole[:, start : start + hidden]
        down_ref[layer] = whole[:, 4 * inner + 2 * hidden :]


def last_kernel(
    turned, order_ref, where_ref, near_ref, far_ref, near_other_ref, far_other_ref, out_ref
):
    core, side = where_ref[0], where_ref[1]
    count, half, split = near_ref.shape
    for source in range(count):
        target = order_ref[where_ref[3] ^ source if turned else source]
        for ref, flip in ((near_ref, 0), (far_ref, 1)):
            here = pl.ds(pl.multiple_of((side ^ flip) * half, half), half)
            other = near_other_ref if ref is near_ref else far_other_ref
            own, swapped = ref[source].astype(F32), other[source].astype(F32)
            out_ref[target, here, :split] = jnp.where(core == 0, own, swapped)
            out_ref[target, here, split:] = jnp.where(core == 0, swapped, own)


def pair_kernel(mine_ref, other_ref, pair_ref, low_ref):
    pair = mine_ref[...] + other_ref[...].astype(F32)
    pair_ref[...] = pair
    low_ref[...] = pair.astype(BF16)


def finish_pair(mine, theirs, after=()):
    other = swap_core(theirs)
    outs = [sds(*mine.shape, dtype=F32), sds(*mine.shape)]
    pair, low = call(pair_kernel, outs, mine, other, after=after)
    return pair, swap_x(low)


def layer_forward(
    pieces, residual, first_weight, second_weight, gains, shifts, tables, inner, last, at
):
    chunks = len(residual)
    queries, keys, values, keys_t, values_t = qkv_call(
        pieces, first_weight, tables, inner, ()
    )
    keep(*pieces, queries, keys, values, keys_t, values_t, first_weight)
    context, logsum, first_norm, hidden_pieces, pairs = [], [], [], [], []
    for k in range(chunks):
        args = (queries, keys, values_t, first_weight)
        theirs = attend_call(2 * k + 1, *args, BF16)
        keep(theirs[0])
        mine = attend_call(2 * k, *args, F32)
        keep(mine[0])
        context += [mine[0], theirs[0]]
        logsum += [mine[1], theirs[1]]
        pairs.append(finish_pair(mine[2], theirs[2], at(("pair", k))))
    drop(values_t)
    logsum = jnp.concatenate(logsum, axis=1)
    keep(logsum)
    if callable(second_weight):
        second_weight = second_weight()
    second_norm, result, result_pieces, second_pairs = [], [], [], []
    for k in range(chunks):
        low, *kept = norm_call(
            residual[k], *pairs[k], gains[0:1], shifts[0:1], False, at(("norm_one", k))
        )
        first_norm.append(kept)
        hidden_pieces += [low, swap_core(low)]
        keep(*kept)
        mine = mlp_call(hidden_pieces[2 * k], second_weight, F32)
        keep(hidden_pieces[2 * k], second_weight)
        theirs = mlp_call(hidden_pieces[2 * k + 1], second_weight, BF16)
        keep(hidden_pieces[2 * k + 1])
        second_pairs.append(finish_pair(mine, theirs))
    for k in range(chunks):
        low, *kept = norm_call(
            hidden_pieces[2 * k], *second_pairs[k], gains[1:2], shifts[1:2], last,
            at(("norm_two", k)),
        )
        keep(*kept[:2])
        second_norm.append(kept[:2])
        result += kept[2:]
        result_pieces.append(low)
    saved = (
        pieces, queries, keys, values, keys_t, context, logsum,
        first_norm, hidden_pieces, second_norm, first_weight, second_weight,
    )
    return result, result_pieces, saved


def layer_backward(incoming, saved, gains, tables, parity, count, at):
    (
        pieces, queries, keys, values, keys_t, context, logsum,
        first_norm, hidden_pieces, second_norm, first_weight, second_weight,
    ) = saved
    chunks = len(incoming)
    mixed, active, vectors_two, pair_grads, pairs = [], [], [], [], []
    for k in range(chunks):
        low, vector = norm_back_call(
            incoming[k], *second_norm[k], gains[1:2], at(("norm_two", k))
        )
        drop(*second_norm[k])
        vectors_two.append(vector)
        mixed += [low, swap_core(low)]
        for h, dtype in ((0, F32), (1, BF16)):
            act, grad, out = mlp_back_call(
                hidden_pieces[2 * k + h], mixed[2 * k + h], second_weight, dtype
            )
            keep(act, grad, mixed[2 * k + h])
            active.append(act)
            pair_grads.append(grad)
            if h == 0:
                mine = out
        pairs.append(finish_pair(mine, out))
    drop(second_weight)
    at("sums")
    late = scatter_start(
        weight_call(parity, [(hidden_pieces, pair_grads), (mixed, active)], count)
    )
    at(late)
    drop(*hidden_pieces, *pair_grads, *active, *mixed[1::2])
    attended, vectors_one, carried = [], [], ()
    for k in range(chunks):
        low, vector = norm_back_call(
            (mixed[2 * k], *pairs[k]), *first_norm[k], gains[0:1], at(("norm_one", k))
        )
        drop(*first_norm[k], mixed[2 * k])
        vectors_one.append(vector)
        if k == chunks - 1:
            at(("vectors", vectors_one + vectors_two))
        attended += [low, swap_core(low)]
        context_grad = context_back_call(*attended[2 * k :], first_weight)
        keep(*attended[2 * k :])
        operands = (queries, context_grad, logsum, keys, values, keys_t, *tables[:2])
        out, dk, dv = attend_back_call(
            k * context_grad.shape[0], k == chunks - 1, operands, carried, at(("attend_back", k))
        )
        carried = (dk, dv, out)
        at(("attend", k))
    drop(queries, logsum, keys, values, keys_t)
    return out, (pieces, attended, context), late


def rotary_tables(length):
    half = HD // 2
    angles = np.arange(length, dtype=np.float64)[:, None] * np.exp(
        np.arange(half, dtype=np.float64)[None, :] * (-2.0 * math.log(rotary_base) / HD)
    )
    cosine, sine = np.cos(angles), np.sin(angles)
    return (
        np.concatenate([cosine] * 4, axis=1).astype(np.float32),
        np.concatenate([-sine, sine] * 2, axis=1).astype(np.float32),
    )


def turn_kernel(where_ref, in_ref, *out_refs):
    index = where_ref[3]
    for step in range(4):
        for flip in range(2):
            out_refs[flip][step] = in_ref[index ^ (2 * step + flip)]


def couple_kernel(own_ref, other_ref, *out_refs):
    for step, out_ref in enumerate(out_refs):
        out_ref[0] = own_ref[step]
        out_ref[1] = other_ref[step]


def join_kernel(*refs):
    *in_refs, out_ref = refs
    for step, ref in enumerate(in_refs):
        out_ref[2 * step : 2 * step + 2] = ref[...]


def exchange_start(blocks, where):
    _, rows, width = blocks.shape
    own, sent = call(turn_kernel, [sds(4, rows, width)] * 2, where, blocks, scalars=1)
    return own, swap_dp(sent, 1)


def exchange_middle(own, sent, after=()):
    _, rows, width = own.shape
    pairs = call(couple_kernel, [sds(2, rows, width)] * 4, own, sent, after=after)
    return [pairs[0]] + [swap_dp(pairs[step], 2 * step) for step in (1, 2, 3)]


def exchange_finish(moved, after=()):
    _, rows, width = moved[0].shape
    return call(join_kernel, [sds(8, rows, width)], *moved, after=after)[0]


def deal_kernel(where_ref, *refs):
    *in_refs, out_ref = refs
    core, own, index = where_ref[0], where_ref[2], where_ref[3]
    count, share, _ = in_refs[0].shape
    part = out_ref.shape[0] // count
    for step in range(count):
        source = index ^ step
        quarter = source // 2
        block = 2 * ((quarter // 2) * 2 + ((quarter % 2) ^ core)) + source % 2
        for offset, ref in enumerate(in_refs):
            start = pl.multiple_of(block * part + (own ^ offset) * share, share)
            out_ref[pl.ds(start, share), :] = ref[step]


def deal_steps(tokens, dealing_order, where):
    count, part, width = tokens.shape
    share = part // 4
    mine = lax.dynamic_slice_in_dim(tokens, where[2] * share, share, 1)
    picked = jnp.take(mine, dealing_order, axis=0)
    state = []

    def spread(arrived):
        far = swap_x(arrived)
        state[:] = [arrived, swap_core(arrived), far, swap_core(far)]

    if count != 8 or share % 16:
        spread(lax.all_to_all(picked, "dp", split_axis=0, concat_axis=0, tiled=True))
        return [], state
    state[:] = exchange_start(picked, where)

    def middle():
        state[:] = exchange_middle(*state)

    def finish():
        spread(exchange_finish(state))

    return [middle, finish], state


def deal_finish(pieces, where, local_order):
    count, share, width = pieces[0].shape
    length = 4 * count * share
    if count == 8 and share % 16 == 0:
        return call(deal_kernel, [sds(length, width)], where, *pieces, scalars=1)[0]
    stacked = jnp.stack(pieces)
    blocks = [
        lax.dynamic_index_in_dim(stacked, where[2] ^ slot, 0, keepdims=False) for slot in range(4)
    ]
    whole = jnp.stack(blocks, axis=1).reshape(length, width)
    return local_order(whole).reshape(length, width)


def pack_kernel(project_ref, gate_up_ref, output_ref, down_ref, *out_refs):
    inner, hidden = output_ref.shape[1], down_ref.shape[2]
    columns = [project_ref[0, part] for part in range(3)] + [output_ref[0].T]
    columns += [gate_up_ref[0, :, part] for part in range(2)] + [down_ref[0]]
    start = 0
    for column in columns:
        low, size = column.astype(BF16), column.shape[1]
        first = 0
        for ref in out_refs[1:]:
            last = first + ref.shape[1]
            if first <= start < last:
                ref[:, start - first : start - first + size] = low
            first = last
        out_refs[0][:, start : start + size] = low
        start += size


def pack_call(layer, halves, project, gate_up, output, down, after=()):
    operands = (jnp.swapaxes(project, 1, 2), gate_up, output, jnp.swapaxes(down, 1, 2))
    rows, inner, hidden = project.shape[1], output.shape[1], down.shape[1]
    total, cut = 4 * inner + 3 * hidden, 4 * inner + hidden
    outs = [sds(rows, n) for n in ([total, cut, total - cut] if halves else [total])]
    after = (*after, *Order.last)

    def spec(w):
        return pl.BlockSpec((1, *w.shape[1:]), lambda i: (layer,) + (0,) * (w.ndim - 1))

    def body(*refs):
        pack_kernel(*refs[:4], *refs[4 + len(after) :])

    results = pl.pallas_call(
        body,
        grid=(1,),
        in_specs=[spec(w) for w in operands] + [pl.BlockSpec(memory_space=pl.ANY)] * len(after),
        out_specs=[pl.BlockSpec(out.shape, lambda i: (0, 0)) for out in outs],
        out_shape=outs,
        compiler_params=pltpu.CompilerParams(vmem_limit_bytes=VMEM_LIMIT),
        cost_estimate=pl.CostEstimate(flops=0, bytes_accessed=1000, transcendentals=0),
    )(*operands, *after)
    Order.last = (results[-1],)
    return results


def on_device(
    tokens, dealing_order, lengths, project_weight, gate_up_weight, output_weight, down_weight,
    norm_gains, norm_biases, cotangent,
):
    Order.last, Order.waiting, Order.kept = (), (), []
    dp_index = lax.axis_index("dp")
    tensor_index = lax.axis_index("tensor")
    core, side = tensor_index % 2, tensor_index // 2
    count, part, width = tokens.shape
    dp_count = lax.axis_size("dp")
    length = 4 * cotangent.shape[1]
    quarter = length // 4
    chunks = 2
    inner = output_weight.shape[1]
    hidden = down_weight.shape[1]
    rows_here = project_weight.shape[1]

    sources = (project_weight, gate_up_weight, output_weight, down_weight)
    length_now = jnp.take(lengths, jnp.take(dealing_order, dp_index))
    where = jnp.stack([core, side, tensor_index, dp_index, length_now, dp_index % 2]).astype(jnp.int32)
    own = cotangent[0]
    other = swap_x(own)

    def local_order(rows):
        split = rows.reshape(chunks, 2, quarter, rows.shape[-1])
        return jnp.where(core == 0, split, split[:, ::-1])

    places = jnp.arange(length)[:, None]
    marks = jnp.where(places < length_now, 0.0, -1e30).astype(F32)
    tables = tuple(
        local_order(table).reshape(length, 128)
        for table in (*map(jnp.asarray, rotary_tables(length)), jnp.broadcast_to(marks, (length, 128)))
    )
    shard = pack_call(0, False, *sources)[0]
    meanwhile, moving = deal_steps(tokens, dealing_order, where)
    started = [first_gather(shard, meanwhile)]
    weights, saved_all = [], []
    keep(*tables[:2])
    for layer in range(LAYERS):
        points = {}
        if layer < LAYERS - 1:
            before = [started[layer][key] for key in ((2, 0), (7, 0))] if len(started[layer]) > 1 else ()
            packed = pack_call(layer + 1, True, *sources, after=before)
            started.append(gather_start(packed[0], packed[1:]))
            if len(started[-1]) > 1:
                cut = packed[1].shape[1]
                points = {
                    "place": ((2, 0),),
                    ("pair", 0): ((4, 0),),
                    ("norm_one", 0): ((4, cut), (3, 0)),
                    ("norm_one", 1): ((6, 0), (1, 0), (5, 0)),
                    ("norm_two", 0): ((6, cut), (5, cut)),
                    ("norm_two", 1): ((7, 0),),
                }

        def at(point, points=points):
            return tuple(started[-1][key] for key in points.get(point, ()))

        weights.append(gather_finish(where, started[layer], 4 * inner, at("place")))
        if layer == 0:
            dealt = deal_finish(moving, where, local_order)
            pieces = [dealt]
            residual = [dealt[2 * k * quarter : (2 * k + 1) * quarter] for k in range(chunks)]
        current, residual, saved = layer_forward(
            pieces, residual, *weights[layer], norm_gains[layer], norm_biases[layer], tables,
            inner, layer == LAYERS - 1, at,
        )
        saved_all.append(saved)
        if layer < LAYERS - 1:
            pieces = [p for piece in residual for p in (piece, swap_core(piece))]
    layer_outputs = call(
        show_kernel, [sds(quarter, width, dtype=F32)], where, *current, scalars=1
    )
    incoming = [
        call(
            functools.partial(seed_kernel, k), [sds(quarter, width)], where, own, other, scalars=1
        )
        for k in range(chunks)
    ]
    received, vectors, steps = [None] * LAYERS, [None] * LAYERS, []
    for step in (1, 2):
        steps.append(lambda v, s=step: lax.ppermute(v, "tensor", [(i, i ^ s) for i in range(4)]))
    step = 1
    while step < dp_count:
        steps.append(functools.partial(swap_dp, step=step))
        step *= 2
    split = where if stepwise(rows_here) else None
    own_sums, above = {}, {}

    def sum_norms(index):
        if index < len(steps):
            own_sums["norms"] = add_call(own_sums["norms"], steps[index](own_sums["norms"]), F32)

    def at(layer, point):
        if isinstance(point, list):
            own_sums["second"] = point
            return ()
        if point[0] == "vectors":
            vectors[layer] = point[1]
            if layer == 0:
                flat = [v for group in vectors for v in group]
                own_sums["norms"] = call(
                    gather_vectors_kernel, [sds(len(flat), width, dtype=F32)], *flat
                )[0]
            return ()
        if split is None:
            return ()
        if layer:
            after = {("norm_one", 0): 1, ("norm_one", 1): 2, ("input", 0): 3}
        else:
            after = {("attend_back", 0): 1, ("attend_back", 1): 2, "input": 3}
        if point in after:
            return (own_sums["second"][after[point]],)
        if layer == LAYERS - 1:
            return ()
        if point == "sums":
            above["first"] = scatter_finish(where, above["first"])
        after = {
            ("norm_two", 0): ("second", 1), ("norm_two", 1): ("second", 2),
            ("norm_one", 0): ("second", 3), ("norm_one", 1): ("first", 1),
        }
        if point in after:
            name, number = after[point]
            return tuple(above[name][number : number + 3]) if name == "first" else (above[name][number],)
        return ()

    for layer in reversed(range(LAYERS)):
        triple, (rows_in, attended, context), late = layer_backward(
            incoming, saved_all[layer], norm_gains[layer], tables, split, dp_count,
            functools.partial(at, layer),
        )
        first_weight = weights[layer][0]
        if layer:
            incoming = []
            for k in range(chunks):
                theirs = input_back_call(
                    2 * k + 1, triple, first_weight, BF16, at(layer, ("input", k))
                )
                mine = input_back_call(2 * k, triple, first_weight, F32)
                incoming.append((attended[2 * k], *finish_pair(mine, theirs)))
            drop(first_weight)
            above["second"] = scatter_finish(where, late)
            sums = weight_call(split, [(rows_in, [triple]), (attended, context)], dp_count)
            drop(*rows_in, *attended[1::2], *context)
            above["first"] = scatter_start(sums)
            if split is None:
                above["first"] = scatter_finish(where, above["first"])

    kept, sent = input_last_call(where, triple, first_weight, attended[::2], at(0, "input"))
    sent = swap_core(sent)
    drop(first_weight, *tables[:2])
    second_sum = scatter_finish(where, late)
    arriving = [second_sum[step : step + 1] for step in (2, 3, 1)]
    sum_norms(0)
    sums = weight_call(split, [(rows_in, [triple]), (attended, context)], dp_count)
    Order.kept = []
    sums = scatter_start(sums)
    mine, theirs = call(
        side_kernel,
        [sds(count, part // 2, width // 2, dtype=F32), sds(count, part // 2, width // 2)],
        where, kept, sent, scalars=1,
    )
    sum_norms(1)
    total = add_call(mine, swap_x(theirs), BF16, arriving[0])
    if split is None:
        near = lax.all_to_all(total, "dp", split_axis=0, concat_axis=0, tiled=True)
        first_sum = scatter_finish(where, sums)
    else:
        moving = exchange_start(total, where)
        first_sum = scatter_finish(where, sums)
        sum_norms(2)
        moving = exchange_middle(*moving, arriving[1])
        sum_norms(3)
        near = exchange_finish(moving, arriving[2])
    far = swap_x(near)
    for index in range(2 if split is None else 4, len(steps) - 1):
        sum_norms(index)
    norms = own_sums["norms"]
    gains_total, biases_total = call(
        norms_kernel, [sds(LAYERS, 2, width, dtype=F32)] * 2, norms, steps[-1](norms)
    )
    received[1] = [total_call(above["first"]), total_call(above["second"])]
    received[0] = [first_sum, second_sum]
    returned = call(
        functools.partial(last_kernel, split is not None), [sds(count, part, width, dtype=F32)],
        dealing_order, where, near, far, swap_core(near), swap_core(far), scalars=2,
        after=first_sum[1:],
    )[0]

    shapes = (
        jnp.swapaxes(project_weight, 1, 2), gate_up_weight, output_weight,
        jnp.swapaxes(down_weight, 1, 2),
    )
    project_grad, gate_up_grad, output_grad, down_grad = call(
        functools.partial(grads_kernel, tuple(tuple(len(g) for g in r) for r in received)),
        [sds(*w.shape, dtype=F32) for w in shapes],
        *[r for groups in received for group in groups for r in group],
    )
    return (
        layer_outputs[0][None], returned, jnp.swapaxes(project_grad, 1, 2), gate_up_grad, output_grad,
        jnp.swapaxes(down_grad, 1, 2), gains_total, biases_total,
    )


def solution(mesh):
    placed = (
        P(None, "dp", None),
        P(),
        P(),
        P(None, "dp", None, "tensor"),
        P(None, "dp", None, "tensor"),
        P(None, "tensor", "dp"),
        P(None, "tensor", "dp"),
        P(),
        P(),
        P("dp", "tensor", None),
    )
    return jax.shard_map(
        on_device,
        mesh=mesh,
        in_specs=placed,
        out_specs=(
            P("dp", "tensor", None),
            P(None, "dp", None),
            P(None, "dp", None, "tensor"),
            P(None, "dp", None, "tensor"),
            P(None, "tensor", "dp"),
            P(None, "tensor", "dp"),
            P(),
            P(),
        ),
        check_vma=False,
    )
```

```python
import functools
import math

import jax
import jax.numpy as jnp
import numpy as np
from jax import lax
from jax.experimental import pallas as pl
from jax.experimental.pallas import tpu as pltpu
from jax.sharding import PartitionSpec as P

HD = 64
LAYERS = 2
epsilon = 1e-05
rotary_base = 1000.0
LOG2E = math.log2(math.e)
F32 = jnp.float32
BF16 = jnp.bfloat16
VMEM_LIMIT = 12 * 1024 * 1024
COST = 0.001
KEEP = True


def sds(*shape, dtype=BF16):
    return jax.ShapeDtypeStruct(shape, dtype)


class Order:
    last = ()
    waiting = ()
    kept = []


def keep(*arrays):
    Order.kept.extend(arrays)


def drop(*arrays):
    gone = {id(a) for a in arrays}
    Order.kept = [a for a in Order.kept if id(a) not in gone]


def call(kernel, outs, *operands, flops=0, trans=0, scalars=0, after=(), alias=None):
    after = (*after, *Order.waiting, *Order.last)
    Order.waiting = ()
    taken = {id(a) for a in operands}
    held = [a for a in Order.kept if id(a) not in taken] if KEEP else []
    vmem = pl.BlockSpec(memory_space=pltpu.VMEM)
    smem = pl.BlockSpec(memory_space=pltpu.SMEM)
    moved = sum(a.size * a.dtype.itemsize for a in list(operands) + list(outs))
    used = len(operands)

    def body(*refs):
        kernel(*refs[:used], *refs[used + len(held) + len(after) :])

    results = pl.pallas_call(
        body,
        in_specs=[smem] * scalars
        + [vmem] * (used - scalars + len(held))
        + [pl.BlockSpec(memory_space=pl.ANY)] * len(after),
        out_specs=[vmem] * len(outs),
        out_shape=list(outs),
        input_output_aliases=alias or {},
        compiler_params=pltpu.CompilerParams(vmem_limit_bytes=VMEM_LIMIT),
        cost_estimate=pl.CostEstimate(
            flops=int(COST * flops),
            bytes_accessed=int(COST * moved),
            transcendentals=int(COST * trans),
        ),
    )(*operands, *held, *after)
    Order.last = (min(results, key=lambda r: r.size * r.dtype.itemsize),)
    return results


def swap_core(value):
    return lax.ppermute(value, "tensor", [(i, i ^ 1) for i in range(lax.axis_size("tensor"))])


def swap_x(value):
    return lax.ppermute(value, "tensor", [(i, i ^ 2) for i in range(lax.axis_size("tensor"))])


def swap_dp(value, step):
    return lax.ppermute(value, "dp", [(i, i ^ step) for i in range(lax.axis_size("dp"))])


def stepwise(rows):
    return lax.axis_size("dp") == 8 and rows % 16 == 0


def place_kernel(offsets, index_ref, *refs):
    pieces, out_refs = refs[: len(offsets)], refs[len(offsets) :]
    rows = pieces[0].shape[0]
    for offset, piece in zip(offsets, pieces):
        here = pl.ds(pl.multiple_of((index_ref[3] ^ offset) * rows, rows), rows)
        start = 0
        for out_ref in out_refs:
            last = start + out_ref.shape[1]
            out_ref[here, :] = piece[:, start:last]
            start = last


def copy_kernel(in_ref, out_ref):
    out_ref[...] = in_ref[...]


def gather_start(shard):
    if not stepwise(shard.shape[0]):
        return {0: lax.all_gather(shard, "dp", axis=0, tiled=True)}
    pieces = {0: shard, 1: swap_dp(shard, 1)}
    for step in (2, 4, 6):
        pieces[step] = swap_dp(shard, step)
        pieces[step + 1] = swap_dp(pieces[step], 1)
    return pieces


def first_gather(shard, meanwhile):
    if not stepwise(shard.shape[0]):
        for step in meanwhile:
            step()
        return {0: lax.all_gather(shard, "dp", axis=0, tiled=True)}
    pieces = {0: shard, 1: swap_dp(shard, 1), 2: swap_dp(shard, 2), 4: swap_dp(shard, 4)}
    after = [pieces[1], pieces[2], pieces[4]]
    for step in meanwhile:
        step()
    sent = call(copy_kernel, [sds(*shard.shape)], shard, after=after)[0]
    pieces[6] = swap_dp(sent, 6)
    for step in (2, 4, 6):
        pieces[step + 1] = swap_dp(pieces[step], 1)
    return pieces


def gather_finish(where, pieces, widths, after=()):
    if len(pieces) == 1:
        whole, parts = pieces[0], []
        for width in widths:
            parts.append(whole[:, :width])
            whole = whole[:, width:]
        return parts
    rows = pieces[0].shape[0]
    return call(
        functools.partial(place_kernel, tuple(pieces)),
        [sds(8 * rows, width) for width in widths],
        where, *pieces.values(), scalars=1, after=after,
    )


def scatter_add_kernel(index_ref, kept_ref, *refs):
    steps = kept_ref.shape[0]
    other_refs, out_refs = refs[:-steps], refs[-steps:]
    own = index_ref[3] // 2
    for step, out_ref in enumerate(out_refs):
        start = 0
        for other_ref in other_refs:
            here = pl.ds(start, other_ref.shape[2])
            total = kept_ref[own ^ step, :, here].astype(F32) + other_ref[own ^ step].astype(F32)
            out_ref[:, here] = total.astype(BF16)
            start += other_ref.shape[2]


def scatter_start(sums):
    if isinstance(sums, (list, tuple)):
        return [sums[0]] + [swap_dp(part, 1) for part in sums[1:]]
    return [lax.psum_scatter(sums, "dp", scatter_dimension=0, tiled=True)]


def scatter_finish(where, started):
    if len(started) == 1:
        return started
    kept, *others = started
    count, rows, width = kept.shape
    outs = call(scatter_add_kernel, [sds(rows, width)] * count, where, kept, *others, scalars=1)
    return [outs[0]] + [swap_dp(out, 2 * step) for step, out in enumerate(outs) if step]


def total_kernel(*refs):
    *in_refs, out_ref = refs
    out_ref[...] = total_of(in_refs)


def total_call(parts):
    rows, width = parts[0].shape[-2:]
    return [call(total_kernel, [sds(rows, width, dtype=F32)], *parts)[0]]


def dot_nt(left, right):
    return lax.dot_general(left, right, (((1,), (1,)), ((), ())), preferred_element_type=F32)


def dot_nn(left, right):
    return lax.dot_general(left, right, (((1,), (0,)), ((), ())), preferred_element_type=F32)


def dot_tn(left, right):
    return lax.dot_general(left, right, (((0,), (0,)), ((), ())), preferred_element_type=F32)


def swap_halves(values):
    width = values.shape[-1]
    lane = lax.broadcasted_iota(jnp.int32, values.shape, 1)
    return jnp.where(
        lane % HD < HD // 2,
        pltpu.roll(values, width - HD // 2, 1),
        pltpu.roll(values, HD // 2, 1),
    )


def widen(table, width):
    return jnp.concatenate([table] * (width // table.shape[1]), axis=1)


def qkv_kernel(*refs):
    *x_refs, w_ref, cos_ref, sin_ref, bias_ref, q_ref, k_ref, v_ref, kt_ref, vt_ref = refs
    inner = v_ref.shape[1]
    extra = q_ref.shape[1] - inner
    weight = w_ref[:, : 3 * inner]
    block = 256
    parts = [
        x_ref.at[pl.ds(start, block), :]
        for x_ref in x_refs
        for start in range(0, x_ref.shape[0], block)
    ]
    for step, x_ref in enumerate(parts):
        here = pl.ds(step * block, block)
        projected = dot_nn(x_ref[...], weight)
        pair = projected[:, : 2 * inner]
        turned = pair * widen(cos_ref[here, :], 2 * inner) + swap_halves(pair) * widen(
            sin_ref[here, :], 2 * inner
        )
        lane = lax.broadcasted_iota(jnp.int32, (block, extra), 1)
        queries = turned[:, :inner] * (1.0 / math.sqrt(HD))
        keys = turned[:, inner:]
        values = projected[:, 2 * inner :]
        one = jnp.where(lane == 0, 1.0, 0.0)
        mark = jnp.where(lane == 0, bias_ref[here, :extra], 0.0)
        q_ref[here, :] = jnp.concatenate([queries, one], axis=1).astype(BF16)
        k_ref[here, :] = jnp.concatenate([keys, mark], axis=1).astype(BF16)
        v_ref[here, :] = values.astype(BF16)
        kt_ref[:, here] = keys.T.astype(BF16)
        vt_ref[:, here] = values.T.astype(BF16)


def qkv_call(pieces, weight, tables, inner, after):
    rows = sum(p.shape[0] for p in pieces)
    width = weight.shape[0]
    return call(
        qkv_kernel,
        [sds(rows, inner + HD), sds(rows, inner + HD), sds(rows, inner)] + [sds(inner, rows)] * 2,
        *pieces, weight, *tables,
        flops=2 * rows * width * 3 * inner,
        after=after,
    )


def head_mask(shape, head, inner):
    lane = lax.broadcasted_iota(jnp.int32, shape, 1)
    return ((lane >= head * HD) & (lane < (head + 1) * HD)) | (lane >= inner)


def attend_kernel(part, q_ref, k_ref, vt_ref, w_ref, c_ref, lse_ref, out_ref):
    rows, inner = c_ref.shape
    queries = q_ref[pl.ds(part * rows, rows), :]
    columns, stats = [], []
    for head in range(inner // HD):
        masked = jnp.where(head_mask(queries.shape, head, inner), queries, 0)
        scores = dot_nt(k_ref[...], masked)
        shift = jnp.max(scores, axis=0, keepdims=True) * LOG2E
        exps = jnp.exp2(scores * LOG2E - shift)
        total = jnp.sum(exps, axis=0, keepdims=True)
        mixed = dot_nn(vt_ref[head * HD : (head + 1) * HD, :], exps.astype(BF16))
        columns.append(mixed * (1.0 / total))
        stats.append(shift + jnp.log2(total))
    context = jnp.concatenate(columns, axis=0).T.astype(BF16)
    c_ref[...] = context
    pad = lse_ref.shape[0] - len(stats)
    lse_ref[...] = jnp.concatenate(stats + [jnp.zeros((pad, rows), F32)], axis=0)
    out_ref[...] = dot_nt(context, w_ref[:, 3 * inner :]).astype(out_ref.dtype)


def attend_call(part, queries, keys, values_t, weight, dtype, after=()):
    length, padded = queries.shape
    rows, inner, width = length // 4, padded - HD, weight.shape[0]
    return call(
        functools.partial(attend_kernel, part),
        [sds(rows, inner), sds(8, rows, dtype=F32), sds(rows, width, dtype=dtype)],
        queries, keys, values_t, weight,
        flops=4 * rows * length * 256 * (inner // HD) + 2 * rows * inner * width,
        trans=rows * length * (inner // HD),
        after=after,
    )


def norm_kernel(base_ref, pair_ref, other_ref, gain_ref, shift_ref, low_ref, normal_ref, scale_ref, *out):
    values = base_ref[...].astype(F32) + (pair_ref[...] + other_ref[...].astype(F32))
    centred = values - jnp.mean(values, axis=-1, keepdims=True)
    scaled = lax.rsqrt(jnp.mean(centred * centred, axis=-1, keepdims=True) + epsilon)
    normal = centred * scaled
    result = normal * gain_ref[...] + shift_ref[...]
    low_ref[...] = result.astype(BF16)
    normal_ref[...] = normal.astype(BF16)
    scale_ref[...] = jnp.broadcast_to(scaled, scale_ref.shape)
    for ref in out:
        ref[...] = result


def norm_call(base, pair, other, gain, shift, last, after=()):
    rows, width = pair.shape
    return call(
        norm_kernel,
        [sds(rows, width), sds(rows, width), sds(rows, 128, dtype=F32)]
        + [sds(rows, width, dtype=F32)] * last,
        base, pair, other, gain, shift,
        flops=10 * rows * width,
        after=after,
    )


def norm_back_kernel(*refs):
    *in_refs, normal_ref, scale_ref, gain_ref, low_ref, vec_ref = refs
    incoming = in_refs[0][...].astype(F32)
    for ref in in_refs[1:]:
        incoming = incoming + ref[...].astype(F32)
    normal = normal_ref[...].astype(F32)
    weighted = incoming * gain_ref[...]
    result = scale_ref[:, 0:1] * (
        weighted
        - jnp.mean(weighted, axis=-1, keepdims=True)
        - normal * jnp.mean(weighted * normal, axis=-1, keepdims=True)
    )
    low_ref[...] = result.astype(BF16)
    vec_ref[0:1, :] = jnp.sum(incoming * normal, axis=0, keepdims=True)
    vec_ref[1:2, :] = jnp.sum(incoming, axis=0, keepdims=True)


def norm_back_call(incoming, normal, scale, gain, after=()):
    rows, width = normal.shape
    return call(
        norm_back_kernel,
        [sds(rows, width), sds(2, width, dtype=F32)],
        *incoming, normal, scale, gain,
        flops=16 * rows * width,
        after=after,
    )


def mask_of(where_ref, chunk, rows):
    place = lax.broadcasted_iota(jnp.int32, (rows, 128), 0)
    usable = (2 * chunk + where_ref[0]) * rows + place < where_ref[4]
    return jnp.where(usable, 1.0, 0.0)[:, 0:1]


def seed_kernel(chunk, where_ref, own_ref, other_ref, out_ref):
    seed = jnp.where(where_ref[1] == chunk, own_ref[...].astype(F32), other_ref[...].astype(F32))
    out_ref[...] = (seed * mask_of(where_ref, chunk, out_ref.shape[0])).astype(BF16)


def show_kernel(where_ref, first_ref, second_ref, out_ref):
    rows = out_ref.shape[0]
    first = first_ref[...] * mask_of(where_ref, 0, rows)
    second = second_ref[...] * mask_of(where_ref, 1, rows)
    out_ref[...] = jnp.where(where_ref[1] == 0, first, second)


def gather_vectors_kernel(*refs):
    *in_refs, out_ref = refs
    for row in range(out_ref.shape[0] // 2):
        pair = in_refs[2 * row][...] + in_refs[2 * row + 1][...]
        out_ref[2 * row : 2 * row + 2, :] = pair * 0.5


def norms_kernel(left_ref, right_ref, gains_ref, biases_ref):
    for row in range(left_ref.shape[0] // 2):
        for member, out_ref in enumerate((gains_ref, biases_ref)):
            here = pl.ds(2 * row + member, 1)
            out_ref[row // 2, pl.ds(row % 2, 1), :] = left_ref[here, :] + right_ref[here, :]


def add_kernel(left_ref, right_ref, out_ref):
    total = left_ref[...].astype(F32) + right_ref[...].astype(F32)
    out_ref[...] = total.astype(out_ref.dtype)


def add_call(left, right, dtype, after=()):
    return call(add_kernel, [sds(*left.shape, dtype=dtype)], left, right, after=after)[0]


def mlp_parts(w_ref):
    hidden = w_ref.shape[1] // 3
    return [w_ref[:, part * hidden : (part + 1) * hidden] for part in range(3)]


def mlp_kernel(x_ref, w_ref, out_ref):
    gate_weight, up_weight, down_weight = mlp_parts(w_ref)
    rows = x_ref[...]
    gate = dot_nn(rows, gate_weight)
    up = dot_nn(rows, up_weight)
    active = (gate * jax.nn.sigmoid(gate) * up).astype(BF16)
    out_ref[...] = dot_nt(active, down_weight).astype(out_ref.dtype)


def mlp_call(piece, weight, dtype):
    rows, width = piece.shape
    return call(
        mlp_kernel, [sds(rows, width, dtype=dtype)], piece, weight,
        flops=2 * rows * width * weight.shape[1],
        trans=rows * weight.shape[1] // 3,
    )[0]


def mlp_back_kernel(x_ref, grad_ref, w_ref, act_ref, dg_ref, out_ref):
    gate_weight, up_weight, down_weight = mlp_parts(w_ref)
    hidden = act_ref.shape[1]
    rows = x_ref[...]
    gate = dot_nn(rows, gate_weight)
    up = dot_nn(rows, up_weight)
    active_grad = dot_nn(grad_ref[...], down_weight)
    sigmoid = jax.nn.sigmoid(gate)
    silu = gate * sigmoid
    act_ref[...] = (silu * up).astype(BF16)
    gate_grad = (active_grad * up * sigmoid * (1.0 + gate * (1.0 - sigmoid))).astype(BF16)
    up_grad = (active_grad * silu).astype(BF16)
    dg_ref[:, :hidden] = gate_grad
    dg_ref[:, hidden:] = up_grad
    partial = dot_nt(gate_grad, gate_weight) + dot_nt(up_grad, up_weight)
    out_ref[...] = partial.astype(out_ref.dtype)


def mlp_back_call(piece, grad, weight, dtype):
    rows, width = piece.shape
    hidden = weight.shape[1] // 3
    return call(
        mlp_back_kernel,
        [sds(rows, hidden), sds(rows, 2 * hidden), sds(rows, width, dtype=dtype)],
        piece, grad, weight,
        flops=10 * rows * width * hidden,
        trans=rows * hidden,
    )


def context_back_kernel(mine_in, theirs_in, w_ref, dc_ref):
    inner = dc_ref.shape[1]
    half = mine_in.shape[0]
    weight = w_ref[:, 3 * inner :]
    dc_ref[:half, :] = dot_nn(mine_in[...], weight).astype(BF16)
    dc_ref[half:, :] = dot_nn(theirs_in[...], weight).astype(BF16)


def context_back_call(mine, theirs, weight):
    half, width = mine.shape
    inner = weight.shape[1] // 4
    return call(
        context_back_kernel, [sds(2 * half, inner)], mine, theirs, weight,
        flops=4 * half * width * inner,
    )[0]


def attend_back_kernel(
    first, last, q_ref, dc_ref, lse_ref, k_ref, v_ref, kt_ref, cos_ref, sin_ref, *refs
):
    if first:
        dk_in, dv_in, *refs = refs
    if last and first:
        dq_in, *refs = refs
    dq_ref, dk_ref, dv_ref = refs
    rows, inner = dc_ref.shape
    length, padded = k_ref.shape
    block = min(256, rows)

    def turn_back(gradient, cosine, sine):
        cosine = widen(cosine, gradient.shape[1])
        sine = widen(sine, gradient.shape[1])
        return (gradient * cosine - swap_halves(gradient) * sine)[:, :inner]

    if first:
        dk_ref[...] = dk_in[...]
        dv_ref[...] = dv_in[...]
    else:
        dk_ref[...] = jnp.zeros_like(dk_ref)
        dv_ref[...] = jnp.zeros_like(dv_ref)

    def step_of(step, carry):
        start = pl.multiple_of(step * block, block)
        here = pl.ds(start, block)
        there = pl.ds(pl.multiple_of(first + step * block, block), block)
        queries = q_ref[there, :]
        context_grad = dc_ref[here, :]
        columns = []
        for head in range(inner // HD):
            masked = jnp.where(head_mask(queries.shape, head, inner), queries, 0)
            masked_grad = jnp.where(head_mask(context_grad.shape, head, inner), context_grad, 0)
            scores = dot_nt(k_ref[...], masked)
            weights = jnp.exp2(scores * LOG2E - lse_ref[head : head + 1, there])
            weight_grad = dot_nt(v_ref[...], masked_grad)
            inner_sum = jnp.sum(weights * weight_grad, axis=0, keepdims=True)
            score_grad = (weights * (weight_grad - inner_sum)).astype(BF16)
            dk_ref[...] += dot_nn(score_grad, masked)
            dv_ref[...] += dot_nn(weights.astype(BF16), masked_grad)
            columns.append(dot_nn(kt_ref[head * HD : (head + 1) * HD, :], score_grad))
        columns.append(jnp.zeros((padded - inner, block), F32))
        query_grad = jnp.concatenate(columns, axis=0).T * (1.0 / math.sqrt(HD))
        turned = turn_back(query_grad, cos_ref[there, :], sin_ref[there, :]).astype(BF16)
        dq_ref[there if last else here, :inner] = turned
        return carry

    lax.fori_loop(0, rows // block, step_of, 0)
    if last:
        if first:
            dq_ref[:first, :inner] = dq_in[...]
        dq_ref[:, inner : 2 * inner] = turn_back(dk_ref[...], cos_ref[...], sin_ref[...]).astype(
            BF16
        )
        dq_ref[:, 2 * inner :] = dv_ref[...].astype(BF16)


def attend_back_call(first, last, operands, carried, after):
    length, padded = operands[0].shape
    rows, inner = operands[1].shape
    out = sds(length, 3 * inner) if last else sds(rows, inner)
    return call(
        functools.partial(attend_back_kernel, first, last),
        [out, sds(length, padded, dtype=F32), sds(length, inner, dtype=F32)],
        *operands, *carried,
        flops=10 * rows * length * 256 * (inner // HD),
        trans=rows * length * (inner // HD),
        after=after,
    )


def input_back_kernel(part, dp_ref, w_ref, out_ref):
    rows = out_ref.shape[0]
    here = pl.ds(part * rows, rows)
    out_ref[...] = dot_nt(dp_ref[here, :], w_ref[:, : dp_ref.shape[1]]).astype(out_ref.dtype)


def input_back_call(part, triple, weight, dtype, after=()):
    rows, width = triple.shape[0] // 4, weight.shape[0]
    return call(
        functools.partial(input_back_kernel, part),
        [sds(rows, width, dtype=dtype)],
        triple, weight,
        flops=2 * rows * triple.shape[1] * width,
        after=after,
    )[0]


def input_last_kernel(index_ref, dp_ref, w_ref, *refs):
    *grad_refs, kept_ref, sent_ref = refs
    core, side = index_ref[0], index_ref[1]
    rows, total = dp_ref.shape
    quarter = rows // 4
    split = kept_ref.shape[1]
    weight = w_ref[:, :total]
    for step in range(4):
        chunk, part = step // 2, step % 2
        partial = dot_nt(dp_ref[pl.ds(step * quarter, quarter), :], weight)
        if not part:
            partial = partial + jnp.where(side == chunk, grad_refs[chunk][...].astype(F32), 0.0)
        start = pl.multiple_of((2 * chunk + (core ^ part)) * quarter, quarter)
        low, high = partial[:, :split], partial[:, split:]
        kept_ref[pl.ds(start, quarter), :] = jnp.where(core == 0, low, high)
        sent_ref[pl.ds(start, quarter), :] = jnp.where(core == 0, high, low).astype(BF16)


def input_last_call(index, triple, weight, grads, after):
    rows, width = triple.shape[0], weight.shape[0]
    return call(
        input_last_kernel,
        [sds(rows, width // 2, dtype=F32), sds(rows, width // 2)],
        index, triple, weight, *grads,
        flops=2 * rows * triple.shape[1] * width, scalars=1, after=after,
    )


def side_kernel(index_ref, kept_ref, other_ref, mine_ref, theirs_ref):
    side = index_ref[1]
    count, half, _ = mine_ref.shape
    for block in range(count):
        halves = []
        for part in range(2):
            here = pl.ds((2 * block + part) * half, half)
            halves.append(kept_ref[here, :] + other_ref[here, :].astype(F32))
        mine_ref[block] = jnp.where(side == 0, halves[0], halves[1])
        theirs_ref[block] = jnp.where(side == 0, halves[1], halves[0]).astype(BF16)


SHARE = 768


def weight_kernel(counts, index_ref, *refs):
    in_count = sum(left + right for left, right in counts)
    in_refs, (kept_ref, *sent_refs) = refs[:in_count], refs[in_count:]
    blocks, rows, _ = kept_ref.shape
    width = blocks * rows * (2 if sent_refs else 1)
    wide = 4 * rows if width % (4 * rows) == 0 and (4 * rows) % 128 == 0 else width
    column = 0
    lefts, rights = [], []
    for left_count, right_count in counts:
        lefts.append(in_refs[:left_count])
        rights.append(in_refs[left_count : left_count + right_count])
        in_refs = in_refs[left_count + right_count :]
    for left, right in zip(lefts, rights):
        columns = right[0].shape[1]
        share = min(columns, SHARE)
        ratio = len(left) // len(right)
        for start in range(0, columns, share):
            for first in range(0, width, wide):
                total = None
                for number, left_ref in enumerate(left):
                    size = left_ref.shape[0]
                    right_ref = right[number // ratio]
                    term = dot_tn(
                        left_ref[:, first : first + wide],
                        right_ref[
                            pl.ds((number % ratio) * size, size), start : start + share
                        ],
                    )
                    total = term if total is None else total + term
                where = pl.ds(column + start, share)
                there = pl.ds((column + start) % SHARE, share)
                for offset in range(0, wide, 2 * rows):
                    even = total[offset : offset + rows].astype(BF16)
                    odd = total[offset + rows : offset + 2 * rows].astype(BF16)
                    block = (first + offset) // (2 * rows)
                    if not sent_refs:
                        kept_ref[2 * block, :, where] = even
                        kept_ref[2 * block + 1, :, where] = odd
                    else:
                        sent_ref = sent_refs[(column + start) // SHARE]
                        kept_ref[block, :, where] = jnp.where(index_ref[5] == 0, even, odd)
                        sent_ref[block, :, there] = jnp.where(index_ref[5] == 0, odd, even)
        column += columns


def weight_call(parity, pairs, count, after=()):
    width = pairs[0][0][0].shape[1]
    total = sum(right[0].shape[1] for _, right in pairs)
    rows = sum(piece.shape[0] for piece in pairs[0][0])
    operands = [piece for left, right in pairs for piece in (*left, *right)]
    counts = tuple((len(left), len(right)) for left, right in pairs)
    flops = 2 * rows * width * total
    if parity is None:
        return call(
            functools.partial(weight_kernel, counts, None),
            [sds(count, width // count, total)],
            *operands, flops=flops, after=after,
        )[0]
    shape = (count // 2, width // count)
    return call(
        functools.partial(weight_kernel, counts),
        [sds(*shape, total)] + [sds(*shape, SHARE)] * (total // SHARE),
        parity, *operands, flops=flops, scalars=1, after=after,
    )


def total_of(refs):
    parts = [
        part
        for ref in refs
        for part in ([ref[i] for i in range(ref.shape[0])] if len(ref.shape) == 3 else [ref[...]])
    ]
    total = parts[0].astype(F32)
    for part in parts[1:]:
        total = total + part.astype(F32)
    return total


def grads_kernel(counts, *refs):
    out_refs = refs[-4:]
    position = 0
    for layer, groups in enumerate(counts):
        parts = []
        for count in groups:
            parts.append(total_of(refs[position : position + count]))
            position += count
        whole = jnp.concatenate(parts, axis=1)
        project_ref, gate_up_ref, output_ref, down_ref = out_refs
        inner, hidden = output_ref.shape[1], down_ref.shape[2]
        for part in range(3):
            project_ref[layer, part] = whole[:, part * inner : (part + 1) * inner]
        output_ref[layer] = whole[:, 3 * inner : 4 * inner].T
        for part in range(2):
            start = 4 * inner + part * hidden
            gate_up_ref[layer, :, part, :] = whole[:, start : start + hidden]
        down_ref[layer] = whole[:, 4 * inner + 2 * hidden :]


def last_kernel(
    turned, order_ref, where_ref, near_ref, far_ref, near_other_ref, far_other_ref, out_ref
):
    core, side = where_ref[0], where_ref[1]
    count, half, split = near_ref.shape
    for source in range(count):
        target = order_ref[where_ref[3] ^ source if turned else source]
        for ref, flip in ((near_ref, 0), (far_ref, 1)):
            here = pl.ds(pl.multiple_of((side ^ flip) * half, half), half)
            other = near_other_ref if ref is near_ref else far_other_ref
            own, swapped = ref[source].astype(F32), other[source].astype(F32)
            out_ref[target, here, :split] = jnp.where(core == 0, own, swapped)
            out_ref[target, here, split:] = jnp.where(core == 0, swapped, own)


def pair_kernel(mine_ref, other_ref, pair_ref, low_ref):
    pair = mine_ref[...] + other_ref[...].astype(F32)
    pair_ref[...] = pair
    low_ref[...] = pair.astype(BF16)


def finish_pair(mine, theirs, after=()):
    other = swap_core(theirs)
    outs = [sds(*mine.shape, dtype=F32), sds(*mine.shape)]
    pair, low = call(pair_kernel, outs, mine, other, after=after)
    return pair, swap_x(low)


def layer_forward(
    pieces, residual, first_weight, second_weight, gains, shifts, tables, inner, last, at
):
    chunks = len(residual)
    queries, keys, values, keys_t, values_t = qkv_call(
        pieces, first_weight, tables, inner, ()
    )
    keep(*pieces, queries, keys, values, keys_t, values_t, first_weight)
    context, logsum, first_norm, hidden_pieces, pairs = [], [], [], [], []
    for k in range(chunks):
        args = (queries, keys, values_t, first_weight)
        theirs = attend_call(2 * k + 1, *args, BF16)
        keep(theirs[0])
        mine = attend_call(2 * k, *args, F32)
        keep(mine[0])
        context += [mine[0], theirs[0]]
        logsum += [mine[1], theirs[1]]
        pairs.append(finish_pair(mine[2], theirs[2], ()))
    drop(values_t)
    logsum = jnp.concatenate(logsum, axis=1)
    keep(logsum)
    second_norm, result, result_pieces, second_pairs = [], [], [], []
    mine, theirs = [], []
    for k in range(chunks):
        low, *kept = norm_call(
            residual[k], *pairs[k], gains[0:1], shifts[0:1], False, at(("norm_one", k))
        )
        first_norm.append(kept)
        hidden_pieces += [low, swap_core(low)]
        keep(*kept)
        if k == 0:
            second_weight = second_weight()
        mine.append(mlp_call(low, second_weight, F32))
        keep(low, second_weight)
    for k in range(chunks):
        theirs.append(mlp_call(hidden_pieces[2 * k + 1], second_weight, BF16))
        keep(hidden_pieces[2 * k + 1])
    for k in range(chunks):
        second_pairs.append(finish_pair(mine[k], theirs[k]))
    for k in range(chunks):
        low, *kept = norm_call(
            hidden_pieces[2 * k], *second_pairs[k], gains[1:2], shifts[1:2], last,
            at(("norm_two", k)),
        )
        keep(*kept[:2])
        second_norm.append(kept[:2])
        result += kept[2:]
        result_pieces.append(low)
    saved = (
        pieces, queries, keys, values, keys_t, context, logsum,
        first_norm, hidden_pieces, second_norm, first_weight, second_weight,
    )
    return result, result_pieces, saved


def layer_backward(incoming, saved, gains, tables, parity, count, at):
    (
        pieces, queries, keys, values, keys_t, context, logsum,
        first_norm, hidden_pieces, second_norm, first_weight, second_weight,
    ) = saved
    chunks = len(incoming)
    mixed, active, vectors_two, pair_grads, pairs = [], [], [], [], []
    outs = []
    for k in range(chunks):
        low, vector = norm_back_call(
            incoming[k], *second_norm[k], gains[1:2], at(("norm_two", k))
        )
        drop(*second_norm[k])
        vectors_two.append(vector)
        mixed += [low, swap_core(low)]
        outs += mlp_back_call(hidden_pieces[2 * k], low, second_weight, F32)
        keep(*outs[-3:-1], low)
    for k in range(chunks):
        outs += mlp_back_call(hidden_pieces[2 * k + 1], mixed[2 * k + 1], second_weight, BF16)
        keep(*outs[-3:-1], mixed[2 * k + 1])
    for k in range(chunks):
        here, there = outs[3 * k : 3 * k + 3], outs[3 * (chunks + k) : 3 * (chunks + k) + 3]
        active += [here[0], there[0]]
        pair_grads += [here[1], there[1]]
        pairs.append(finish_pair(here[2], there[2]))
    drop(second_weight)
    at("sums")
    late = scatter_start(
        weight_call(parity, [(hidden_pieces, pair_grads), (mixed, active)], count)
    )
    at(late)
    drop(*hidden_pieces, *pair_grads, *active, *mixed[1::2])
    attended, vectors_one, carried = [], [], ()
    for k in range(chunks):
        low, vector = norm_back_call(
            (mixed[2 * k], *pairs[k]), *first_norm[k], gains[0:1], at(("norm_one", k))
        )
        drop(*first_norm[k], mixed[2 * k])
        vectors_one.append(vector)
        if k == chunks - 1:
            at(("vectors", vectors_one + vectors_two))
        attended += [low, swap_core(low)]
        context_grad = context_back_call(*attended[2 * k :], first_weight)
        keep(*attended[2 * k :])
        operands = (queries, context_grad, logsum, keys, values, keys_t, *tables[:2])
        out, dk, dv = attend_back_call(
            k * context_grad.shape[0], k == chunks - 1, operands, carried, at(("attend_back", k))
        )
        carried = (dk, dv, out)
        at(("attend", k))
    drop(queries, logsum, keys, values, keys_t)
    return out, (pieces, attended, context), late


def rotary_tables(length):
    half = HD // 2
    angles = np.arange(length, dtype=np.float64)[:, None] * np.exp(
        np.arange(half, dtype=np.float64)[None, :] * (-2.0 * math.log(rotary_base) / HD)
    )
    cosine, sine = np.cos(angles), np.sin(angles)
    return (
        np.concatenate([cosine] * 4, axis=1).astype(np.float32),
        np.concatenate([-sine, sine] * 2, axis=1).astype(np.float32),
    )


def turn_kernel(where_ref, in_ref, *out_refs):
    index = where_ref[3]
    for step in range(4):
        for flip in range(2):
            out_refs[flip][step] = in_ref[index ^ (2 * step + flip)]


def couple_kernel(own_ref, other_ref, *out_refs):
    for step, out_ref in enumerate(out_refs):
        out_ref[0] = own_ref[step]
        out_ref[1] = other_ref[step]


def join_kernel(*refs):
    *in_refs, out_ref = refs
    for step, ref in enumerate(in_refs):
        out_ref[2 * step : 2 * step + 2] = ref[...]


def exchange_start(blocks, where):
    _, rows, width = blocks.shape
    own, sent = call(turn_kernel, [sds(4, rows, width)] * 2, where, blocks, scalars=1)
    return own, swap_dp(sent, 1)


def exchange_middle(own, sent, after=()):
    _, rows, width = own.shape
    pairs = call(couple_kernel, [sds(2, rows, width)] * 4, own, sent, after=after)
    return [pairs[0]] + [swap_dp(pairs[step], 2 * step) for step in (1, 2, 3)]


def exchange_finish(moved, after=()):
    _, rows, width = moved[0].shape
    return call(join_kernel, [sds(8, rows, width)], *moved, after=after)[0]


def deal_kernel(where_ref, *refs):
    *in_refs, out_ref = refs
    core, own, index = where_ref[0], where_ref[2], where_ref[3]
    count, share, _ = in_refs[0].shape
    part = out_ref.shape[0] // count
    for step in range(count):
        source = index ^ step
        quarter = source // 2
        block = 2 * ((quarter // 2) * 2 + ((quarter % 2) ^ core)) + source % 2
        for offset, ref in enumerate(in_refs):
            start = pl.multiple_of(block * part + (own ^ offset) * share, share)
            out_ref[pl.ds(start, share), :] = ref[step]


def deal_steps(tokens, dealing_order, where):
    count, part, width = tokens.shape
    share = part // 4
    mine = lax.dynamic_slice_in_dim(tokens, where[2] * share, share, 1)
    picked = jnp.take(mine, dealing_order, axis=0)
    state = []

    def spread(arrived):
        far = swap_x(arrived)
        state[:] = [arrived, swap_core(arrived), far, swap_core(far)]

    if count != 8 or share % 16:
        spread(lax.all_to_all(picked, "dp", split_axis=0, concat_axis=0, tiled=True))
        return [], state
    state[:] = exchange_start(picked, where)

    def middle():
        state[:] = exchange_middle(*state)

    def finish():
        spread(exchange_finish(state))

    return [middle, finish], state


def deal_finish(pieces, where, local_order):
    count, share, width = pieces[0].shape
    length = 4 * count * share
    if count == 8 and share % 16 == 0:
        return call(deal_kernel, [sds(length, width)], where, *pieces, scalars=1)[0]
    stacked = jnp.stack(pieces)
    blocks = [
        lax.dynamic_index_in_dim(stacked, where[2] ^ slot, 0, keepdims=False) for slot in range(4)
    ]
    whole = jnp.stack(blocks, axis=1).reshape(length, width)
    return local_order(whole).reshape(length, width)


def pack_kernel(project_ref, gate_up_ref, output_ref, down_ref, *out_refs):
    inner, hidden = output_ref.shape[1], down_ref.shape[2]
    columns = [project_ref[0, part] for part in range(3)] + [output_ref[0].T]
    columns += [gate_up_ref[0, :, part] for part in range(2)] + [down_ref[0]]
    for out_ref in out_refs:
        start = 0
        while start < out_ref.shape[1]:
            column = columns.pop(0)
            out_ref[:, start : start + column.shape[1]] = column.astype(BF16)
            start += column.shape[1]


def pack_call(layer, together, project, gate_up, output, down, after=()):
    operands = (jnp.swapaxes(project, 1, 2), gate_up, output, jnp.swapaxes(down, 1, 2))
    rows, inner, hidden = project.shape[1], output.shape[1], down.shape[1]
    sizes = [4 * inner, 3 * hidden]
    outs = [sds(rows, n) for n in ([sum(sizes)] if together else sizes)]
    after = (*after, *Order.last)

    def spec(w):
        return pl.BlockSpec((1, *w.shape[1:]), lambda i: (layer,) + (0,) * (w.ndim - 1))

    def body(*refs):
        pack_kernel(*refs[:4], *refs[4 + len(after) :])

    results = pl.pallas_call(
        body,
        grid=(1,),
        in_specs=[spec(w) for w in operands] + [pl.BlockSpec(memory_space=pl.ANY)] * len(after),
        out_specs=[pl.BlockSpec(out.shape, lambda i: (0, 0)) for out in outs],
        out_shape=outs,
        compiler_params=pltpu.CompilerParams(vmem_limit_bytes=VMEM_LIMIT),
        cost_estimate=pl.CostEstimate(flops=0, bytes_accessed=1000, transcendentals=0),
    )(*operands, *after)
    Order.last = (results[0],)
    return results


def on_device(
    tokens, dealing_order, lengths, project_weight, gate_up_weight, output_weight, down_weight,
    norm_gains, norm_biases, cotangent,
):
    Order.last, Order.waiting, Order.kept = (), (), []
    dp_index = lax.axis_index("dp")
    tensor_index = lax.axis_index("tensor")
    core, side = tensor_index % 2, tensor_index // 2
    count, part, width = tokens.shape
    dp_count = lax.axis_size("dp")
    length = 4 * cotangent.shape[1]
    quarter = length // 4
    chunks = 2
    inner = output_weight.shape[1]
    hidden = down_weight.shape[1]
    rows_here = project_weight.shape[1]

    sources = (project_weight, gate_up_weight, output_weight, down_weight)
    length_now = jnp.take(lengths, jnp.take(dealing_order, dp_index))
    where = jnp.stack([core, side, tensor_index, dp_index, length_now, dp_index % 2]).astype(jnp.int32)
    own = cotangent[0]
    other = swap_x(own)

    def local_order(rows):
        split = rows.reshape(chunks, 2, quarter, rows.shape[-1])
        return jnp.where(core == 0, split, split[:, ::-1])

    places = jnp.arange(length)[:, None]
    marks = jnp.where(places < length_now, 0.0, -1e30).astype(F32)
    tables = tuple(
        local_order(table).reshape(length, 128)
        for table in (*map(jnp.asarray, rotary_tables(length)), jnp.broadcast_to(marks, (length, 128)))
    )
    shard = pack_call(0, True, *sources)[0]
    meanwhile, moving = deal_steps(tokens, dealing_order, where)
    pieces = first_gather(shard, meanwhile)
    widths = (4 * inner, 3 * hidden)
    coming = [(pieces, None)]
    saved_all = []
    keep(*tables[:2])
    for layer in range(LAYERS):
        here, points = coming[layer], {}
        if layer < LAYERS - 1:
            before = [pieces[step] for step in (6, 3, 5)] if layer == 0 and len(pieces) > 1 else ()
            packed = pack_call(layer + 1, False, *sources, after=before)
            first, second = (gather_start(part) for part in packed)
            coming.append((first, second))
            if len(first) > 1:
                points = {
                    "place": (first, (2, 4, 6)),
                    ("norm_one", 0): (first, (1, 3, 5, 7)),
                    ("norm_one", 1): (second, (2, 4, 1)),
                    ("norm_two", 0): (second, (3,)),
                    ("norm_two", 1): (second, (6, 5)),
                }
        if layer and len(here[0]) > 1:
            points[("norm_one", 0)] = (here[1], (7,))

        def at(point, points=points):
            found, steps = points.get(point, ({}, ()))
            return tuple(found[step] for step in steps)

        if layer == 0:
            first_weight, second_weight = gather_finish(where, here[0], widths, at("place"))
            dealt = deal_finish(moving, where, local_order)
            pieces = [dealt]
            residual = [dealt[2 * k * quarter : (2 * k + 1) * quarter] for k in range(chunks)]
            late_weight = lambda: second_weight
        else:
            (first_weight,) = gather_finish(where, here[0], widths[:1])
            late_weight = lambda here=here: gather_finish(where, here[1], widths[1:])[0]
        current, residual, saved = layer_forward(
            pieces, residual, first_weight, late_weight, norm_gains[layer], norm_biases[layer],
            tables, inner, layer == LAYERS - 1, at,
        )
        saved_all.append(saved)
        if layer < LAYERS - 1:
            pieces = [p for piece in residual for p in (piece, swap_core(piece))]
    layer_outputs = call(
        show_kernel, [sds(quarter, width, dtype=F32)], where, *current, scalars=1
    )
    incoming = [
        call(
            functools.partial(seed_kernel, k), [sds(quarter, width)], where, own, other, scalars=1
        )
        for k in range(chunks)
    ]
    received, vectors, steps = [None] * LAYERS, [None] * LAYERS, []
    for step in (1, 2):
        steps.append(lambda v, s=step: lax.ppermute(v, "tensor", [(i, i ^ s) for i in range(4)]))
    step = 1
    while step < dp_count:
        steps.append(functools.partial(swap_dp, step=step))
        step *= 2
    split = where if stepwise(rows_here) else None
    own_sums, above = {}, {}

    def sum_norms(index):
        if index < len(steps):
            own_sums["norms"] = add_call(own_sums["norms"], steps[index](own_sums["norms"]), F32)

    def at(layer, point):
        if isinstance(point, list):
            own_sums["second"] = point
            return ()
        if point[0] == "vectors":
            vectors[layer] = point[1]
            if layer == 0:
                flat = [v for group in vectors for v in group]
                own_sums["norms"] = call(
                    gather_vectors_kernel, [sds(len(flat), width, dtype=F32)], *flat
                )[0]
            return ()
        if split is None:
            return ()
        if layer:
            after = {("norm_one", 0): 1, ("norm_one", 1): 2, ("input", 0): 3}
        else:
            after = {("norm_one", 1): 1, ("attend_back", 1): 2, "input": 3}
        found = ()
        if point in after:
            found = (own_sums["second"][after[point]],)
        if layer == LAYERS - 1:
            return found
        if point == ("norm_two", 1):
            return tuple(above["second"][1:3])
        if point == ("norm_one", 0):
            above["first"] = scatter_finish(where, above["first"])
        if point == ("norm_one", 1):
            return found + tuple(above["first"][1:])
        if point == ("attend_back", 1):
            return found + tuple(above["second"][3:])
        return found

    for layer in reversed(range(LAYERS)):
        triple, (rows_in, attended, context), late = layer_backward(
            incoming, saved_all[layer], norm_gains[layer], tables, split, dp_count,
            functools.partial(at, layer),
        )
        first_weight = saved_all[layer][-2]
        if layer:
            incoming = []
            for k in range(chunks):
                theirs = input_back_call(
                    2 * k + 1, triple, first_weight, BF16, at(layer, ("input", k))
                )
                mine = input_back_call(2 * k, triple, first_weight, F32)
                incoming.append((attended[2 * k], *finish_pair(mine, theirs)))
            drop(first_weight)
            above["second"] = scatter_finish(where, late)
            sums = weight_call(split, [(rows_in, [triple]), (attended, context)], dp_count)
            drop(*rows_in, *attended[1::2], *context)
            above["first"] = scatter_start(sums)
            if split is None:
                above["first"] = scatter_finish(where, above["first"])

    kept, sent = input_last_call(where, triple, first_weight, attended[::2], at(0, "input"))
    sent = swap_core(sent)
    drop(first_weight, *tables[:2])
    second_sum = scatter_finish(where, late)
    arriving = [second_sum[1:2], [], second_sum[2:]]
    sum_norms(0)
    sums = weight_call(split, [(rows_in, [triple]), (attended, context)], dp_count)
    Order.kept = []
    sums = scatter_start(sums)
    mine, theirs = call(
        side_kernel,
        [sds(count, part // 2, width // 2, dtype=F32), sds(count, part // 2, width // 2)],
        where, kept, sent, scalars=1,
    )
    sum_norms(1)
    total = add_call(mine, swap_x(theirs), BF16, arriving[0])
    if split is None:
        near = lax.all_to_all(total, "dp", split_axis=0, concat_axis=0, tiled=True)
        first_sum = scatter_finish(where, sums)
    else:
        moving = exchange_start(total, where)
        first_sum = scatter_finish(where, sums)
        sum_norms(2)
        moving = exchange_middle(*moving, arriving[1])
        sum_norms(3)
        near = exchange_finish(moving, arriving[2] + first_sum[1:])
    far = swap_x(near)
    for index in range(2 if split is None else 4, len(steps) - 1):
        sum_norms(index)
    norms = own_sums["norms"]
    gains_total, biases_total = call(
        norms_kernel, [sds(LAYERS, 2, width, dtype=F32)] * 2, norms, steps[-1](norms)
    )
    received[1] = [total_call(above["first"]), total_call(above["second"])]
    received[0] = [first_sum, second_sum]
    returned = call(
        functools.partial(last_kernel, split is not None), [sds(count, part, width, dtype=F32)],
        dealing_order, where, near, far, swap_core(near), swap_core(far), scalars=2,
    )[0]

    shapes = (
        jnp.swapaxes(project_weight, 1, 2), gate_up_weight, output_weight,
        jnp.swapaxes(down_weight, 1, 2),
    )
    project_grad, gate_up_grad, output_grad, down_grad = call(
        functools.partial(grads_kernel, tuple(tuple(len(g) for g in r) for r in received)),
        [sds(*w.shape, dtype=F32) for w in shapes],
        *[r for groups in received for group in groups for r in group],
    )
    return (
        layer_outputs[0][None], returned, jnp.swapaxes(project_grad, 1, 2), gate_up_grad, output_grad,
        jnp.swapaxes(down_grad, 1, 2), gains_total, biases_total,
    )


def solution(mesh):
    placed = (
        P(None, "dp", None),
        P(),
        P(),
        P(None, "dp", None, "tensor"),
        P(None, "dp", None, "tensor"),
        P(None, "tensor", "dp"),
        P(None, "tensor", "dp"),
        P(),
        P(),
        P("dp", "tensor", None),
    )
    return jax.shard_map(
        on_device,
        mesh=mesh,
        in_specs=placed,
        out_specs=(
            P("dp", "tensor", None),
            P(None, "dp", None),
            P(None, "dp", None, "tensor"),
            P(None, "dp", None, "tensor"),
            P(None, "tensor", "dp"),
            P(None, "tensor", "dp"),
            P(),
            P(),
        ),
        check_vma=False,
    )
```

```python
import functools
import math

import jax
import jax.numpy as jnp
import numpy as np
from jax import lax
from jax.experimental import pallas as pl
from jax.experimental.pallas import tpu as pltpu
from jax.sharding import PartitionSpec as P

HD = 64
LAYERS = 2
epsilon = 1e-05
rotary_base = 1000.0
LOG2E = math.log2(math.e)
F32 = jnp.float32
BF16 = jnp.bfloat16
VMEM_LIMIT = 12 * 1024 * 1024
COST = 0.001
KEEP = True


def sds(*shape, dtype=BF16):
    return jax.ShapeDtypeStruct(shape, dtype)


class Order:
    last = ()
    waiting = ()
    kept = []


def keep(*arrays):
    Order.kept.extend(arrays)


def drop(*arrays):
    gone = {id(a) for a in arrays}
    Order.kept = [a for a in Order.kept if id(a) not in gone]


def call(kernel, outs, *operands, flops=0, trans=0, scalars=0, after=(), alias=None):
    after = (*after, *Order.waiting, *Order.last)
    Order.waiting = ()
    taken = {id(a) for a in operands}
    held = [a for a in Order.kept if id(a) not in taken] if KEEP else []
    vmem = pl.BlockSpec(memory_space=pltpu.VMEM)
    smem = pl.BlockSpec(memory_space=pltpu.SMEM)
    moved = sum(a.size * a.dtype.itemsize for a in list(operands) + list(outs))
    used = len(operands)

    def body(*refs):
        kernel(*refs[:used], *refs[used + len(held) + len(after) :])

    results = pl.pallas_call(
        body,
        in_specs=[smem] * scalars
        + [vmem] * (used - scalars + len(held))
        + [pl.BlockSpec(memory_space=pl.ANY)] * len(after),
        out_specs=[vmem] * len(outs),
        out_shape=list(outs),
        input_output_aliases=alias or {},
        compiler_params=pltpu.CompilerParams(vmem_limit_bytes=VMEM_LIMIT),
        cost_estimate=pl.CostEstimate(
            flops=int(COST * flops),
            bytes_accessed=int(COST * moved),
            transcendentals=int(COST * trans),
        ),
    )(*operands, *held, *after)
    Order.last = (min(results, key=lambda r: r.size * r.dtype.itemsize),)
    return results


def swap_core(value):
    return lax.ppermute(value, "tensor", [(i, i ^ 1) for i in range(lax.axis_size("tensor"))])


def swap_x(value):
    return lax.ppermute(value, "tensor", [(i, i ^ 2) for i in range(lax.axis_size("tensor"))])


def swap_dp(value, step):
    return lax.ppermute(value, "dp", [(i, i ^ step) for i in range(lax.axis_size("dp"))])


def stepwise(rows):
    return lax.axis_size("dp") == 8 and rows % 16 == 0


def place_kernel(offsets, index_ref, *refs):
    pieces, out_refs = refs[: len(offsets)], refs[len(offsets) :]
    rows = pieces[0].shape[0]
    for offset, piece in zip(offsets, pieces):
        here = pl.ds(pl.multiple_of((index_ref[3] ^ offset) * rows, rows), rows)
        start = 0
        for out_ref in out_refs:
            last = start + out_ref.shape[1]
            out_ref[here, :] = piece[:, start:last]
            start = last


def copy_kernel(in_ref, out_ref):
    out_ref[...] = in_ref[...]


def gather_start(shard):
    if not stepwise(shard.shape[0]):
        return {0: lax.all_gather(shard, "dp", axis=0, tiled=True)}
    pieces = {0: shard, 1: swap_dp(shard, 1)}
    for step in (2, 4, 6):
        pieces[step] = swap_dp(shard, step)
        pieces[step + 1] = swap_dp(pieces[step], 1)
    return pieces


def first_gather(shard, meanwhile):
    if not stepwise(shard.shape[0]):
        for step in meanwhile:
            step()
        return {0: lax.all_gather(shard, "dp", axis=0, tiled=True)}
    pieces = {0: shard, 1: swap_dp(shard, 1), 2: swap_dp(shard, 2), 4: swap_dp(shard, 4)}
    after = [pieces[1], pieces[2], pieces[4]]
    for step in meanwhile:
        step()
    sent = call(copy_kernel, [sds(*shard.shape)], shard, after=after)[0]
    pieces[6] = swap_dp(sent, 6)
    for step in (2, 4, 6):
        pieces[step + 1] = swap_dp(pieces[step], 1)
    return pieces


def gather_finish(where, pieces, widths, after=()):
    if len(pieces) == 1:
        whole, parts = pieces[0], []
        for width in widths:
            parts.append(whole[:, :width])
            whole = whole[:, width:]
        return parts
    rows = pieces[0].shape[0]
    return call(
        functools.partial(place_kernel, tuple(pieces)),
        [sds(8 * rows, width) for width in widths],
        where, *pieces.values(), scalars=1, after=after,
    )


def scatter_add_kernel(index_ref, kept_ref, *refs):
    steps = kept_ref.shape[0]
    other_refs, out_refs = refs[:-steps], refs[-steps:]
    own = index_ref[3] // 2
    for step, out_ref in enumerate(out_refs):
        start = 0
        for other_ref in other_refs:
            here = pl.ds(start, other_ref.shape[2])
            total = kept_ref[own ^ step, :, here].astype(F32) + other_ref[own ^ step].astype(F32)
            out_ref[:, here] = total.astype(BF16)
            start += other_ref.shape[2]


def scatter_start(sums):
    if isinstance(sums, (list, tuple)):
        return [sums[0]] + [swap_dp(part, 1) for part in sums[1:]]
    return [lax.psum_scatter(sums, "dp", scatter_dimension=0, tiled=True)]


def scatter_finish(where, started):
    if len(started) == 1:
        return started
    kept, *others = started
    count, rows, width = kept.shape
    outs = call(scatter_add_kernel, [sds(rows, width)] * count, where, kept, *others, scalars=1)
    return [outs[0]] + [swap_dp(out, 2 * step) for step, out in enumerate(outs) if step]


def total_kernel(*refs):
    *in_refs, out_ref = refs
    out_ref[...] = total_of(in_refs)


def total_call(parts):
    rows, width = parts[0].shape[-2:]
    return [call(total_kernel, [sds(rows, width, dtype=F32)], *parts)[0]]


def dot_nt(left, right):
    return lax.dot_general(left, right, (((1,), (1,)), ((), ())), preferred_element_type=F32)


def dot_nn(left, right):
    return lax.dot_general(left, right, (((1,), (0,)), ((), ())), preferred_element_type=F32)


def dot_tn(left, right):
    return lax.dot_general(left, right, (((0,), (0,)), ((), ())), preferred_element_type=F32)


def swap_halves(values):
    width = values.shape[-1]
    lane = lax.broadcasted_iota(jnp.int32, values.shape, 1)
    return jnp.where(
        lane % HD < HD // 2,
        pltpu.roll(values, width - HD // 2, 1),
        pltpu.roll(values, HD // 2, 1),
    )


def widen(table, width):
    return jnp.concatenate([table] * (width // table.shape[1]), axis=1)


def qkv_kernel(*refs):
    *x_refs, w_ref, cos_ref, sin_ref, bias_ref, q_ref, k_ref, v_ref, kt_ref, vt_ref = refs
    inner = v_ref.shape[1]
    extra = q_ref.shape[1] - inner
    weight = w_ref[:, : 3 * inner]
    block = 256
    parts = [
        x_ref.at[pl.ds(start, block), :]
        for x_ref in x_refs
        for start in range(0, x_ref.shape[0], block)
    ]
    for step, x_ref in enumerate(parts):
        here = pl.ds(step * block, block)
        projected = dot_nn(x_ref[...], weight)
        pair = projected[:, : 2 * inner]
        turned = pair * widen(cos_ref[here, :], 2 * inner) + swap_halves(pair) * widen(
            sin_ref[here, :], 2 * inner
        )
        lane = lax.broadcasted_iota(jnp.int32, (block, extra), 1)
        queries = turned[:, :inner] * (1.0 / math.sqrt(HD))
        keys = turned[:, inner:]
        values = projected[:, 2 * inner :]
        one = jnp.where(lane == 0, 1.0, 0.0)
        mark = jnp.where(lane == 0, bias_ref[here, :extra], 0.0)
        q_ref[here, :] = jnp.concatenate([queries, one], axis=1).astype(BF16)
        k_ref[here, :] = jnp.concatenate([keys, mark], axis=1).astype(BF16)
        v_ref[here, :] = values.astype(BF16)
        kt_ref[:, here] = keys.T.astype(BF16)
        vt_ref[:, here] = values.T.astype(BF16)


def qkv_call(pieces, weight, tables, inner, after):
    rows = sum(p.shape[0] for p in pieces)
    width = weight.shape[0]
    return call(
        qkv_kernel,
        [sds(rows, inner + HD), sds(rows, inner + HD), sds(rows, inner)] + [sds(inner, rows)] * 2,
        *pieces, weight, *tables,
        flops=2 * rows * width * 3 * inner,
        after=after,
    )


def head_mask(shape, head, inner):
    lane = lax.broadcasted_iota(jnp.int32, shape, 1)
    return ((lane >= head * HD) & (lane < (head + 1) * HD)) | (lane >= inner)


def attend_kernel(part, q_ref, k_ref, vt_ref, w_ref, c_ref, lse_ref, out_ref):
    rows, inner = c_ref.shape
    queries = q_ref[pl.ds(part * rows, rows), :]
    columns, stats = [], []
    for head in range(inner // HD):
        masked = jnp.where(head_mask(queries.shape, head, inner), queries, 0)
        scores = dot_nt(k_ref[...], masked)
        shift = jnp.max(scores, axis=0, keepdims=True) * LOG2E
        exps = jnp.exp2(scores * LOG2E - shift)
        total = jnp.sum(exps, axis=0, keepdims=True)
        mixed = dot_nn(vt_ref[head * HD : (head + 1) * HD, :], exps.astype(BF16))
        columns.append(mixed * (1.0 / total))
        stats.append(shift + jnp.log2(total))
    context = jnp.concatenate(columns, axis=0).T.astype(BF16)
    c_ref[...] = context
    pad = lse_ref.shape[0] - len(stats)
    lse_ref[...] = jnp.concatenate(stats + [jnp.zeros((pad, rows), F32)], axis=0)
    out_ref[...] = dot_nt(context, w_ref[:, 3 * inner :]).astype(out_ref.dtype)


def attend_call(part, queries, keys, values_t, weight, dtype, after=()):
    length, padded = queries.shape
    rows, inner, width = length // 4, padded - HD, weight.shape[0]
    return call(
        functools.partial(attend_kernel, part),
        [sds(rows, inner), sds(8, rows, dtype=F32), sds(rows, width, dtype=dtype)],
        queries, keys, values_t, weight,
        flops=4 * rows * length * 256 * (inner // HD) + 2 * rows * inner * width,
        trans=rows * length * (inner // HD),
        after=after,
    )


def norm_kernel(base_ref, pair_ref, other_ref, gain_ref, shift_ref, low_ref, normal_ref, scale_ref, *out):
    values = base_ref[...].astype(F32) + (pair_ref[...] + other_ref[...].astype(F32))
    centred = values - jnp.mean(values, axis=-1, keepdims=True)
    scaled = lax.rsqrt(jnp.mean(centred * centred, axis=-1, keepdims=True) + epsilon)
    normal = centred * scaled
    result = normal * gain_ref[...] + shift_ref[...]
    low_ref[...] = result.astype(BF16)
    normal_ref[...] = normal.astype(BF16)
    scale_ref[...] = jnp.broadcast_to(scaled, scale_ref.shape)
    for ref in out:
        ref[...] = result


def norm_call(base, pair, other, gain, shift, last, after=()):
    rows, width = pair.shape
    return call(
        norm_kernel,
        [sds(rows, width), sds(rows, width), sds(rows, 128, dtype=F32)]
        + [sds(rows, width, dtype=F32)] * last,
        base, pair, other, gain, shift,
        flops=10 * rows * width,
        after=after,
    )


def norm_back_kernel(*refs):
    *in_refs, normal_ref, scale_ref, gain_ref, low_ref, vec_ref = refs
    incoming = in_refs[0][...].astype(F32)
    for ref in in_refs[1:]:
        incoming = incoming + ref[...].astype(F32)
    normal = normal_ref[...].astype(F32)
    weighted = incoming * gain_ref[...]
    result = scale_ref[:, 0:1] * (
        weighted
        - jnp.mean(weighted, axis=-1, keepdims=True)
        - normal * jnp.mean(weighted * normal, axis=-1, keepdims=True)
    )
    low_ref[...] = result.astype(BF16)
    vec_ref[0:1, :] = jnp.sum(incoming * normal, axis=0, keepdims=True)
    vec_ref[1:2, :] = jnp.sum(incoming, axis=0, keepdims=True)


def norm_back_call(incoming, normal, scale, gain, after=()):
    rows, width = normal.shape
    return call(
        norm_back_kernel,
        [sds(rows, width), sds(2, width, dtype=F32)],
        *incoming, normal, scale, gain,
        flops=16 * rows * width,
        after=after,
    )


def mask_of(where_ref, chunk, rows):
    place = lax.broadcasted_iota(jnp.int32, (rows, 128), 0)
    usable = (2 * chunk + where_ref[0]) * rows + place < where_ref[4]
    return jnp.where(usable, 1.0, 0.0)[:, 0:1]


def seed_kernel(chunk, where_ref, own_ref, other_ref, out_ref):
    seed = jnp.where(where_ref[1] == chunk, own_ref[...].astype(F32), other_ref[...].astype(F32))
    out_ref[...] = (seed * mask_of(where_ref, chunk, out_ref.shape[0])).astype(BF16)


def show_kernel(where_ref, first_ref, second_ref, out_ref):
    rows = out_ref.shape[0]
    first = first_ref[...] * mask_of(where_ref, 0, rows)
    second = second_ref[...] * mask_of(where_ref, 1, rows)
    out_ref[...] = jnp.where(where_ref[1] == 0, first, second)


def gather_vectors_kernel(*refs):
    *in_refs, out_ref = refs
    for row in range(out_ref.shape[0] // 2):
        pair = in_refs[2 * row][...] + in_refs[2 * row + 1][...]
        out_ref[2 * row : 2 * row + 2, :] = pair * 0.5


def norms_kernel(left_ref, right_ref, gains_ref, biases_ref):
    for row in range(left_ref.shape[0] // 2):
        for member, out_ref in enumerate((gains_ref, biases_ref)):
            here = pl.ds(2 * row + member, 1)
            out_ref[row // 2, pl.ds(row % 2, 1), :] = left_ref[here, :] + right_ref[here, :]


def add_kernel(left_ref, right_ref, out_ref):
    total = left_ref[...].astype(F32) + right_ref[...].astype(F32)
    out_ref[...] = total.astype(out_ref.dtype)


def add_call(left, right, dtype, after=()):
    return call(add_kernel, [sds(*left.shape, dtype=dtype)], left, right, after=after)[0]


def mlp_parts(w_ref):
    hidden = w_ref.shape[1] // 3
    return [w_ref[:, part * hidden : (part + 1) * hidden] for part in range(3)]


def mlp_kernel(x_ref, w_ref, out_ref):
    gate_weight, up_weight, down_weight = mlp_parts(w_ref)
    rows = x_ref[...]
    gate = dot_nn(rows, gate_weight)
    up = dot_nn(rows, up_weight)
    active = (gate * jax.nn.sigmoid(gate) * up).astype(BF16)
    out_ref[...] = dot_nt(active, down_weight).astype(out_ref.dtype)


def mlp_call(piece, weight, dtype):
    rows, width = piece.shape
    return call(
        mlp_kernel, [sds(rows, width, dtype=dtype)], piece, weight,
        flops=2 * rows * width * weight.shape[1],
        trans=rows * weight.shape[1] // 3,
    )[0]


def mlp_back_kernel(x_ref, grad_ref, w_ref, act_ref, dg_ref, out_ref):
    gate_weight, up_weight, down_weight = mlp_parts(w_ref)
    hidden = act_ref.shape[1]
    rows = x_ref[...]
    gate = dot_nn(rows, gate_weight)
    up = dot_nn(rows, up_weight)
    active_grad = dot_nn(grad_ref[...], down_weight)
    sigmoid = jax.nn.sigmoid(gate)
    silu = gate * sigmoid
    act_ref[...] = (silu * up).astype(BF16)
    gate_grad = (active_grad * up * sigmoid * (1.0 + gate * (1.0 - sigmoid))).astype(BF16)
    up_grad = (active_grad * silu).astype(BF16)
    dg_ref[:, :hidden] = gate_grad
    dg_ref[:, hidden:] = up_grad
    partial = dot_nt(gate_grad, gate_weight) + dot_nt(up_grad, up_weight)
    out_ref[...] = partial.astype(out_ref.dtype)


def mlp_back_call(piece, grad, weight, dtype):
    rows, width = piece.shape
    hidden = weight.shape[1] // 3
    return call(
        mlp_back_kernel,
        [sds(rows, hidden), sds(rows, 2 * hidden), sds(rows, width, dtype=dtype)],
        piece, grad, weight,
        flops=10 * rows * width * hidden,
        trans=rows * hidden,
    )


def context_back_kernel(mine_in, theirs_in, w_ref, dc_ref):
    inner = dc_ref.shape[1]
    half = mine_in.shape[0]
    weight = w_ref[:, 3 * inner :]
    dc_ref[:half, :] = dot_nn(mine_in[...], weight).astype(BF16)
    dc_ref[half:, :] = dot_nn(theirs_in[...], weight).astype(BF16)


def context_back_call(mine, theirs, weight):
    half, width = mine.shape
    inner = weight.shape[1] // 4
    return call(
        context_back_kernel, [sds(2 * half, inner)], mine, theirs, weight,
        flops=4 * half * width * inner,
    )[0]


def attend_back_kernel(
    first, last, q_ref, dc_ref, lse_ref, k_ref, v_ref, kt_ref, cos_ref, sin_ref, *refs
):
    if first:
        dk_in, dv_in, *refs = refs
    if last and first:
        dq_in, *refs = refs
    dq_ref, dk_ref, dv_ref = refs
    rows, inner = dc_ref.shape
    length, padded = k_ref.shape
    block = min(256, rows)

    def turn_back(gradient, cosine, sine):
        cosine = widen(cosine, gradient.shape[1])
        sine = widen(sine, gradient.shape[1])
        return (gradient * cosine - swap_halves(gradient) * sine)[:, :inner]

    if first:
        dk_ref[...] = dk_in[...]
        dv_ref[...] = dv_in[...]
    else:
        dk_ref[...] = jnp.zeros_like(dk_ref)
        dv_ref[...] = jnp.zeros_like(dv_ref)

    def step_of(step, carry):
        start = pl.multiple_of(step * block, block)
        here = pl.ds(start, block)
        there = pl.ds(pl.multiple_of(first + step * block, block), block)
        queries = q_ref[there, :]
        context_grad = dc_ref[here, :]
        columns = []
        for head in range(inner // HD):
            masked = jnp.where(head_mask(queries.shape, head, inner), queries, 0)
            masked_grad = jnp.where(head_mask(context_grad.shape, head, inner), context_grad, 0)
            scores = dot_nt(k_ref[...], masked)
            weights = jnp.exp2(scores * LOG2E - lse_ref[head : head + 1, there])
            weight_grad = dot_nt(v_ref[...], masked_grad)
            inner_sum = jnp.sum(weights * weight_grad, axis=0, keepdims=True)
            score_grad = (weights * (weight_grad - inner_sum)).astype(BF16)
            dk_ref[...] += dot_nn(score_grad, masked)
            dv_ref[...] += dot_nn(weights.astype(BF16), masked_grad)
            columns.append(dot_nn(kt_ref[head * HD : (head + 1) * HD, :], score_grad))
        columns.append(jnp.zeros((padded - inner, block), F32))
        query_grad = jnp.concatenate(columns, axis=0).T * (1.0 / math.sqrt(HD))
        turned = turn_back(query_grad, cos_ref[there, :], sin_ref[there, :]).astype(BF16)
        dq_ref[there if last else here, :inner] = turned
        return carry

    lax.fori_loop(0, rows // block, step_of, 0)
    if last:
        if first:
            dq_ref[:first, :inner] = dq_in[...]
        dq_ref[:, inner : 2 * inner] = turn_back(dk_ref[...], cos_ref[...], sin_ref[...]).astype(
            BF16
        )
        dq_ref[:, 2 * inner :] = dv_ref[...].astype(BF16)


def attend_back_call(first, last, operands, carried, after):
    length, padded = operands[0].shape
    rows, inner = operands[1].shape
    out = sds(length, 3 * inner) if last else sds(rows, inner)
    return call(
        functools.partial(attend_back_kernel, first, last),
        [out, sds(length, padded, dtype=F32), sds(length, inner, dtype=F32)],
        *operands, *carried,
        flops=10 * rows * length * 256 * (inner // HD),
        trans=rows * length * (inner // HD),
        after=after,
    )


def input_back_kernel(part, dp_ref, w_ref, out_ref):
    rows = out_ref.shape[0]
    here = pl.ds(part * rows, rows)
    out_ref[...] = dot_nt(dp_ref[here, :], w_ref[:, : dp_ref.shape[1]]).astype(out_ref.dtype)


def input_back_call(part, triple, weight, dtype, after=()):
    rows, width = triple.shape[0] // 4, weight.shape[0]
    return call(
        functools.partial(input_back_kernel, part),
        [sds(rows, width, dtype=dtype)],
        triple, weight,
        flops=2 * rows * triple.shape[1] * width,
        after=after,
    )[0]


def input_last_kernel(index_ref, dp_ref, w_ref, *refs):
    *grad_refs, kept_ref, sent_ref = refs
    core, side = index_ref[0], index_ref[1]
    rows, total = dp_ref.shape
    quarter = rows // 4
    split = kept_ref.shape[1]
    weight = w_ref[:, :total]
    for step in range(4):
        chunk, part = step // 2, step % 2
        partial = dot_nt(dp_ref[pl.ds(step * quarter, quarter), :], weight)
        if not part:
            partial = partial + jnp.where(side == chunk, grad_refs[chunk][...].astype(F32), 0.0)
        start = pl.multiple_of((2 * chunk + (core ^ part)) * quarter, quarter)
        low, high = partial[:, :split], partial[:, split:]
        kept_ref[pl.ds(start, quarter), :] = jnp.where(core == 0, low, high)
        sent_ref[pl.ds(start, quarter), :] = jnp.where(core == 0, high, low).astype(BF16)


def input_last_call(index, triple, weight, grads, after):
    rows, width = triple.shape[0], weight.shape[0]
    return call(
        input_last_kernel,
        [sds(rows, width // 2, dtype=F32), sds(rows, width // 2)],
        index, triple, weight, *grads,
        flops=2 * rows * triple.shape[1] * width, scalars=1, after=after,
    )


def side_kernel(index_ref, kept_ref, other_ref, mine_ref, theirs_ref):
    side = index_ref[1]
    count, half, _ = mine_ref.shape
    for block in range(count):
        halves = []
        for part in range(2):
            here = pl.ds((2 * block + part) * half, half)
            halves.append(kept_ref[here, :] + other_ref[here, :].astype(F32))
        mine_ref[block] = jnp.where(side == 0, halves[0], halves[1])
        theirs_ref[block] = jnp.where(side == 0, halves[1], halves[0]).astype(BF16)


SHARE = 768


def weight_kernel(counts, index_ref, *refs):
    in_count = sum(left + right for left, right in counts)
    in_refs, (kept_ref, *sent_refs) = refs[:in_count], refs[in_count:]
    blocks, rows, _ = kept_ref.shape
    width = blocks * rows * (2 if sent_refs else 1)
    wide = 4 * rows if width % (4 * rows) == 0 and (4 * rows) % 128 == 0 else width
    column = 0
    lefts, rights = [], []
    for left_count, right_count in counts:
        lefts.append(in_refs[:left_count])
        rights.append(in_refs[left_count : left_count + right_count])
        in_refs = in_refs[left_count + right_count :]
    for left, right in zip(lefts, rights):
        columns = right[0].shape[1]
        share = min(columns, SHARE)
        ratio = len(left) // len(right)
        for start in range(0, columns, share):
            for first in range(0, width, wide):
                total = None
                for number, left_ref in enumerate(left):
                    size = left_ref.shape[0]
                    right_ref = right[number // ratio]
                    term = dot_tn(
                        left_ref[:, first : first + wide],
                        right_ref[
                            pl.ds((number % ratio) * size, size), start : start + share
                        ],
                    )
                    total = term if total is None else total + term
                where = pl.ds(column + start, share)
                there = pl.ds((column + start) % SHARE, share)
                for offset in range(0, wide, 2 * rows):
                    even = total[offset : offset + rows].astype(BF16)
                    odd = total[offset + rows : offset + 2 * rows].astype(BF16)
                    block = (first + offset) // (2 * rows)
                    if not sent_refs:
                        kept_ref[2 * block, :, where] = even
                        kept_ref[2 * block + 1, :, where] = odd
                    else:
                        sent_ref = sent_refs[(column + start) // SHARE]
                        kept_ref[block, :, where] = jnp.where(index_ref[5] == 0, even, odd)
                        sent_ref[block, :, there] = jnp.where(index_ref[5] == 0, odd, even)
        column += columns


def weight_call(parity, pairs, count, after=()):
    width = pairs[0][0][0].shape[1]
    total = sum(right[0].shape[1] for _, right in pairs)
    rows = sum(piece.shape[0] for piece in pairs[0][0])
    operands = [piece for left, right in pairs for piece in (*left, *right)]
    counts = tuple((len(left), len(right)) for left, right in pairs)
    flops = 2 * rows * width * total
    if parity is None:
        return call(
            functools.partial(weight_kernel, counts, None),
            [sds(count, width // count, total)],
            *operands, flops=flops, after=after,
        )[0]
    shape = (count // 2, width // count)
    return call(
        functools.partial(weight_kernel, counts),
        [sds(*shape, total)] + [sds(*shape, SHARE)] * (total // SHARE),
        parity, *operands, flops=flops, scalars=1, after=after,
    )


def total_of(refs):
    parts = [
        part
        for ref in refs
        for part in ([ref[i] for i in range(ref.shape[0])] if len(ref.shape) == 3 else [ref[...]])
    ]
    total = parts[0].astype(F32)
    for part in parts[1:]:
        total = total + part.astype(F32)
    return total


def grads_kernel(counts, *refs):
    out_refs = refs[-4:]
    position = 0
    for layer, groups in enumerate(counts):
        parts = []
        for count in groups:
            parts.append(total_of(refs[position : position + count]))
            position += count
        whole = jnp.concatenate(parts, axis=1)
        project_ref, gate_up_ref, output_ref, down_ref = out_refs
        inner, hidden = output_ref.shape[1], down_ref.shape[2]
        for part in range(3):
            project_ref[layer, part] = whole[:, part * inner : (part + 1) * inner]
        output_ref[layer] = whole[:, 3 * inner : 4 * inner].T
        for part in range(2):
            start = 4 * inner + part * hidden
            gate_up_ref[layer, :, part, :] = whole[:, start : start + hidden]
        down_ref[layer] = whole[:, 4 * inner + 2 * hidden :]


def last_kernel(
    turned, order_ref, where_ref, near_ref, far_ref, near_other_ref, far_other_ref, out_ref
):
    core, side = where_ref[0], where_ref[1]
    count, half, split = near_ref.shape
    for source in range(count):
        target = order_ref[where_ref[3] ^ source if turned else source]
        for ref, flip in ((near_ref, 0), (far_ref, 1)):
            here = pl.ds(pl.multiple_of((side ^ flip) * half, half), half)
            other = near_other_ref if ref is near_ref else far_other_ref
            own, swapped = ref[source].astype(F32), other[source].astype(F32)
            out_ref[target, here, :split] = jnp.where(core == 0, own, swapped)
            out_ref[target, here, split:] = jnp.where(core == 0, swapped, own)


def pair_kernel(mine_ref, other_ref, pair_ref, low_ref):
    pair = mine_ref[...] + other_ref[...].astype(F32)
    pair_ref[...] = pair
    low_ref[...] = pair.astype(BF16)


def finish_pair(mine, theirs, after=()):
    other = swap_core(theirs)
    outs = [sds(*mine.shape, dtype=F32), sds(*mine.shape)]
    pair, low = call(pair_kernel, outs, mine, other, after=after)
    return pair, swap_x(low)


def layer_forward(
    pieces, residual, first_weight, second_weight, gains, shifts, tables, inner, last, at
):
    chunks = len(residual)
    queries, keys, values, keys_t, values_t = qkv_call(
        pieces, first_weight, tables, inner, ()
    )
    keep(*pieces, queries, keys, values, keys_t, values_t, first_weight)
    context, logsum, first_norm, hidden_pieces, pairs = [], [], [], [], []
    for k in range(chunks):
        args = (queries, keys, values_t, first_weight)
        theirs = attend_call(2 * k + 1, *args, BF16)
        keep(theirs[0])
        mine = attend_call(2 * k, *args, F32)
        keep(mine[0])
        context += [mine[0], theirs[0]]
        logsum += [mine[1], theirs[1]]
        pairs.append(finish_pair(mine[2], theirs[2], ()))
    drop(values_t)
    logsum = jnp.concatenate(logsum, axis=1)
    keep(logsum)
    second_norm, result, result_pieces, second_pairs = [], [], [], []
    mine, theirs = [], []
    for k in range(chunks):
        low, *kept = norm_call(
            residual[k], *pairs[k], gains[0:1], shifts[0:1], False, at(("norm_one", k))
        )
        first_norm.append(kept)
        hidden_pieces += [low, swap_core(low)]
        keep(*kept)
        if k == 0:
            second_weight = second_weight()
        mine.append(mlp_call(low, second_weight, F32))
        keep(low, second_weight)
    for k in range(chunks):
        theirs.append(mlp_call(hidden_pieces[2 * k + 1], second_weight, BF16))
        keep(hidden_pieces[2 * k + 1])
    for k in range(chunks):
        second_pairs.append(finish_pair(mine[k], theirs[k]))
    for k in range(chunks):
        low, *kept = norm_call(
            hidden_pieces[2 * k], *second_pairs[k], gains[1:2], shifts[1:2], last,
            at(("norm_two", k)),
        )
        keep(*kept[:2])
        second_norm.append(kept[:2])
        result += kept[2:]
        result_pieces.append(low)
    saved = (
        pieces, queries, keys, values, keys_t, context, logsum,
        first_norm, hidden_pieces, second_norm, first_weight, second_weight,
    )
    return result, result_pieces, saved


def layer_backward(incoming, saved, gains, tables, parity, count, at):
    (
        pieces, queries, keys, values, keys_t, context, logsum,
        first_norm, hidden_pieces, second_norm, first_weight, second_weight,
    ) = saved
    chunks = len(incoming)
    mixed, active, vectors_two, pair_grads, pairs = [], [], [], [], []
    outs = []
    for k in range(chunks):
        low, vector = norm_back_call(
            incoming[k], *second_norm[k], gains[1:2], at(("norm_two", k))
        )
        drop(*second_norm[k])
        vectors_two.append(vector)
        mixed += [low, swap_core(low)]
        outs += mlp_back_call(hidden_pieces[2 * k], low, second_weight, F32)
        keep(*outs[-3:-1], low)
    for k in range(chunks):
        outs += mlp_back_call(hidden_pieces[2 * k + 1], mixed[2 * k + 1], second_weight, BF16)
        keep(*outs[-3:-1], mixed[2 * k + 1])
    for k in range(chunks):
        here, there = outs[3 * k : 3 * k + 3], outs[3 * (chunks + k) : 3 * (chunks + k) + 3]
        active += [here[0], there[0]]
        pair_grads += [here[1], there[1]]
        pairs.append(finish_pair(here[2], there[2]))
    drop(second_weight)
    at("sums")
    late = scatter_start(
        weight_call(parity, [(hidden_pieces, pair_grads), (mixed, active)], count)
    )
    at(late)
    drop(*hidden_pieces, *pair_grads, *active, *mixed[1::2])
    attended, vectors_one, carried = [], [], ()
    for k in range(chunks):
        low, vector = norm_back_call(
            (mixed[2 * k], *pairs[k]), *first_norm[k], gains[0:1], at(("norm_one", k))
        )
        drop(*first_norm[k], mixed[2 * k])
        vectors_one.append(vector)
        if k == chunks - 1:
            at(("vectors", vectors_one + vectors_two))
        attended += [low, swap_core(low)]
        context_grad = context_back_call(*attended[2 * k :], first_weight)
        keep(*attended[2 * k :])
        operands = (queries, context_grad, logsum, keys, values, keys_t, *tables[:2])
        out, dk, dv = attend_back_call(
            k * context_grad.shape[0], k == chunks - 1, operands, carried, at(("attend_back", k))
        )
        carried = (dk, dv, out)
        at(("attend", k))
    drop(queries, logsum, keys, values, keys_t)
    return out, (pieces, attended, context), late


def rotary_tables(length):
    half = HD // 2
    angles = np.arange(length, dtype=np.float64)[:, None] * np.exp(
        np.arange(half, dtype=np.float64)[None, :] * (-2.0 * math.log(rotary_base) / HD)
    )
    cosine, sine = np.cos(angles), np.sin(angles)
    return (
        np.concatenate([cosine] * 4, axis=1).astype(np.float32),
        np.concatenate([-sine, sine] * 2, axis=1).astype(np.float32),
    )


def turn_kernel(where_ref, in_ref, *out_refs):
    index = where_ref[3]
    for step in range(4):
        for flip in range(2):
            out_refs[flip][step] = in_ref[index ^ (2 * step + flip)]


def couple_kernel(own_ref, other_ref, *out_refs):
    for step, out_ref in enumerate(out_refs):
        out_ref[0] = own_ref[step]
        out_ref[1] = other_ref[step]


def join_kernel(*refs):
    *in_refs, out_ref = refs
    for step, ref in enumerate(in_refs):
        out_ref[2 * step : 2 * step + 2] = ref[...]


def exchange_start(blocks, where):
    _, rows, width = blocks.shape
    own, sent = call(turn_kernel, [sds(4, rows, width)] * 2, where, blocks, scalars=1)
    return own, swap_dp(sent, 1)


def exchange_middle(own, sent, after=()):
    _, rows, width = own.shape
    pairs = call(couple_kernel, [sds(2, rows, width)] * 4, own, sent, after=after)
    return [pairs[0]] + [swap_dp(pairs[step], 2 * step) for step in (1, 2, 3)]


def exchange_finish(moved, after=()):
    _, rows, width = moved[0].shape
    return call(join_kernel, [sds(8, rows, width)], *moved, after=after)[0]


def deal_kernel(where_ref, *refs):
    *in_refs, out_ref = refs
    core, own, index = where_ref[0], where_ref[2], where_ref[3]
    count, share, _ = in_refs[0].shape
    part = out_ref.shape[0] // count
    for step in range(count):
        source = index ^ step
        quarter = source // 2
        block = 2 * ((quarter // 2) * 2 + ((quarter % 2) ^ core)) + source % 2
        for offset, ref in enumerate(in_refs):
            start = pl.multiple_of(block * part + (own ^ offset) * share, share)
            out_ref[pl.ds(start, share), :] = ref[step]


def deal_steps(tokens, dealing_order, where):
    count, part, width = tokens.shape
    share = part // 4
    mine = lax.dynamic_slice_in_dim(tokens, where[2] * share, share, 1)
    picked = jnp.take(mine, dealing_order, axis=0)
    state = []

    def spread(arrived):
        far = swap_x(arrived)
        state[:] = [arrived, swap_core(arrived), far, swap_core(far)]

    if count != 8 or share % 16:
        spread(lax.all_to_all(picked, "dp", split_axis=0, concat_axis=0, tiled=True))
        return [], state
    state[:] = exchange_start(picked, where)

    def middle():
        state[:] = exchange_middle(*state)

    def finish():
        spread(exchange_finish(state))

    return [middle, finish], state


def deal_finish(pieces, where, local_order):
    count, share, width = pieces[0].shape
    length = 4 * count * share
    if count == 8 and share % 16 == 0:
        return call(deal_kernel, [sds(length, width)], where, *pieces, scalars=1)[0]
    stacked = jnp.stack(pieces)
    blocks = [
        lax.dynamic_index_in_dim(stacked, where[2] ^ slot, 0, keepdims=False) for slot in range(4)
    ]
    whole = jnp.stack(blocks, axis=1).reshape(length, width)
    return local_order(whole).reshape(length, width)


def pack_kernel(project_ref, gate_up_ref, output_ref, down_ref, *out_refs):
    inner, hidden = output_ref.shape[1], down_ref.shape[2]
    columns = [project_ref[0, part] for part in range(3)] + [output_ref[0].T]
    columns += [gate_up_ref[0, :, part] for part in range(2)] + [down_ref[0]]
    for out_ref in out_refs:
        start = 0
        while start < out_ref.shape[1]:
            column = columns.pop(0)
            out_ref[:, start : start + column.shape[1]] = column.astype(BF16)
            start += column.shape[1]


def pack_call(layer, together, project, gate_up, output, down, after=()):
    operands = (jnp.swapaxes(project, 1, 2), gate_up, output, jnp.swapaxes(down, 1, 2))
    rows, inner, hidden = project.shape[1], output.shape[1], down.shape[1]
    sizes = [4 * inner, 3 * hidden]
    outs = [sds(rows, n) for n in ([sum(sizes)] if together else sizes)]
    after = (*after, *Order.last)

    def spec(w):
        return pl.BlockSpec((1, *w.shape[1:]), lambda i: (layer,) + (0,) * (w.ndim - 1))

    def body(*refs):
        pack_kernel(*refs[:4], *refs[4 + len(after) :])

    results = pl.pallas_call(
        body,
        grid=(1,),
        in_specs=[spec(w) for w in operands] + [pl.BlockSpec(memory_space=pl.ANY)] * len(after),
        out_specs=[pl.BlockSpec(out.shape, lambda i: (0, 0)) for out in outs],
        out_shape=outs,
        compiler_params=pltpu.CompilerParams(vmem_limit_bytes=VMEM_LIMIT),
        cost_estimate=pl.CostEstimate(flops=0, bytes_accessed=1000, transcendentals=0),
    )(*operands, *after)
    Order.last = (results[0],)
    return results


def on_device(
    tokens, dealing_order, lengths, project_weight, gate_up_weight, output_weight, down_weight,
    norm_gains, norm_biases, cotangent,
):
    Order.last, Order.waiting, Order.kept = (), (), []
    dp_index = lax.axis_index("dp")
    tensor_index = lax.axis_index("tensor")
    core, side = tensor_index % 2, tensor_index // 2
    count, part, width = tokens.shape
    dp_count = lax.axis_size("dp")
    length = 4 * cotangent.shape[1]
    quarter = length // 4
    chunks = 2
    inner = output_weight.shape[1]
    hidden = down_weight.shape[1]
    rows_here = project_weight.shape[1]

    sources = (project_weight, gate_up_weight, output_weight, down_weight)
    length_now = jnp.take(lengths, jnp.take(dealing_order, dp_index))
    where = jnp.stack([core, side, tensor_index, dp_index, length_now, dp_index % 2]).astype(jnp.int32)
    own = cotangent[0]
    other = swap_x(own)

    def local_order(rows):
        split = rows.reshape(chunks, 2, quarter, rows.shape[-1])
        return jnp.where(core == 0, split, split[:, ::-1])

    places = jnp.arange(length)[:, None]
    marks = jnp.where(places < length_now, 0.0, -1e30).astype(F32)
    tables = tuple(
        local_order(table).reshape(length, 128)
        for table in (*map(jnp.asarray, rotary_tables(length)), jnp.broadcast_to(marks, (length, 128)))
    )
    shard = pack_call(0, True, *sources)[0]
    meanwhile, moving = deal_steps(tokens, dealing_order, where)
    pieces = first_gather(shard, meanwhile)
    widths = (4 * inner, 3 * hidden)
    coming = [(pieces, None)]
    saved_all = []
    keep(*tables[:2])
    for layer in range(LAYERS):
        here, points = coming[layer], {}
        if layer < LAYERS - 1:
            before = [pieces[step] for step in (6, 3, 5)] if layer == 0 and len(pieces) > 1 else ()
            packed = pack_call(layer + 1, False, *sources, after=before)
            first, second = (gather_start(part) for part in packed)
            coming.append((first, second))
            if len(first) > 1:
                points = {
                    "place": (first, (2, 4)),
                    ("norm_one", 0): (first, (6, 1, 3, 5)),
                    ("norm_one", 1): (second, (2, 4, 1)),
                    ("norm_two", 0): (second, (3,)),
                    ("norm_two", 1): (second, (6, 5)),
                }
        if layer and len(here[0]) > 1:
            points[("norm_one", 0)] = (here[1], (7,))

        def at(point, points=points, layer=layer):
            if layer == 0 and point == ("norm_one", 0):
                for k in range(chunks):
                    incoming.append(
                        call(
                            functools.partial(seed_kernel, k), [sds(quarter, width)],
                            where, own, other, scalars=1,
                        )
                    )
                    keep(*incoming[-1])
            found, steps = points.get(point, ({}, ()))
            return tuple(found[step] for step in steps)

        if layer == 0:
            incoming = []
            first_weight, second_weight = gather_finish(where, here[0], widths, at("place"))
            dealt = deal_finish(moving, where, local_order)
            pieces = [dealt]
            residual = [dealt[2 * k * quarter : (2 * k + 1) * quarter] for k in range(chunks)]
            late_weight = lambda: second_weight
        else:
            (first_weight,) = gather_finish(where, here[0], widths[:1])
            late_weight = lambda here=here: gather_finish(where, here[1], widths[1:])[0]
        current, residual, saved = layer_forward(
            pieces, residual, first_weight, late_weight, norm_gains[layer], norm_biases[layer],
            tables, inner, layer == LAYERS - 1, at,
        )
        saved_all.append(saved)
        if layer < LAYERS - 1:
            pieces = [p for piece in residual for p in (piece, swap_core(piece))]
    keep(*current)
    shown = []
    received, vectors, steps = [None] * LAYERS, [None] * LAYERS, []
    for step in (1, 2):
        steps.append(lambda v, s=step: lax.ppermute(v, "tensor", [(i, i ^ s) for i in range(4)]))
    step = 1
    while step < dp_count:
        steps.append(functools.partial(swap_dp, step=step))
        step *= 2
    split = where if stepwise(rows_here) else None
    own_sums, above = {}, {}

    def sum_norms(index):
        if index < len(steps):
            own_sums["norms"] = add_call(own_sums["norms"], steps[index](own_sums["norms"]), F32)

    def at(layer, point):
        if isinstance(point, list):
            own_sums["second"] = point
            if not shown:
                shown.extend(
                    call(
                        show_kernel, [sds(quarter, width, dtype=F32)], where, *current, scalars=1
                    )
                )
                drop(*current)
            return ()
        if point[0] == "vectors":
            vectors[layer] = point[1]
            if layer == 0:
                flat = [v for group in vectors for v in group]
                own_sums["norms"] = call(
                    gather_vectors_kernel, [sds(len(flat), width, dtype=F32)], *flat
                )[0]
            return ()
        if split is None:
            return ()
        if layer:
            after = {("norm_one", 0): 1, ("norm_one", 1): 2, ("input", 0): 3}
        else:
            after = {("norm_one", 1): 1, ("attend_back", 1): 2, "input": 3}
        found = ()
        if point in after:
            found = (own_sums["second"][after[point]],)
        if layer == LAYERS - 1:
            return found
        if point == ("norm_two", 1):
            return tuple(above["second"][2:3])
        if point == ("norm_one", 0):
            above["first"] = scatter_finish(where, above["first"])
            return tuple(above["second"][1:2])
        if point == ("attend_back", 1):
            return found + tuple(above["second"][3:])
        if point == "input":
            return found + tuple(above["first"][1:])
        return found

    for layer in reversed(range(LAYERS)):
        triple, (rows_in, attended, context), late = layer_backward(
            incoming, saved_all[layer], norm_gains[layer], tables, split, dp_count,
            functools.partial(at, layer),
        )
        first_weight = saved_all[layer][-2]
        if layer:
            incoming = []
            for k in range(chunks):
                theirs = input_back_call(
                    2 * k + 1, triple, first_weight, BF16, at(layer, ("input", k))
                )
                mine = input_back_call(2 * k, triple, first_weight, F32)
                incoming.append((attended[2 * k], *finish_pair(mine, theirs)))
            drop(first_weight)
            above["second"] = scatter_finish(where, late)
            sums = weight_call(split, [(rows_in, [triple]), (attended, context)], dp_count)
            drop(*rows_in, *attended[1::2], *context)
            above["first"] = scatter_start(sums)
            if split is None:
                above["first"] = scatter_finish(where, above["first"])

    kept, sent = input_last_call(where, triple, first_weight, attended[::2], at(0, "input"))
    sent = swap_core(sent)
    drop(first_weight, *tables[:2])
    second_sum = scatter_finish(where, late)
    arriving = [second_sum[1:2], [], second_sum[2:]]
    sum_norms(0)
    sums = weight_call(split, [(rows_in, [triple]), (attended, context)], dp_count)
    Order.kept = []
    sums = scatter_start(sums)
    mine, theirs = call(
        side_kernel,
        [sds(count, part // 2, width // 2, dtype=F32), sds(count, part // 2, width // 2)],
        where, kept, sent, scalars=1,
    )
    sum_norms(1)
    total = add_call(mine, swap_x(theirs), BF16, arriving[0])
    if split is None:
        near = lax.all_to_all(total, "dp", split_axis=0, concat_axis=0, tiled=True)
        first_sum = scatter_finish(where, sums)
    else:
        moving = exchange_start(total, where)
        first_sum = scatter_finish(where, sums)
        sum_norms(2)
        moving = exchange_middle(*moving, arriving[1])
        sum_norms(3)
        near = exchange_finish(moving, arriving[2] + first_sum[1:])
    far = swap_x(near)
    for index in range(2 if split is None else 4, len(steps) - 1):
        sum_norms(index)
    norms = own_sums["norms"]
    gains_total, biases_total = call(
        norms_kernel, [sds(LAYERS, 2, width, dtype=F32)] * 2, norms, steps[-1](norms)
    )
    received[1] = [total_call(above["first"]), total_call(above["second"])]
    received[0] = [first_sum, second_sum]
    shapes = (
        jnp.swapaxes(project_weight, 1, 2), gate_up_weight, output_weight,
        jnp.swapaxes(down_weight, 1, 2),
    )
    project_grad, gate_up_grad, output_grad, down_grad = call(
        functools.partial(grads_kernel, tuple(tuple(len(g) for g in r) for r in received)),
        [sds(*w.shape, dtype=F32) for w in shapes],
        *[r for groups in received for group in groups for r in group],
    )
    returned = call(
        functools.partial(last_kernel, split is not None), [sds(count, part, width, dtype=F32)],
        dealing_order, where, near, far, swap_core(near), swap_core(far), scalars=2,
    )[0]

    return (
        shown[0][None], returned, jnp.swapaxes(project_grad, 1, 2), gate_up_grad, output_grad,
        jnp.swapaxes(down_grad, 1, 2), gains_total, biases_total,
    )


def solution(mesh):
    placed = (
        P(None, "dp", None),
        P(),
        P(),
        P(None, "dp", None, "tensor"),
        P(None, "dp", None, "tensor"),
        P(None, "tensor", "dp"),
        P(None, "tensor", "dp"),
        P(),
        P(),
        P("dp", "tensor", None),
    )
    return jax.shard_map(
        on_device,
        mesh=mesh,
        in_specs=placed,
        out_specs=(
            P("dp", "tensor", None),
            P(None, "dp", None),
            P(None, "dp", None, "tensor"),
            P(None, "dp", None, "tensor"),
            P(None, "tensor", "dp"),
            P(None, "tensor", "dp"),
            P(),
            P(),
        ),
        check_vma=False,
    )
```

```python
import functools
import math

import jax
import jax.numpy as jnp
import numpy as np
from jax import lax
from jax.experimental import pallas as pl
from jax.experimental.pallas import tpu as pltpu
from jax.sharding import PartitionSpec as P

HD = 64
LAYERS = 2
epsilon = 1e-05
rotary_base = 1000.0
LOG2E = math.log2(math.e)
F32 = jnp.float32
BF16 = jnp.bfloat16
VMEM_LIMIT = 12 * 1024 * 1024
COST = 0.001
KEEP = True


def sds(*shape, dtype=BF16):
    return jax.ShapeDtypeStruct(shape, dtype)


class Order:
    last = ()
    waiting = ()
    kept = []


def keep(*arrays):
    Order.kept.extend(arrays)


def drop(*arrays):
    gone = {id(a) for a in arrays}
    Order.kept = [a for a in Order.kept if id(a) not in gone]


def call(kernel, outs, *operands, flops=0, trans=0, scalars=0, after=(), alias=None):
    after = (*after, *Order.waiting, *Order.last)
    Order.waiting = ()
    taken = {id(a) for a in operands}
    held = [a for a in Order.kept if id(a) not in taken] if KEEP else []
    vmem = pl.BlockSpec(memory_space=pltpu.VMEM)
    smem = pl.BlockSpec(memory_space=pltpu.SMEM)
    moved = sum(a.size * a.dtype.itemsize for a in list(operands) + list(outs))
    used = len(operands)

    def body(*refs):
        kernel(*refs[:used], *refs[used + len(held) + len(after) :])

    results = pl.pallas_call(
        body,
        in_specs=[smem] * scalars
        + [vmem] * (used - scalars + len(held))
        + [pl.BlockSpec(memory_space=pl.ANY)] * len(after),
        out_specs=[vmem] * len(outs),
        out_shape=list(outs),
        input_output_aliases=alias or {},
        compiler_params=pltpu.CompilerParams(vmem_limit_bytes=VMEM_LIMIT),
        cost_estimate=pl.CostEstimate(
            flops=int(COST * flops),
            bytes_accessed=int(COST * moved),
            transcendentals=int(COST * trans),
        ),
    )(*operands, *held, *after)
    Order.last = (min(results, key=lambda r: r.size * r.dtype.itemsize),)
    return results


def swap_core(value):
    return lax.ppermute(value, "tensor", [(i, i ^ 1) for i in range(lax.axis_size("tensor"))])


def swap_x(value):
    return lax.ppermute(value, "tensor", [(i, i ^ 2) for i in range(lax.axis_size("tensor"))])


def swap_dp(value, step):
    return lax.ppermute(value, "dp", [(i, i ^ step) for i in range(lax.axis_size("dp"))])


def stepwise(rows):
    return lax.axis_size("dp") == 8 and rows % 16 == 0


def place_kernel(offsets, index_ref, *refs):
    pieces, out_refs = refs[: len(offsets)], refs[len(offsets) :]
    rows = pieces[0].shape[0]
    for offset, piece in zip(offsets, pieces):
        here = pl.ds(pl.multiple_of((index_ref[3] ^ offset) * rows, rows), rows)
        start = 0
        for out_ref in out_refs:
            last = start + out_ref.shape[1]
            out_ref[here, :] = piece[:, start:last]
            start = last


def copy_kernel(in_ref, out_ref):
    out_ref[...] = in_ref[...]


def gather_start(shard):
    if not stepwise(shard.shape[0]):
        return {0: lax.all_gather(shard, "dp", axis=0, tiled=True)}
    pieces = {0: shard, 1: swap_dp(shard, 1)}
    for step in (2, 4, 6):
        pieces[step] = swap_dp(shard, step)
        pieces[step + 1] = swap_dp(pieces[step], 1)
    return pieces


def first_gather(shard, meanwhile):
    if not stepwise(shard.shape[0]):
        for step in meanwhile:
            step()
        return {0: lax.all_gather(shard, "dp", axis=0, tiled=True)}
    pieces = {0: shard, 1: swap_dp(shard, 1), 2: swap_dp(shard, 2), 4: swap_dp(shard, 4)}
    after = [pieces[1], pieces[2], pieces[4]]
    for step in meanwhile:
        step()
    sent = call(copy_kernel, [sds(*shard.shape)], shard, after=after)[0]
    pieces[6] = swap_dp(sent, 6)
    for step in (2, 4, 6):
        pieces[step + 1] = swap_dp(pieces[step], 1)
    return pieces


def gather_finish(where, pieces, widths, after=()):
    if len(pieces) == 1:
        whole, parts = pieces[0], []
        for width in widths:
            parts.append(whole[:, :width])
            whole = whole[:, width:]
        return parts
    rows = pieces[0].shape[0]
    return call(
        functools.partial(place_kernel, tuple(pieces)),
        [sds(8 * rows, width) for width in widths],
        where, *pieces.values(), scalars=1, after=after,
    )


def scatter_add_kernel(index_ref, kept_ref, *refs):
    steps = kept_ref.shape[0]
    other_refs, out_refs = refs[:-steps], refs[-steps:]
    own = index_ref[3] // 2
    for step, out_ref in enumerate(out_refs):
        start = 0
        for other_ref in other_refs:
            here = pl.ds(start, other_ref.shape[2])
            total = kept_ref[own ^ step, :, here].astype(F32) + other_ref[own ^ step].astype(F32)
            out_ref[:, here] = total.astype(BF16)
            start += other_ref.shape[2]


def scatter_start(sums):
    if isinstance(sums, (list, tuple)):
        return [sums[0]] + [swap_dp(part, 1) for part in sums[1:]]
    return [lax.psum_scatter(sums, "dp", scatter_dimension=0, tiled=True)]


def scatter_finish(where, started):
    if len(started) == 1:
        return started
    kept, *others = started
    count, rows, width = kept.shape
    outs = call(scatter_add_kernel, [sds(rows, width)] * count, where, kept, *others, scalars=1)
    return [outs[0]] + [swap_dp(out, 2 * step) for step, out in enumerate(outs) if step]


def total_kernel(*refs):
    *in_refs, out_ref = refs
    out_ref[...] = total_of(in_refs)


def total_call(parts):
    rows, width = parts[0].shape[-2:]
    return [call(total_kernel, [sds(rows, width, dtype=F32)], *parts)[0]]


def dot_nt(left, right):
    return lax.dot_general(left, right, (((1,), (1,)), ((), ())), preferred_element_type=F32)


def dot_nn(left, right):
    return lax.dot_general(left, right, (((1,), (0,)), ((), ())), preferred_element_type=F32)


def dot_tn(left, right):
    return lax.dot_general(left, right, (((0,), (0,)), ((), ())), preferred_element_type=F32)


def swap_halves(values):
    width = values.shape[-1]
    lane = lax.broadcasted_iota(jnp.int32, values.shape, 1)
    return jnp.where(
        lane % HD < HD // 2,
        pltpu.roll(values, width - HD // 2, 1),
        pltpu.roll(values, HD // 2, 1),
    )


def widen(table, width):
    return jnp.concatenate([table] * (width // table.shape[1]), axis=1)


def qkv_kernel(*refs):
    *x_refs, w_ref, cos_ref, sin_ref, bias_ref, q_ref, k_ref, v_ref, kt_ref, vt_ref = refs
    inner = v_ref.shape[1]
    extra = q_ref.shape[1] - inner
    weight = w_ref[:, : 3 * inner]
    block = 256
    parts = [
        x_ref.at[pl.ds(start, block), :]
        for x_ref in x_refs
        for start in range(0, x_ref.shape[0], block)
    ]
    for step, x_ref in enumerate(parts):
        here = pl.ds(step * block, block)
        projected = dot_nn(x_ref[...], weight)
        pair = projected[:, : 2 * inner]
        turned = pair * widen(cos_ref[here, :], 2 * inner) + swap_halves(pair) * widen(
            sin_ref[here, :], 2 * inner
        )
        lane = lax.broadcasted_iota(jnp.int32, (block, extra), 1)
        queries = turned[:, :inner] * (1.0 / math.sqrt(HD))
        keys = turned[:, inner:]
        values = projected[:, 2 * inner :]
        one = jnp.where(lane == 0, 1.0, 0.0)
        mark = jnp.where(lane == 0, bias_ref[here, :extra], 0.0)
        q_ref[here, :] = jnp.concatenate([queries, one], axis=1).astype(BF16)
        k_ref[here, :] = jnp.concatenate([keys, mark], axis=1).astype(BF16)
        v_ref[here, :] = values.astype(BF16)
        kt_ref[:, here] = keys.T.astype(BF16)
        vt_ref[:, here] = values.T.astype(BF16)


def qkv_call(pieces, weight, tables, inner, after):
    rows = sum(p.shape[0] for p in pieces)
    width = weight.shape[0]
    return call(
        qkv_kernel,
        [sds(rows, inner + HD), sds(rows, inner + HD), sds(rows, inner)] + [sds(inner, rows)] * 2,
        *pieces, weight, *tables,
        flops=2 * rows * width * 3 * inner,
        after=after,
    )


def head_mask(shape, head, inner):
    lane = lax.broadcasted_iota(jnp.int32, shape, 1)
    return ((lane >= head * HD) & (lane < (head + 1) * HD)) | (lane >= inner)


def attend_kernel(part, q_ref, k_ref, vt_ref, w_ref, c_ref, lse_ref, out_ref):
    rows, inner = c_ref.shape
    queries = q_ref[pl.ds(part * rows, rows), :]
    columns, stats = [], []
    for head in range(inner // HD):
        masked = jnp.where(head_mask(queries.shape, head, inner), queries, 0)
        scores = dot_nt(k_ref[...], masked)
        shift = jnp.max(scores, axis=0, keepdims=True) * LOG2E
        exps = jnp.exp2(scores * LOG2E - shift)
        total = jnp.sum(exps, axis=0, keepdims=True)
        mixed = dot_nn(vt_ref[head * HD : (head + 1) * HD, :], exps.astype(BF16))
        columns.append(mixed * (1.0 / total))
        stats.append(shift + jnp.log2(total))
    context = jnp.concatenate(columns, axis=0).T.astype(BF16)
    c_ref[...] = context
    pad = lse_ref.shape[0] - len(stats)
    lse_ref[...] = jnp.concatenate(stats + [jnp.zeros((pad, rows), F32)], axis=0)
    out_ref[...] = dot_nt(context, w_ref[:, 3 * inner :]).astype(out_ref.dtype)


def attend_call(part, queries, keys, values_t, weight, dtype, after=()):
    length, padded = queries.shape
    rows, inner, width = length // 4, padded - HD, weight.shape[0]
    return call(
        functools.partial(attend_kernel, part),
        [sds(rows, inner), sds(8, rows, dtype=F32), sds(rows, width, dtype=dtype)],
        queries, keys, values_t, weight,
        flops=4 * rows * length * 256 * (inner // HD) + 2 * rows * inner * width,
        trans=rows * length * (inner // HD),
        after=after,
    )


def norm_kernel(base_ref, pair_ref, other_ref, gain_ref, shift_ref, low_ref, normal_ref, scale_ref, *out):
    values = base_ref[...].astype(F32) + (pair_ref[...] + other_ref[...].astype(F32))
    centred = values - jnp.mean(values, axis=-1, keepdims=True)
    scaled = lax.rsqrt(jnp.mean(centred * centred, axis=-1, keepdims=True) + epsilon)
    normal = centred * scaled
    result = normal * gain_ref[...] + shift_ref[...]
    low_ref[...] = result.astype(BF16)
    normal_ref[...] = normal.astype(BF16)
    scale_ref[...] = jnp.broadcast_to(scaled, scale_ref.shape)
    for ref in out:
        ref[...] = result


def norm_call(base, pair, other, gain, shift, last, after=()):
    rows, width = pair.shape
    return call(
        norm_kernel,
        [sds(rows, width), sds(rows, width), sds(rows, 128, dtype=F32)]
        + [sds(rows, width, dtype=F32)] * last,
        base, pair, other, gain, shift,
        flops=10 * rows * width,
        after=after,
    )


def norm_back_kernel(*refs):
    *in_refs, normal_ref, scale_ref, gain_ref, low_ref, vec_ref = refs
    incoming = in_refs[0][...].astype(F32)
    for ref in in_refs[1:]:
        incoming = incoming + ref[...].astype(F32)
    normal = normal_ref[...].astype(F32)
    weighted = incoming * gain_ref[...]
    result = scale_ref[:, 0:1] * (
        weighted
        - jnp.mean(weighted, axis=-1, keepdims=True)
        - normal * jnp.mean(weighted * normal, axis=-1, keepdims=True)
    )
    low_ref[...] = result.astype(BF16)
    vec_ref[0:1, :] = jnp.sum(incoming * normal, axis=0, keepdims=True)
    vec_ref[1:2, :] = jnp.sum(incoming, axis=0, keepdims=True)


def norm_back_call(incoming, normal, scale, gain, after=()):
    rows, width = normal.shape
    return call(
        norm_back_kernel,
        [sds(rows, width), sds(2, width, dtype=F32)],
        *incoming, normal, scale, gain,
        flops=16 * rows * width,
        after=after,
    )


def mask_of(where_ref, chunk, rows):
    place = lax.broadcasted_iota(jnp.int32, (rows, 128), 0)
    usable = (2 * chunk + where_ref[0]) * rows + place < where_ref[4]
    return jnp.where(usable, 1.0, 0.0)[:, 0:1]


def seed_kernel(chunk, where_ref, own_ref, other_ref, out_ref):
    seed = jnp.where(where_ref[1] == chunk, own_ref[...].astype(F32), other_ref[...].astype(F32))
    out_ref[...] = (seed * mask_of(where_ref, chunk, out_ref.shape[0])).astype(BF16)


def show_kernel(where_ref, first_ref, second_ref, out_ref):
    rows = out_ref.shape[0]
    first = first_ref[...].astype(F32) * mask_of(where_ref, 0, rows)
    second = second_ref[...].astype(F32) * mask_of(where_ref, 1, rows)
    out_ref[...] = jnp.where(where_ref[1] == 0, first, second)


def gather_vectors_kernel(*refs):
    *in_refs, out_ref = refs
    for row in range(out_ref.shape[0] // 2):
        pair = in_refs[2 * row][...] + in_refs[2 * row + 1][...]
        out_ref[2 * row : 2 * row + 2, :] = pair * 0.5


def norms_kernel(left_ref, right_ref, gains_ref, biases_ref):
    for row in range(left_ref.shape[0] // 2):
        for member, out_ref in enumerate((gains_ref, biases_ref)):
            here = pl.ds(2 * row + member, 1)
            out_ref[row // 2, pl.ds(row % 2, 1), :] = left_ref[here, :] + right_ref[here, :]


def add_kernel(left_ref, right_ref, out_ref):
    total = left_ref[...].astype(F32) + right_ref[...].astype(F32)
    out_ref[...] = total.astype(out_ref.dtype)


def add_call(left, right, dtype, after=()):
    return call(add_kernel, [sds(*left.shape, dtype=dtype)], left, right, after=after)[0]


def mlp_parts(w_ref):
    hidden = w_ref.shape[1] // 3
    return [w_ref[:, part * hidden : (part + 1) * hidden] for part in range(3)]


def mlp_kernel(x_ref, w_ref, out_ref):
    gate_weight, up_weight, down_weight = mlp_parts(w_ref)
    rows = x_ref[...]
    gate = dot_nn(rows, gate_weight)
    up = dot_nn(rows, up_weight)
    active = (gate * jax.nn.sigmoid(gate) * up).astype(BF16)
    out_ref[...] = dot_nt(active, down_weight).astype(out_ref.dtype)


def mlp_call(piece, weight, dtype):
    rows, width = piece.shape
    return call(
        mlp_kernel, [sds(rows, width, dtype=dtype)], piece, weight,
        flops=2 * rows * width * weight.shape[1],
        trans=rows * weight.shape[1] // 3,
    )[0]


def mlp_back_kernel(x_ref, grad_ref, w_ref, act_ref, dg_ref, out_ref):
    gate_weight, up_weight, down_weight = mlp_parts(w_ref)
    hidden = act_ref.shape[1]
    rows = x_ref[...]
    gate = dot_nn(rows, gate_weight)
    up = dot_nn(rows, up_weight)
    active_grad = dot_nn(grad_ref[...], down_weight)
    sigmoid = jax.nn.sigmoid(gate)
    silu = gate * sigmoid
    act_ref[...] = (silu * up).astype(BF16)
    gate_grad = (active_grad * up * sigmoid * (1.0 + gate * (1.0 - sigmoid))).astype(BF16)
    up_grad = (active_grad * silu).astype(BF16)
    dg_ref[:, :hidden] = gate_grad
    dg_ref[:, hidden:] = up_grad
    partial = dot_nt(gate_grad, gate_weight) + dot_nt(up_grad, up_weight)
    out_ref[...] = partial.astype(out_ref.dtype)


def mlp_back_call(piece, grad, weight, dtype):
    rows, width = piece.shape
    hidden = weight.shape[1] // 3
    return call(
        mlp_back_kernel,
        [sds(rows, hidden), sds(rows, 2 * hidden), sds(rows, width, dtype=dtype)],
        piece, grad, weight,
        flops=10 * rows * width * hidden,
        trans=rows * hidden,
    )


def context_back_kernel(mine_in, theirs_in, w_ref, dc_ref):
    inner = dc_ref.shape[1]
    half = mine_in.shape[0]
    weight = w_ref[:, 3 * inner :]
    dc_ref[:half, :] = dot_nn(mine_in[...], weight).astype(BF16)
    dc_ref[half:, :] = dot_nn(theirs_in[...], weight).astype(BF16)


def context_back_call(mine, theirs, weight):
    half, width = mine.shape
    inner = weight.shape[1] // 4
    return call(
        context_back_kernel, [sds(2 * half, inner)], mine, theirs, weight,
        flops=4 * half * width * inner,
    )[0]


def attend_back_kernel(
    first, last, q_ref, dc_ref, lse_ref, k_ref, v_ref, kt_ref, cos_ref, sin_ref, *refs
):
    if first:
        dk_in, dv_in, *refs = refs
    if last and first:
        dq_in, *refs = refs
    dq_ref, dk_ref, dv_ref = refs
    rows, inner = dc_ref.shape
    length, padded = k_ref.shape
    block = min(256, rows)

    def turn_back(gradient, cosine, sine):
        cosine = widen(cosine, gradient.shape[1])
        sine = widen(sine, gradient.shape[1])
        return (gradient * cosine - swap_halves(gradient) * sine)[:, :inner]

    if first:
        dk_ref[...] = dk_in[...]
        dv_ref[...] = dv_in[...]
    else:
        dk_ref[...] = jnp.zeros_like(dk_ref)
        dv_ref[...] = jnp.zeros_like(dv_ref)

    def step_of(step, carry):
        start = pl.multiple_of(step * block, block)
        here = pl.ds(start, block)
        there = pl.ds(pl.multiple_of(first + step * block, block), block)
        queries = q_ref[there, :]
        context_grad = dc_ref[here, :]
        columns, score_grads, all_weights, all_masked, all_grads = [], [], [], [], []
        for head in range(inner // HD):
            masked = jnp.where(head_mask(queries.shape, head, inner), queries, 0)
            masked_grad = jnp.where(head_mask(context_grad.shape, head, inner), context_grad, 0)
            scores = dot_nt(k_ref[...], masked)
            weights = jnp.exp2(scores * LOG2E - lse_ref[head : head + 1, there])
            weight_grad = dot_nt(v_ref[...], masked_grad)
            inner_sum = jnp.sum(weights * weight_grad, axis=0, keepdims=True)
            score_grad = (weights * (weight_grad - inner_sum)).astype(BF16)
            columns.append(dot_nn(kt_ref[head * HD : (head + 1) * HD, :], score_grad))
            score_grads.append(score_grad)
            all_weights.append(weights.astype(BF16))
            all_masked.append(masked)
            all_grads.append(masked_grad)
        join = jnp.concatenate
        dk_ref[...] += dot_nn(join(score_grads, axis=1), join(all_masked, axis=0))
        dv_ref[...] += dot_nn(join(all_weights, axis=1), join(all_grads, axis=0))
        columns.append(jnp.zeros((padded - inner, block), F32))
        query_grad = jnp.concatenate(columns, axis=0).T * (1.0 / math.sqrt(HD))
        turned = turn_back(query_grad, cos_ref[there, :], sin_ref[there, :]).astype(BF16)
        dq_ref[there if last else here, :inner] = turned
        return carry

    lax.fori_loop(0, rows // block, step_of, 0)
    if last:
        if first:
            dq_ref[:first, :inner] = dq_in[...]
        dq_ref[:, inner : 2 * inner] = turn_back(dk_ref[...], cos_ref[...], sin_ref[...]).astype(
            BF16
        )
        dq_ref[:, 2 * inner :] = dv_ref[...].astype(BF16)


def attend_back_call(first, last, operands, carried, after):
    length, padded = operands[0].shape
    rows, inner = operands[1].shape
    out = sds(length, 3 * inner) if last else sds(rows, inner)
    return call(
        functools.partial(attend_back_kernel, first, last),
        [out, sds(length, padded, dtype=F32), sds(length, inner, dtype=F32)],
        *operands, *carried,
        flops=10 * rows * length * 256 * (inner // HD),
        trans=rows * length * (inner // HD),
        after=after,
    )


def input_back_kernel(part, dp_ref, w_ref, out_ref):
    rows = out_ref.shape[0]
    here = pl.ds(part * rows, rows)
    out_ref[...] = dot_nt(dp_ref[here, :], w_ref[:, : dp_ref.shape[1]]).astype(out_ref.dtype)


def input_back_call(part, triple, weight, dtype, after=()):
    rows, width = triple.shape[0] // 4, weight.shape[0]
    return call(
        functools.partial(input_back_kernel, part),
        [sds(rows, width, dtype=dtype)],
        triple, weight,
        flops=2 * rows * triple.shape[1] * width,
        after=after,
    )[0]


def input_last_kernel(index_ref, dp_ref, w_ref, *refs):
    *grad_refs, kept_ref, sent_ref = refs
    core, side = index_ref[0], index_ref[1]
    rows, total = dp_ref.shape
    quarter = rows // 4
    split = kept_ref.shape[1]
    weight = w_ref[:, :total]
    for step in range(4):
        chunk, part = step // 2, step % 2
        partial = dot_nt(dp_ref[pl.ds(step * quarter, quarter), :], weight)
        if not part:
            partial = partial + jnp.where(side == chunk, grad_refs[chunk][...].astype(F32), 0.0)
        start = pl.multiple_of((2 * chunk + (core ^ part)) * quarter, quarter)
        low, high = partial[:, :split], partial[:, split:]
        kept_ref[pl.ds(start, quarter), :] = jnp.where(core == 0, low, high)
        sent_ref[pl.ds(start, quarter), :] = jnp.where(core == 0, high, low).astype(BF16)


def input_last_call(index, triple, weight, grads, after):
    rows, width = triple.shape[0], weight.shape[0]
    return call(
        input_last_kernel,
        [sds(rows, width // 2, dtype=F32), sds(rows, width // 2)],
        index, triple, weight, *grads,
        flops=2 * rows * triple.shape[1] * width, scalars=1, after=after,
    )


def side_kernel(index_ref, kept_ref, other_ref, mine_ref, theirs_ref):
    side = index_ref[1]
    count, half, _ = mine_ref.shape
    for block in range(count):
        halves = []
        for part in range(2):
            here = pl.ds((2 * block + part) * half, half)
            halves.append(kept_ref[here, :] + other_ref[here, :].astype(F32))
        mine_ref[block] = jnp.where(side == 0, halves[0], halves[1])
        theirs_ref[block] = jnp.where(side == 0, halves[1], halves[0]).astype(BF16)


SHARE = 768


def weight_kernel(counts, index_ref, *refs):
    in_count = sum(left + right for left, right in counts)
    in_refs, (kept_ref, *sent_refs) = refs[:in_count], refs[in_count:]
    blocks, rows, _ = kept_ref.shape
    width = blocks * rows * (2 if sent_refs else 1)
    wide = 4 * rows if width % (4 * rows) == 0 and (4 * rows) % 128 == 0 else width
    column = 0
    lefts, rights = [], []
    for left_count, right_count in counts:
        lefts.append(in_refs[:left_count])
        rights.append(in_refs[left_count : left_count + right_count])
        in_refs = in_refs[left_count + right_count :]
    for left, right in zip(lefts, rights):
        columns = right[0].shape[1]
        share = min(columns, SHARE)
        ratio = len(left) // len(right)
        for start in range(0, columns, share):
            for first in range(0, width, wide):
                total = None
                for number, left_ref in enumerate(left):
                    size = left_ref.shape[0]
                    right_ref = right[number // ratio]
                    term = dot_tn(
                        left_ref[:, first : first + wide],
                        right_ref[
                            pl.ds((number % ratio) * size, size), start : start + share
                        ],
                    )
                    total = term if total is None else total + term
                where = pl.ds(column + start, share)
                there = pl.ds((column + start) % SHARE, share)
                for offset in range(0, wide, 2 * rows):
                    even = total[offset : offset + rows].astype(BF16)
                    odd = total[offset + rows : offset + 2 * rows].astype(BF16)
                    block = (first + offset) // (2 * rows)
                    if not sent_refs:
                        kept_ref[2 * block, :, where] = even
                        kept_ref[2 * block + 1, :, where] = odd
                    else:
                        sent_ref = sent_refs[(column + start) // SHARE]
                        kept_ref[block, :, where] = jnp.where(index_ref[5] == 0, even, odd)
                        sent_ref[block, :, there] = jnp.where(index_ref[5] == 0, odd, even)
        column += columns


def weight_call(parity, pairs, count, after=()):
    width = pairs[0][0][0].shape[1]
    total = sum(right[0].shape[1] for _, right in pairs)
    rows = sum(piece.shape[0] for piece in pairs[0][0])
    operands = [piece for left, right in pairs for piece in (*left, *right)]
    counts = tuple((len(left), len(right)) for left, right in pairs)
    flops = 2 * rows * width * total
    if parity is None:
        return call(
            functools.partial(weight_kernel, counts, None),
            [sds(count, width // count, total)],
            *operands, flops=flops, after=after,
        )[0]
    shape = (count // 2, width // count)
    return call(
        functools.partial(weight_kernel, counts),
        [sds(*shape, total)] + [sds(*shape, SHARE)] * (total // SHARE),
        parity, *operands, flops=flops, scalars=1, after=after,
    )


def total_of(refs):
    parts = [
        part
        for ref in refs
        for part in ([ref[i] for i in range(ref.shape[0])] if len(ref.shape) == 3 else [ref[...]])
    ]
    total = parts[0].astype(F32)
    for part in parts[1:]:
        total = total + part.astype(F32)
    return total


def grads_kernel(counts, *refs):
    out_refs = refs[-4:]
    position = 0
    for layer, groups in enumerate(counts):
        parts = []
        for count in groups:
            parts.append(total_of(refs[position : position + count]))
            position += count
        whole = jnp.concatenate(parts, axis=1)
        project_ref, gate_up_ref, output_ref, down_ref = out_refs
        inner, hidden = output_ref.shape[1], down_ref.shape[2]
        for part in range(3):
            project_ref[layer, part] = whole[:, part * inner : (part + 1) * inner]
        output_ref[layer] = whole[:, 3 * inner : 4 * inner].T
        for part in range(2):
            start = 4 * inner + part * hidden
            gate_up_ref[layer, :, part, :] = whole[:, start : start + hidden]
        down_ref[layer] = whole[:, 4 * inner + 2 * hidden :]


def last_kernel(
    turned, order_ref, where_ref, near_ref, far_ref, near_other_ref, far_other_ref, out_ref
):
    core, side = where_ref[0], where_ref[1]
    count, half, split = near_ref.shape
    for source in range(count):
        target = order_ref[where_ref[3] ^ source if turned else source]
        for ref, flip in ((near_ref, 0), (far_ref, 1)):
            here = pl.ds(pl.multiple_of((side ^ flip) * half, half), half)
            other = near_other_ref if ref is near_ref else far_other_ref
            own, swapped = ref[source].astype(F32), other[source].astype(F32)
            out_ref[target, here, :split] = jnp.where(core == 0, own, swapped)
            out_ref[target, here, split:] = jnp.where(core == 0, swapped, own)


def pair_kernel(mine_ref, other_ref, pair_ref, low_ref):
    pair = mine_ref[...] + other_ref[...].astype(F32)
    pair_ref[...] = pair
    low_ref[...] = pair.astype(BF16)


def finish_pair(mine, theirs, after=()):
    other = swap_core(theirs)
    outs = [sds(*mine.shape, dtype=F32), sds(*mine.shape)]
    pair, low = call(pair_kernel, outs, mine, other, after=after)
    return pair, swap_x(low)


def layer_forward(
    pieces, residual, first_weight, second_weight, gains, shifts, tables, inner, last, at
):
    chunks = len(residual)
    queries, keys, values, keys_t, values_t = qkv_call(
        pieces, first_weight, tables, inner, ()
    )
    keep(*pieces, queries, keys, values, keys_t, values_t, first_weight)
    context, logsum, first_norm, hidden_pieces, pairs = [], [], [], [], []
    for k in range(chunks):
        args = (queries, keys, values_t, first_weight)
        theirs = attend_call(2 * k + 1, *args, BF16)
        keep(theirs[0])
        mine = attend_call(2 * k, *args, F32)
        keep(mine[0])
        context += [mine[0], theirs[0]]
        logsum += [mine[1], theirs[1]]
        pairs.append(finish_pair(mine[2], theirs[2], ()))
    drop(values_t)
    logsum = jnp.concatenate(logsum, axis=1)
    keep(logsum)
    second_norm, result, result_pieces, second_pairs = [], [], [], []
    mine, theirs = [], []
    for k in range(chunks):
        low, *kept = norm_call(
            residual[k], *pairs[k], gains[0:1], shifts[0:1], False, at(("norm_one", k))
        )
        first_norm.append(kept)
        hidden_pieces += [low, swap_core(low)]
        keep(*kept)
        if k == 0:
            second_weight = second_weight()
        mine.append(mlp_call(low, second_weight, F32))
        keep(low, second_weight)
    for k in range(chunks):
        theirs.append(mlp_call(hidden_pieces[2 * k + 1], second_weight, BF16))
        keep(hidden_pieces[2 * k + 1])
    for k in range(chunks):
        second_pairs.append(finish_pair(mine[k], theirs[k]))
    for k in range(chunks):
        low, *kept = norm_call(
            hidden_pieces[2 * k], *second_pairs[k], gains[1:2], shifts[1:2], last,
            at(("norm_two", k)),
        )
        keep(*kept[:2])
        second_norm.append(kept[:2])
        result += kept[2:]
        result_pieces.append(low)
    saved = (
        pieces, queries, keys, values, keys_t, context, logsum,
        first_norm, hidden_pieces, second_norm, first_weight, second_weight,
    )
    return result, result_pieces, saved


def layer_backward(incoming, saved, gains, tables, parity, count, at):
    (
        pieces, queries, keys, values, keys_t, context, logsum,
        first_norm, hidden_pieces, second_norm, first_weight, second_weight,
    ) = saved
    chunks = len(incoming)
    mixed, active, vectors_two, pair_grads, pairs = [], [], [], [], []
    outs = []
    for k in range(chunks):
        low, vector = norm_back_call(
            incoming[k], *second_norm[k], gains[1:2], at(("norm_two", k))
        )
        drop(*second_norm[k])
        vectors_two.append(vector)
        mixed += [low, swap_core(low)]
        outs += mlp_back_call(hidden_pieces[2 * k], low, second_weight, F32)
        keep(*outs[-3:-1], low)
    for k in range(chunks):
        outs += mlp_back_call(hidden_pieces[2 * k + 1], mixed[2 * k + 1], second_weight, BF16)
        keep(*outs[-3:-1], mixed[2 * k + 1])
    for k in range(chunks):
        here, there = outs[3 * k : 3 * k + 3], outs[3 * (chunks + k) : 3 * (chunks + k) + 3]
        active += [here[0], there[0]]
        pair_grads += [here[1], there[1]]
        pairs.append(finish_pair(here[2], there[2]))
    drop(second_weight)
    at("sums")
    late = scatter_start(
        weight_call(parity, [(hidden_pieces, pair_grads), (mixed, active)], count)
    )
    at(late)
    drop(*hidden_pieces, *pair_grads, *active, *mixed[1::2])
    attended, vectors_one, carried = [], [], ()
    for k in range(chunks):
        low, vector = norm_back_call(
            (mixed[2 * k], *pairs[k]), *first_norm[k], gains[0:1], at(("norm_one", k))
        )
        drop(*first_norm[k], mixed[2 * k])
        vectors_one.append(vector)
        if k == chunks - 1:
            at(("vectors", vectors_one + vectors_two))
        attended += [low, swap_core(low)]
        context_grad = context_back_call(*attended[2 * k :], first_weight)
        keep(*attended[2 * k :])
        operands = (queries, context_grad, logsum, keys, values, keys_t, *tables[:2])
        out, dk, dv = attend_back_call(
            k * context_grad.shape[0], k == chunks - 1, operands, carried, at(("attend_back", k))
        )
        carried = (dk, dv, out)
        at(("attend", k))
    drop(queries, logsum, keys, values, keys_t)
    return out, (pieces, attended, context), late


def rotary_tables(length):
    half = HD // 2
    angles = np.arange(length, dtype=np.float64)[:, None] * np.exp(
        np.arange(half, dtype=np.float64)[None, :] * (-2.0 * math.log(rotary_base) / HD)
    )
    cosine, sine = np.cos(angles), np.sin(angles)
    return (
        np.concatenate([cosine] * 4, axis=1).astype(np.float32),
        np.concatenate([-sine, sine] * 2, axis=1).astype(np.float32),
    )


def turn_kernel(where_ref, in_ref, *out_refs):
    index = where_ref[3]
    for step in range(4):
        for flip in range(2):
            out_refs[flip][step] = in_ref[index ^ (2 * step + flip)]


def couple_kernel(own_ref, other_ref, *out_refs):
    for step, out_ref in enumerate(out_refs):
        out_ref[0] = own_ref[step]
        out_ref[1] = other_ref[step]


def join_kernel(*refs):
    *in_refs, out_ref = refs
    for step, ref in enumerate(in_refs):
        out_ref[2 * step : 2 * step + 2] = ref[...]


def exchange_start(blocks, where):
    _, rows, width = blocks.shape
    own, sent = call(turn_kernel, [sds(4, rows, width)] * 2, where, blocks, scalars=1)
    return own, swap_dp(sent, 1)


def exchange_middle(own, sent, after=()):
    _, rows, width = own.shape
    pairs = call(couple_kernel, [sds(2, rows, width)] * 4, own, sent, after=after)
    return [pairs[0]] + [swap_dp(pairs[step], 2 * step) for step in (1, 2, 3)]


def exchange_finish(moved, after=()):
    _, rows, width = moved[0].shape
    return call(join_kernel, [sds(8, rows, width)], *moved, after=after)[0]


def deal_kernel(where_ref, *refs):
    *in_refs, out_ref = refs
    core, own, index = where_ref[0], where_ref[2], where_ref[3]
    count, share, _ = in_refs[0].shape
    part = out_ref.shape[0] // count
    for step in range(count):
        source = index ^ step
        quarter = source // 2
        block = 2 * ((quarter // 2) * 2 + ((quarter % 2) ^ core)) + source % 2
        for offset, ref in enumerate(in_refs):
            start = pl.multiple_of(block * part + (own ^ offset) * share, share)
            out_ref[pl.ds(start, share), :] = ref[step]


def deal_steps(tokens, dealing_order, where):
    count, part, width = tokens.shape
    share = part // 4
    mine = lax.dynamic_slice_in_dim(tokens, where[2] * share, share, 1)
    picked = jnp.take(mine, dealing_order, axis=0)
    state = []

    def spread(arrived):
        far = swap_x(arrived)
        state[:] = [arrived, swap_core(arrived), far, swap_core(far)]

    if count != 8 or share % 16:
        spread(lax.all_to_all(picked, "dp", split_axis=0, concat_axis=0, tiled=True))
        return [], state
    state[:] = exchange_start(picked, where)

    def middle():
        state[:] = exchange_middle(*state)

    def finish():
        spread(exchange_finish(state))

    return [middle, finish], state


def deal_finish(pieces, where, local_order):
    count, share, width = pieces[0].shape
    length = 4 * count * share
    if count == 8 and share % 16 == 0:
        return call(deal_kernel, [sds(length, width)], where, *pieces, scalars=1)[0]
    stacked = jnp.stack(pieces)
    blocks = [
        lax.dynamic_index_in_dim(stacked, where[2] ^ slot, 0, keepdims=False) for slot in range(4)
    ]
    whole = jnp.stack(blocks, axis=1).reshape(length, width)
    return local_order(whole).reshape(length, width)


def pack_kernel(project_ref, gate_up_ref, output_ref, down_ref, *out_refs):
    inner, hidden = output_ref.shape[1], down_ref.shape[2]
    columns = [project_ref[0, part] for part in range(3)] + [output_ref[0].T]
    columns += [gate_up_ref[0, :, part] for part in range(2)] + [down_ref[0]]
    for out_ref in out_refs:
        start = 0
        while start < out_ref.shape[1]:
            column = columns.pop(0)
            out_ref[:, start : start + column.shape[1]] = column.astype(BF16)
            start += column.shape[1]


def pack_call(layer, together, project, gate_up, output, down, after=()):
    operands = (jnp.swapaxes(project, 1, 2), gate_up, output, jnp.swapaxes(down, 1, 2))
    rows, inner, hidden = project.shape[1], output.shape[1], down.shape[1]
    sizes = [4 * inner, 3 * hidden]
    outs = [sds(rows, n) for n in ([sum(sizes)] if together else sizes)]
    after = (*after, *Order.last)

    def spec(w):
        return pl.BlockSpec((1, *w.shape[1:]), lambda i: (layer,) + (0,) * (w.ndim - 1))

    def body(*refs):
        pack_kernel(*refs[:4], *refs[4 + len(after) :])

    results = pl.pallas_call(
        body,
        grid=(1,),
        in_specs=[spec(w) for w in operands] + [pl.BlockSpec(memory_space=pl.ANY)] * len(after),
        out_specs=[pl.BlockSpec(out.shape, lambda i: (0, 0)) for out in outs],
        out_shape=outs,
        compiler_params=pltpu.CompilerParams(vmem_limit_bytes=VMEM_LIMIT),
        cost_estimate=pl.CostEstimate(flops=0, bytes_accessed=1000, transcendentals=0),
    )(*operands, *after)
    Order.last = (results[0],)
    return results


def on_device(
    tokens, dealing_order, lengths, project_weight, gate_up_weight, output_weight, down_weight,
    norm_gains, norm_biases, cotangent,
):
    Order.last, Order.waiting, Order.kept = (), (), []
    dp_index = lax.axis_index("dp")
    tensor_index = lax.axis_index("tensor")
    core, side = tensor_index % 2, tensor_index // 2
    count, part, width = tokens.shape
    dp_count = lax.axis_size("dp")
    length = 4 * cotangent.shape[1]
    quarter = length // 4
    chunks = 2
    inner = output_weight.shape[1]
    hidden = down_weight.shape[1]
    rows_here = project_weight.shape[1]

    sources = (project_weight, gate_up_weight, output_weight, down_weight)
    length_now = jnp.take(lengths, jnp.take(dealing_order, dp_index))
    where = jnp.stack([core, side, tensor_index, dp_index, length_now, dp_index % 2]).astype(jnp.int32)
    own = cotangent[0]
    other = swap_x(own)

    def local_order(rows):
        split = rows.reshape(chunks, 2, quarter, rows.shape[-1])
        return jnp.where(core == 0, split, split[:, ::-1])

    places = jnp.arange(length)[:, None]
    marks = jnp.where(places < length_now, 0.0, -1e30).astype(F32)
    tables = tuple(
        local_order(table).reshape(length, 128)
        for table in (*map(jnp.asarray, rotary_tables(length)), jnp.broadcast_to(marks, (length, 128)))
    )
    shard = pack_call(0, True, *sources)[0]
    meanwhile, moving = deal_steps(tokens, dealing_order, where)
    pieces = first_gather(shard, meanwhile)
    widths = (4 * inner, 3 * hidden)
    coming = [(pieces, None)]
    saved_all = []
    keep(*tables[:2])
    for layer in range(LAYERS):
        here, points = coming[layer], {}
        if layer < LAYERS - 1:
            before = [pieces[step] for step in (6, 3, 5)] if layer == 0 and len(pieces) > 1 else ()
            packed = pack_call(layer + 1, False, *sources, after=before)
            first, second = (gather_start(part) for part in packed)
            coming.append((first, second))
            if len(first) > 1:
                points = {
                    "place": (first, (2, 4)),
                    ("norm_one", 0): (first, (6, 1, 3, 5)),
                    ("norm_one", 1): (second, (2, 4, 1)),
                    ("norm_two", 0): (second, (3,)),
                    ("norm_two", 1): (second, (6, 5)),
                }
        if layer and len(here[0]) > 1:
            points[("norm_one", 0)] = (here[1], (7,))

        def at(point, points=points, layer=layer):
            if layer == 0 and point == ("norm_one", 0):
                for k in range(chunks):
                    incoming.append(
                        call(
                            functools.partial(seed_kernel, k), [sds(quarter, width)],
                            where, own, other, scalars=1,
                        )
                    )
                    keep(*incoming[-1])
            found, steps = points.get(point, ({}, ()))
            return tuple(found[step] for step in steps)

        if layer == 0:
            incoming = []
            first_weight, second_weight = gather_finish(where, here[0], widths, at("place"))
            dealt = deal_finish(moving, where, local_order)
            pieces = [dealt]
            residual = [dealt[2 * k * quarter : (2 * k + 1) * quarter] for k in range(chunks)]
            late_weight = lambda: second_weight
        else:
            (first_weight,) = gather_finish(where, here[0], widths[:1])
            late_weight = lambda here=here: gather_finish(where, here[1], widths[1:])[0]
        current, residual, saved = layer_forward(
            pieces, residual, first_weight, late_weight, norm_gains[layer], norm_biases[layer],
            tables, inner, False, at,
        )
        saved_all.append(saved)
        if layer < LAYERS - 1:
            pieces = [p for piece in residual for p in (piece, swap_core(piece))]
    current = residual
    keep(*current)
    shown = []
    received, vectors, steps = [None] * LAYERS, [None] * LAYERS, []
    for step in (1, 2):
        steps.append(lambda v, s=step: lax.ppermute(v, "tensor", [(i, i ^ s) for i in range(4)]))
    step = 1
    while step < dp_count:
        steps.append(functools.partial(swap_dp, step=step))
        step *= 2
    split = where if stepwise(rows_here) else None
    own_sums, above = {}, {}

    def sum_norms(index):
        if index < len(steps):
            own_sums["norms"] = add_call(own_sums["norms"], steps[index](own_sums["norms"]), F32)

    def at(layer, point):
        if isinstance(point, list):
            own_sums["second"] = point
            if not shown:
                shown.extend(
                    call(
                        show_kernel, [sds(quarter, width, dtype=F32)], where, *current, scalars=1
                    )
                )
                drop(*current)
            return ()
        if point[0] == "vectors":
            vectors[layer] = point[1]
            if layer == 0:
                flat = [v for group in vectors for v in group]
                own_sums["norms"] = call(
                    gather_vectors_kernel, [sds(len(flat), width, dtype=F32)], *flat
                )[0]
            return ()
        if split is None:
            return ()
        if layer:
            after = {("norm_one", 1): 1, ("attend_back", 1): 2, ("input", 0): 3}
        else:
            after = {("norm_one", 1): 1, ("attend_back", 1): 2, "input": 3}
        found = ()
        if point in after:
            found = (own_sums["second"][after[point]],)
        if layer == LAYERS - 1:
            return found
        if point == ("norm_two", 1):
            return tuple(above["second"][2:3])
        if point == ("norm_one", 0):
            above["first"] = scatter_finish(where, above["first"])
            return tuple(above["second"][1:2])
        if point == ("attend_back", 1):
            return found + tuple(above["second"][3:])
        if point == "input":
            return found + tuple(above["first"][1:])
        return found

    for layer in reversed(range(LAYERS)):
        triple, (rows_in, attended, context), late = layer_backward(
            incoming, saved_all[layer], norm_gains[layer], tables, split, dp_count,
            functools.partial(at, layer),
        )
        first_weight = saved_all[layer][-2]
        if layer:
            incoming = []
            for k in range(chunks):
                theirs = input_back_call(
                    2 * k + 1, triple, first_weight, BF16, at(layer, ("input", k))
                )
                mine = input_back_call(2 * k, triple, first_weight, F32)
                incoming.append((attended[2 * k], *finish_pair(mine, theirs)))
            drop(first_weight)
            above["second"] = scatter_finish(where, late)
            sums = weight_call(split, [(rows_in, [triple]), (attended, context)], dp_count)
            drop(*rows_in, *attended[1::2], *context)
            above["first"] = scatter_start(sums)
            if split is None:
                above["first"] = scatter_finish(where, above["first"])

    kept, sent = input_last_call(where, triple, first_weight, attended[::2], at(0, "input"))
    sent = swap_core(sent)
    drop(first_weight, *tables[:2])
    second_sum = scatter_finish(where, late)
    arriving = [second_sum[1:2], [], second_sum[2:]]
    sum_norms(0)
    sums = weight_call(split, [(rows_in, [triple]), (attended, context)], dp_count)
    Order.kept = []
    sums = scatter_start(sums)
    mine, theirs = call(
        side_kernel,
        [sds(count, part // 2, width // 2, dtype=F32), sds(count, part // 2, width // 2)],
        where, kept, sent, scalars=1,
    )
    sum_norms(1)
    total = add_call(mine, swap_x(theirs), BF16, arriving[0])
    if split is None:
        near = lax.all_to_all(total, "dp", split_axis=0, concat_axis=0, tiled=True)
        first_sum = scatter_finish(where, sums)
    else:
        moving = exchange_start(total, where)
        first_sum = scatter_finish(where, sums)
        sum_norms(2)
        moving = exchange_middle(*moving, arriving[1])
        sum_norms(3)
        near = exchange_finish(moving, arriving[2] + first_sum[1:])
    far = swap_x(near)
    for index in range(2 if split is None else 4, len(steps) - 1):
        sum_norms(index)
    norms = own_sums["norms"]
    gains_total, biases_total = call(
        norms_kernel, [sds(LAYERS, 2, width, dtype=F32)] * 2, norms, steps[-1](norms)
    )
    received[1] = [total_call(above["first"]), total_call(above["second"])]
    received[0] = [first_sum, second_sum]
    shapes = (
        jnp.swapaxes(project_weight, 1, 2), gate_up_weight, output_weight,
        jnp.swapaxes(down_weight, 1, 2),
    )
    project_grad, gate_up_grad, output_grad, down_grad = call(
        functools.partial(grads_kernel, tuple(tuple(len(g) for g in r) for r in received)),
        [sds(*w.shape, dtype=F32) for w in shapes],
        *[r for groups in received for group in groups for r in group],
    )
    returned = call(
        functools.partial(last_kernel, split is not None), [sds(count, part, width, dtype=F32)],
        dealing_order, where, near, far, swap_core(near), swap_core(far), scalars=2,
    )[0]

    return (
        shown[0][None], returned, jnp.swapaxes(project_grad, 1, 2), gate_up_grad, output_grad,
        jnp.swapaxes(down_grad, 1, 2), gains_total, biases_total,
    )


def solution(mesh):
    placed = (
        P(None, "dp", None),
        P(),
        P(),
        P(None, "dp", None, "tensor"),
        P(None, "dp", None, "tensor"),
        P(None, "tensor", "dp"),
        P(None, "tensor", "dp"),
        P(),
        P(),
        P("dp", "tensor", None),
    )
    return jax.shard_map(
        on_device,
        mesh=mesh,
        in_specs=placed,
        out_specs=(
            P("dp", "tensor", None),
            P(None, "dp", None),
            P(None, "dp", None, "tensor"),
            P(None, "dp", None, "tensor"),
            P(None, "tensor", "dp"),
            P(None, "tensor", "dp"),
            P(),
            P(),
        ),
        check_vma=False,
    )
```
